256 devices in a mesh: flow: 16 (over y, x), cy: 8 (over z_hi, core), cz: 2 (over z_lo).
Axes of the slice: x: 4, y: 4, z: 8 (z_hi: 4, z_lo: 2; z = z_hi * 2 + z_lo), core: 2. Of those that a mesh axis runs over, the one named last changes fastest.
Arguments:
- flow_pops: float32 [19, 256, 128, 256], P(None, 'flow', 'cy', 'cz'), may hold values from 0.02 to 0.22
- ion_pos: float32 [7, 256, 128, 256], P(None, 'flow', 'cy', 'cz'), may hold values from 0.05 to 0.25
- ion_neg: float32 [7, 256, 128, 256], P(None, 'flow', 'cy', 'cz'), may hold values from 0.05 to 0.25
- gray_class: int32 [256, 128, 256], P('flow', 'cy', 'cz'), may hold values from 0 to 15
- fraction_table: float32 [16], replicated, may hold values from 0 to 0.9
Outputs:
- flow_new: float32 [19, 256, 128, 256], P(None, 'flow', 'cy', 'cz')
- pos_new: float32 [7, 256, 128, 256], P(None, 'flow', 'cy', 'cz')
- neg_new: float32 [7, 256, 128, 256], P(None, 'flow', 'cy', 'cz')
- potential: float32 [256, 128, 256], P('flow', 'cy', 'cz')
The draws below stay inside these ranges and needn't reach their ends.
All inputs are finite; a program needn't handle non-finite values.
Results may differ from the reference program's by a relative error of at most 0.0003.
Values sent between devices are 32-bit elements; how exact they have to be, the bound alone decides.
A program may use at most 192 MiB of HBM per device.

```python
import math
import jax
import jax.numpy as jnp
from jax import lax

CLASSES = 16
NX = 256
NY = 128
NZ = 256


def stripe_pattern(key):
    phases = jax.random.uniform(key, (2,), jnp.float32, 0.0, 2.0 * math.pi)
    along_y = jnp.arange(NY, dtype=jnp.float32) * (2.0 * math.pi / 5.0) + phases[0]
    along_z = jnp.arange(NZ, dtype=jnp.float32) * (2.0 * math.pi / 7.0) + phases[1]
    return 0.025 * jnp.cos(along_y)[:, None] + 0.045 * jnp.cos(along_z)[None, :]


def draw_ion_pos(key, part):
    pattern = stripe_pattern(key)
    key = jax.random.fold_in(key, 11)
    noise = jax.random.uniform(key, (7, NX, NY, NZ), jnp.float32, -0.03, 0.03)
    return jnp.clip(0.15 + pattern[None, None] + noise, 0.05, 0.25)


def draw_ion_neg(key, part):
    pattern = stripe_pattern(key)
    key = jax.random.fold_in(key, 23)
    noise = jax.random.uniform(key, (7, NX, NY, NZ), jnp.float32, -0.03, 0.03)
    return jnp.clip(0.15 - pattern[None, None] + noise, 0.05, 0.25)


def plant(values, own_key, low, top_value):
    index_at = [jax.random.randint(jax.random.fold_in(own_key, axis), (), 0, length) for axis, length in enumerate(values.shape)]
    main_axis = values.shape.index(max(values.shape))
    beside = index_at[:main_axis] + [(index_at[main_axis] + 1) % values.shape[main_axis]] + index_at[main_axis + 1:]
    return values.at[tuple(index_at)].set(low).at[tuple(beside)].set(top_value)


def block_levels(rng, shape, split, least, high):
    factor_of, own = 1.0, jax.random.fold_in(rng, 6)
    for dim, blocks in split:
        steps = jnp.exp(jax.random.uniform(jax.random.fold_in(own, dim), (blocks,), jnp.float32, least / len(split), high / len(split)))
        factor_of = factor_of * jnp.repeat(steps, shape[dim] // blocks).reshape([-1 if axis == dim else 1 for axis in range(len(shape))])
    return factor_of


def setup_inputs(seed: int = 0) -> dict:
    splits = jax.random.split(jax.random.key(seed), 6)
    return {
        "flow_pops": jnp.clip(0.02 + 0.2 * jax.random.uniform(splits[0], (19, NX, NY, NZ), jnp.float32) ** block_levels(splits[0], (19, NX, NY, NZ), ((1, 16), (2, 8), (3, 2)), -0.2, 0.2), 0.02, 0.22),
        "ion_pos": draw_ion_pos(jax.random.fold_in(splits[5], 71), 0),
        "ion_neg": draw_ion_neg(jax.random.fold_in(splits[5], 71), 0),
        "gray_class": plant(jax.random.randint(splits[3], (NX, NY, NZ), 0, CLASSES), jax.random.fold_in(splits[3], 1), 0, CLASSES - 1).astype(jnp.int32),
        "fraction_table": jnp.clip(jax.random.uniform(splits[4], (CLASSES,), jnp.float32, 0.0, 0.9), 0.0, 0.9),
    }


flow_dirs = ((0, 0, 0), (1, 0, 0), (-1, 0, 0), (0, 1, 0), (0, -1, 0), (0, 0, 1), (0, 0, -1),
             (1, 1, 0), (-1, -1, 0), (1, -1, 0), (-1, 1, 0), (1, 0, 1), (-1, 0, -1),
             (1, 0, -1), (-1, 0, 1), (0, 1, 1), (0, -1, -1), (0, 1, -1), (0, -1, 1))
flow_weights = (1.0 / 3.0,) + (1.0 / 18.0,) * 6 + (1.0 / 36.0,) * 12
ion_weights = (0.25,) + (0.125,) * 6
opposite = (0, 2, 1, 4, 3, 6, 5, 8, 7, 10, 9, 12, 11, 14, 13, 16, 15, 18, 17)
tau_flow = 0.8
tau_ion = 0.9
coupling = 2.0
mobility = 0.5
highest = lax.Precision.HIGHEST


def moments(pops, count):
    directions = jnp.array(flow_dirs[:count], dtype=jnp.float32)
    density = jnp.sum(pops, axis=0)
    momentum = jnp.tensordot(directions, pops, axes=((0,), (0,)), precision=highest)
    return density, momentum


def relax(pops, count, weights, density, drift, solid, relax_time, quadratic):
    directions = jnp.array(flow_dirs[:count], dtype=jnp.float32)
    projected = jnp.tensordot(directions, drift, axes=((1,), (0,)), precision=highest)
    weight_column = jnp.array(weights, dtype=jnp.float32)[:, None, None, None]
    if quadratic:
        speed_sq = jnp.sum(drift * drift, axis=0)
        shape_term = 1.0 + 3.0 * projected + 4.5 * projected * projected - 1.5 * speed_sq
    else:
        shape_term = 1.0 + 4.0 * projected
    balance = weight_column * density * shape_term
    mirrored = pops[jnp.array(opposite[:count], dtype=jnp.int32)]
    return pops + (1.0 - solid) * (balance - pops) / relax_time + solid * (mirrored - pops)


def eigenvalues(length):
    return 2.0 - 2.0 * jnp.cos(jnp.arange(length, dtype=jnp.float32) * (2.0 * math.pi / length))


def solve_potential(charge):
    spectrum = jnp.fft.fftn(charge)
    total = eigenvalues(NX)[:, None, None] + eigenvalues(NY)[None, :, None] + eigenvalues(NZ)[None, None, :]
    green = jnp.where(total > 0.0, coupling / jnp.where(total > 0.0, total, 1.0), 0.0)
    return jnp.real(jnp.fft.ifftn(spectrum * green)).astype(charge.dtype)


def stream_all(post, offsets):
    return jnp.stack([jnp.roll(post[member], offsets[member], (0, 1, 2)) for member in range(len(offsets))])


def reference(flow_pops, ion_pos, ion_neg, gray_class, fraction_table):
    solid = fraction_table[gray_class]
    conc_pos = jnp.sum(ion_pos, axis=0)
    conc_neg = jnp.sum(ion_neg, axis=0)
    charge = conc_pos - conc_neg
    potential = solve_potential(charge)
    field = jnp.stack([
        -0.5 * (jnp.roll(potential, -1, 0) - jnp.roll(potential, 1, 0)),
        -0.5 * (jnp.roll(potential, -1, 1) - jnp.roll(potential, 1, 1)),
        -0.5 * (jnp.roll(potential, -1, 2) - jnp.roll(potential, 1, 2))])
    density, momentum = moments(flow_pops, 19)
    velocity = momentum / density
    drift_flow = velocity + tau_flow * charge * field / density
    flow_post = relax(flow_pops, 19, flow_weights, density, drift_flow, solid, tau_flow, True)
    pos_post = relax(ion_pos, 7, ion_weights, conc_pos, velocity + mobility * field, solid, tau_ion, False)
    neg_post = relax(ion_neg, 7, ion_weights, conc_neg, velocity - mobility * field, solid, tau_ion, False)
    flow_new = stream_all(flow_post, flow_dirs)
    pos_new = stream_all(pos_post, flow_dirs[:7])
    neg_new = stream_all(neg_post, flow_dirs[:7])
    return flow_new, pos_new, neg_new, potential
```

```python
import functools
import math

import jax
import jax.numpy as jnp
import numpy as np
from jax import lax
from jax.experimental import pallas as pl
from jax.experimental.pallas import tpu as pltpu
from jax.sharding import PartitionSpec as P

flow_dirs = (
    (0, 0, 0),
    (1, 0, 0),
    (-1, 0, 0),
    (0, 1, 0),
    (0, -1, 0),
    (0, 0, 1),
    (0, 0, -1),
    (1, 1, 0),
    (-1, -1, 0),
    (1, -1, 0),
    (-1, 1, 0),
    (1, 0, 1),
    (-1, 0, -1),
    (1, 0, -1),
    (-1, 0, 1),
    (0, 1, 1),
    (0, -1, -1),
    (0, 1, -1),
    (0, -1, 1),
)
flow_weights = (1.0 / 3.0,) + (1.0 / 18.0,) * 6 + (1.0 / 36.0,) * 12
ion_weights = (0.25,) + (0.125,) * 6
tau_flow = 0.8
tau_ion = 0.9
coupling = 2.0
mobility = 0.5
NX, NY, NZ = 256, 128, 256
FLOW, CY, CZ = 16, 8, 2
MESH = pl.DeviceIdType.MESH
f32 = jnp.float32

DIRS = flow_dirs + flow_dirs[:7] + flow_dirs[:7]
FACE = {
    (axis, sign): [q for q in range(33) if DIRS[q][axis] == sign]
    for axis in range(3)
    for sign in (1, -1)
}


def cas_table(points_k, points_n, length):
    product = (points_k[:, None].astype(np.int64) * points_n[None, :]) % length
    angle = product * (2.0 * math.pi / length)
    return (np.cos(angle) + np.sin(angle)).astype(np.float32)


def tables():
    order = np.array([16 * a + b for b in range(16) for a in range(16)])
    hx = cas_table(order, order, NX)
    hy = cas_table(np.arange(NY), np.arange(NY), NY)
    hz = cas_table(np.arange(NZ), np.arange(NZ), NZ)

    def lam(modes, length):
        return 4.0 * np.sin(np.pi * modes / length) ** 2

    rows = np.zeros((NX + NY + 8, 128))
    rows[:NX] = lam(order, NX)[:, None]
    rows[NX : NX + NY] = lam(np.arange(NY), NY)[:, None]
    rows[NX + NY : NX + NY + 2] = lam(np.arange(NZ), NZ).reshape(2, 128)
    return hx, hy, hz, rows.astype(np.float32)


def place():
    return lax.axis_index("flow"), lax.axis_index("cy"), lax.axis_index("cz")


def fdot(left, right):
    return jnp.dot(left, right, precision=lax.Precision.HIGHEST, preferred_element_type=f32)


def settle(ref, sem):
    pltpu.make_async_copy(ref, ref, sem).wait()


def column_mask(shape, index):
    return lax.broadcasted_iota(jnp.int32, shape, 1) == index


def row_mask(shape, index):
    return lax.broadcasted_iota(jnp.int32, shape, 0) == index


def swap_across_plane(source, target, send_sem, recv_sem):
    _, cy, cz = place()
    me = cz * CY + cy

    def step(k, carry):
        other = lax.rem(me + k, 16)
        pltpu.make_async_remote_copy(
            src_ref=source(other),
            dst_ref=target(me),
            send_sem=send_sem,
            recv_sem=recv_sem,
            device_id={"cy": lax.rem(other, CY), "cz": lax.div(other, CY)},
            device_id_type=MESH,
        ).start()
        return carry

    lax.fori_loop(1, 16, step, 0)
    pltpu.make_async_copy(source(me), target(me), recv_sem).start()


def swap_along_flow(source, target, send_sem, recv_sem):
    me, _, _ = place()

    def step(k, carry):
        other = lax.rem(me + k, 16)
        pltpu.make_async_remote_copy(
            src_ref=source(other),
            dst_ref=target(me),
            send_sem=send_sem,
            recv_sem=recv_sem,
            device_id={"flow": other},
            device_id_type=MESH,
        ).start()
        return carry

    lax.fori_loop(1, 16, step, 0)
    pltpu.make_async_copy(source(me), target(me), recv_sem).start()


def rows_at(ref, start, count):
    return ref.at[pl.ds(pl.multiple_of(start, count), count), :]


def halves_at(ref, start, count):
    return ref.at[:, pl.ds(pl.multiple_of(start, count), count), :]


def potential_kernel(
    pos_ref,
    neg_ref,
    hx_ref,
    hy_ref,
    hz_ref,
    lam_ref,
    charge_out,
    phi_out,
    xh_out,
    yh_out,
    zh_out,
    ions,
    s0,
    r0,
    s1,
    r1,
    s2,
    r2,
    s3,
    r3,
    s4,
    r4,
    s5,
    r5,
    ys,
    zs,
    xh,
    yh,
    zh,
    load_sem,
    send_sem,
    recv_sem,
    hsend_sem,
    hrecv_sem,
):
    flow, cy, cz = place()
    load_pos = pltpu.make_async_copy(pos_ref, ions.at[pl.ds(0, 7)], load_sem.at[0])
    load_neg = pltpu.make_async_copy(neg_ref, ions.at[pl.ds(7, 7)], load_sem.at[1])
    load_pos.start()
    load_neg.start()
    barrier = pltpu.get_barrier_semaphore()
    me = cz * CY + cy

    def greet(k, carry):
        other = lax.rem(me + k, 16)
        pl.semaphore_signal(
            barrier,
            inc=1,
            device_id={"cy": lax.rem(other, CY), "cz": lax.div(other, CY)},
            device_id_type=MESH,
        )
        pl.semaphore_signal(
            barrier, inc=1, device_id={"flow": lax.rem(flow + k, 16)}, device_id_type=MESH
        )
        return carry

    lax.fori_loop(1, 16, greet, 0)
    load_pos.wait()
    load_neg.wait()
    pos = ions[0]
    neg = ions[7]
    for q in range(1, 7):
        pos = pos + ions[q]
        neg = neg + ions[7 + q]
    s0[...] = pos - neg
    pl.semaphore_wait(barrier, 30)

    swap_across_plane(
        lambda b: rows_at(s0, 16 * b, 16),
        lambda b: rows_at(r0, 16 * b, 16),
        send_sem.at[0],
        recv_sem.at[0],
    )
    charge_out[...] = s0[...]
    settle(r0, recv_sem.at[0])
    hy = hy_ref[...]
    half = [fdot(hy, r0[128 * c : 128 * c + 128, :]) for c in range(2)]
    spectrum = fdot(jnp.concatenate(half, axis=1), hz_ref[...])
    s1[0] = spectrum[:, :128]
    s1[1] = spectrum[:, 128:]
    swap_along_flow(
        lambda a: halves_at(s1, 8 * a, 8),
        lambda a: halves_at(r1, 8 * a, 8),
        send_sem.at[1],
        recv_sem.at[1],
    )
    settle(r1, recv_sem.at[1])
    for b in range(16):
        s2[16 * b : 16 * b + 16, :] = r1[b // CY, pl.ds(b % CY, 16, stride=8), :]
    swap_across_plane(
        lambda b: rows_at(s2, 16 * b, 16),
        lambda b: rows_at(r2, 16 * b, 16),
        send_sem.at[2],
        recv_sem.at[2],
    )
    total = (
        lam_ref[0:NX, :]
        + lam_ref[pl.ds(NX + CY * flow + cy, 1), :]
        + lam_ref[pl.ds(NX + NY + cz, 1), :]
    )
    scale = coupling / (NX * NY * NZ)
    green = jnp.where(total > 0.0, scale / jnp.where(total > 0.0, total, 1.0), 0.0)
    settle(r2, recv_sem.at[2])
    modes = green * fdot(hx_ref[...], r2[...])
    s3[...] = fdot(hx_ref[...], modes)
    swap_across_plane(
        lambda b: rows_at(s3, 16 * b, 16),
        lambda b: rows_at(r3, 16 * b, 16),
        send_sem.at[3],
        recv_sem.at[3],
    )
    settle(r3, recv_sem.at[3])
    for a in range(16):
        for c in range(2):
            s4[c, 8 * a : 8 * a + 8, :] = r3[pl.ds(128 * c + a, 8, stride=16), :]
    swap_along_flow(
        lambda a: halves_at(s4, 8 * a, 8),
        lambda a: halves_at(r4, 8 * a, 8),
        send_sem.at[4],
        recv_sem.at[4],
    )
    settle(r4, recv_sem.at[4])
    half = [fdot(hy, r4[c]) for c in range(2)]
    plane = fdot(jnp.concatenate(half, axis=1), hz_ref[...])
    s5[0:128, :] = plane[:, :128]
    s5[128:256, :] = plane[:, 128:]
    swap_across_plane(
        lambda b: rows_at(s5, 16 * b, 16),
        lambda b: rows_at(r5, 16 * b, 16),
        send_sem.at[5],
        recv_sem.at[5],
    )
    settle(r5, recv_sem.at[5])

    ahead, behind = lax.rem(flow + 1, FLOW), lax.rem(flow + FLOW - 1, FLOW)
    above, below = lax.rem(cy + 1, CY), lax.rem(cy + CY - 1, CY)
    copies = []

    def halo(n, source, target, device):
        copies.append(
            pltpu.make_async_remote_copy(
                src_ref=source,
                dst_ref=target,
                send_sem=hsend_sem.at[n],
                recv_sem=hrecv_sem.at[n],
                device_id=device,
                device_id_type=MESH,
            )
        )
        copies[-1].start()

    halo(0, r5.at[pl.ds(240, 16), :], xh.at[pl.ds(0, 16), :], {"flow": ahead})
    halo(1, r5.at[pl.ds(0, 16), :], xh.at[pl.ds(16, 16), :], {"flow": behind})
    ys[0:16, :] = r5[pl.ds(15, 16, stride=16), :]
    ys[16:32, :] = r5[pl.ds(0, 16, stride=16), :]
    halo(2, ys.at[pl.ds(0, 16), :], yh.at[pl.ds(0, 16), :], {"cy": above})
    halo(3, ys.at[pl.ds(16, 16), :], yh.at[pl.ds(16, 16), :], {"cy": below})
    packed = [jnp.zeros((16, 128), f32), jnp.zeros((16, 128), f32)]
    lane = lax.broadcasted_iota(jnp.int32, (16, 128), 1)
    for x in range(16):
        at = 16 * (x // 2)
        moved = pltpu.roll(r5[16 * x : 16 * x + 16, :], (at + 1) % 128, 1)
        packed[x % 2] = jnp.where((lane == at) | (lane == at + 1), moved, packed[x % 2])
    zs[0:16, :] = packed[0]
    zs[16:32, :] = packed[1]
    halo(4, zs, zh, {"cz": 1 - cz})
    phi_out[...] = r5[...]
    for copy in copies:
        copy.wait()
    xh_out[...] = xh[...]
    yh_out[...] = yh[...]
    zh_out[...] = zh[...]
    for n, ref in enumerate((s0, s1, s2, s3, s4, s5)):
        if n in (1, 4):
            settle(ref.at[:, pl.ds(0, 120), :], send_sem.at[n])
        else:
            settle(ref.at[pl.ds(0, 240), :], send_sem.at[n])


def solve_potential(ion_pos, ion_neg):
    hx, hy, hz, lam = (jnp.asarray(t) for t in tables())
    rows = (256, 128)
    halves = (2, 128, 128)
    vmem = pl.BlockSpec(memory_space=pltpu.VMEM)
    anywhere = pl.BlockSpec(memory_space=pl.ANY)
    shapes = [rows, rows, (32, 128), (32, 128), (32, 128)]
    buffers = [rows, rows, halves, halves, rows, rows, rows, rows, halves, halves, rows, rows]
    buffers += [(32, 128)] * 5
    return pl.pallas_call(
        potential_kernel,
        out_shape=[jax.ShapeDtypeStruct(s, f32) for s in shapes],
        in_specs=[anywhere, anywhere, vmem, vmem, vmem, vmem],
        out_specs=[vmem] * 5,
        scratch_shapes=[pltpu.VMEM((14, 256, 128), f32)]
        + [pltpu.VMEM(s, f32) for s in buffers]
        + [
            pltpu.SemaphoreType.DMA((2,)),
            pltpu.SemaphoreType.DMA((6,)),
            pltpu.SemaphoreType.DMA((6,)),
            pltpu.SemaphoreType.DMA((5,)),
            pltpu.SemaphoreType.DMA((5,)),
        ],
        compiler_params=pltpu.CompilerParams(
            collective_id=0, has_side_effects=True, vmem_limit_bytes=40 << 20
        ),
        name="potential",
    )(ion_pos, ion_neg, hx, hy, hz, lam)


def pick_solid(gray, table_ref):
    bits = [(gray & (1 << n)) != 0 for n in range(4)]
    level = [table_ref[n] for n in range(16)]
    values = [jnp.where(bits[0], level[n + 1], level[n]) for n in range(0, 16, 2)]
    for n in range(1, 4):
        values = [
            jnp.where(bits[n], values[m + 1], values[m]) for m in range(0, len(values), 2)
        ]
    return values[0]


def fill_fields(phi, xh, yh, zh, field):
    lane = lax.broadcasted_iota(jnp.int32, (16, 128), 1)
    row = lax.broadcasted_iota(jnp.int32, (16, 128), 0)
    for x in range(16):
        here = phi[16 * x : 16 * x + 16, :]
        low = xh[0:16, :] if x == 0 else phi[16 * x - 16 : 16 * x, :]
        high = xh[16:32, :] if x == 15 else phi[16 * x + 16 : 16 * x + 32, :]
        field[0, 16 * x : 16 * x + 16, :] = -0.5 * (high - low)
        low = jnp.where(row == 0, yh[x : x + 1, :], pltpu.roll(here, 1, 0))
        high = jnp.where(row == 15, yh[16 + x : 17 + x, :], pltpu.roll(here, 15, 0))
        field[1, 16 * x : 16 * x + 16, :] = -0.5 * (high - low)
        edge = zh[16 * (x % 2) : 16 * (x % 2) + 16, :]
        at = 16 * (x // 2)
        low = jnp.where(lane == 0, pltpu.roll(edge, (128 - at) % 128, 1), pltpu.roll(here, 1, 1))
        high = jnp.where(
            lane == 127, pltpu.roll(edge, (127 - at - 1) % 128, 1), pltpu.roll(here, 127, 1)
        )
        field[2, 16 * x : 16 * x + 16, :] = -0.5 * (high - low)


def collide(f, g, h, gray, table_ref, field, emit):
    solid = pick_solid(gray, table_ref)
    conc_pos = sum(g[1:], g[0])
    conc_neg = sum(h[1:], h[0])
    charge = conc_pos - conc_neg
    density = sum(f[1:], f[0])
    inverse = 1.0 / density
    momentum = []
    for axis in range(3):
        plus = [f[q] for q in range(19) if flow_dirs[q][axis] == 1]
        minus = [f[q] for q in range(19) if flow_dirs[q][axis] == -1]
        momentum.append(sum(plus[1:], plus[0]) - sum(minus[1:], minus[0]))
    velocity = [m * inverse for m in momentum]
    push = (tau_flow * charge) * inverse
    drift = [velocity[d] + push * field[d] for d in range(3)]
    square = drift[0] * drift[0] + drift[1] * drift[1] + drift[2] * drift[2]
    omega = (1.0 - solid) * (1.0 / tau_flow)
    keep = 1.0 - omega - solid
    mass = omega * density
    base = 1.0 - 1.5 * square
    emit(0, (keep + solid) * f[0] + (mass * flow_weights[0]) * base)
    for q in range(1, 19, 2):
        along = None
        for d in range(3):
            if flow_dirs[q][d]:
                term = drift[d]
                if along is None:
                    along = term if flow_dirs[q][d] == 1 else -term
                else:
                    along = along + term if flow_dirs[q][d] == 1 else along - term
        scaled = mass * flow_weights[q]
        even = scaled * (base + 4.5 * along * along)
        odd = (3.0 * scaled) * along
        emit(q, keep * f[q] + solid * f[q + 1] + (even + odd))
        emit(q + 1, keep * f[q + 1] + solid * f[q] + (even - odd))
    omega = (1.0 - solid) * (1.0 / tau_ion)
    keep = 1.0 - omega - solid
    for start, pops, conc, sign in ((19, g, conc_pos, mobility), (26, h, conc_neg, -mobility)):
        mass = omega * conc
        emit(start, (keep + solid) * pops[0] + ion_weights[0] * mass)
        even = ion_weights[1] * mass
        for d in range(3):
            q = 1 + 2 * d
            odd = (4.0 * even) * (velocity[d] + sign * field[d])
            emit(start + q, keep * pops[q] + solid * pops[q + 1] + (even + odd))
            emit(start + q + 1, keep * pops[q + 1] + solid * pops[q] + (even - odd))


def collision_kernel(
    table_ref, flow_ref, pos_ref, neg_ref, gray_ref, phi, xh, yh, zh,
    post, xf, yf, zf, corner, field,
):
    fill_fields(phi, xh, yh, zh, field)

    def block(i, carry):
        at = pl.ds(pl.multiple_of(8 * i, 8), 8)

        def emit(q, values):
            post[q, at, :] = values

        collide(
            [flow_ref[q, at, :] for q in range(19)],
            [pos_ref[q, at, :] for q in range(7)],
            [neg_ref[q, at, :] for q in range(7)],
            gray_ref[at, :],
            table_ref,
            [field[d, at, :] for d in range(3)],
            emit,
        )
        return carry

    lax.fori_loop(0, 32, block, 0)
    gather_faces(post, xf, yf, zf, corner)


def gather_faces(post, xf, yf, zf, corner):
    for n, q in enumerate(FACE[0, 1]):
        xf[n] = post[q, 240:256, :]
    for n, q in enumerate(FACE[0, -1]):
        xf[7 + n] = post[q, 0:16, :]
    for n, q in enumerate(FACE[1, 1]):
        yf[n] = post[q, pl.ds(15, 16, stride=16), :]
    for n, q in enumerate(FACE[1, -1]):
        yf[7 + n] = post[q, pl.ds(0, 16, stride=16), :]
    lane = lax.broadcasted_iota(jnp.int32, (16, 128), 1)
    packed = [jnp.zeros((16, 128), f32), jnp.zeros((16, 128), f32)]
    for n, (up, down) in enumerate(zip(FACE[2, 1], FACE[2, -1])):
        for x in range(16):
            both = jnp.where(
                lane == 127, post[up, 16 * x : 16 * x + 16, :], post[down, 16 * x : 16 * x + 16, :]
            )
            at = 16 * (x // 2) + 2 * n
            moved = pltpu.roll(both, (at + 1) % 128, 1)
            packed[x % 2] = jnp.where((lane == at) | (lane == at + 1), moved, packed[x % 2])
    zf[0:16, :] = packed[0]
    zf[16:32, :] = packed[1]
    corner[0] = post[7, 248:256, :]
    corner[1] = post[8, 0:8, :]
    corner[2] = post[9, 240:248, :]
    corner[3] = post[10, 8:16, :]


def collide_all(table, flow_pops, ion_pos, ion_neg, gray, phi, xh, yh, zh):
    vmem = pl.BlockSpec(memory_space=pltpu.VMEM)
    shapes = [(33, 256, 128), (14, 16, 128), (14, 16, 128), (32, 128), (4, 8, 128)]
    return pl.pallas_call(
        collision_kernel,
        out_shape=[jax.ShapeDtypeStruct(s, f32) for s in shapes],
        in_specs=[pl.BlockSpec(memory_space=pltpu.SMEM)] + [vmem] * 8,
        out_specs=[vmem] * 5,
        scratch_shapes=[pltpu.VMEM((3, 256, 128), f32)],
        compiler_params=pltpu.CompilerParams(vmem_limit_bytes=40 << 20),
        name="collision",
    )(table, flow_pops, ion_pos, ion_neg, gray, phi, xh, yh, zh)


def face_messages(xf, yf, zf, corner, xr, yr, zr, zx, zy, cr):
    up, down = pl.ds(0, 7), pl.ds(7, 7)
    low, high = pl.ds(0, 16), pl.ds(16, 16)
    return [
        (xf.at[up], xr.at[up], 1, 0, 0),
        (xf.at[down], xr.at[down], -1, 0, 0),
        (yf.at[up], yr.at[up], 0, 1, 0),
        (yf.at[down], yr.at[down], 0, -1, 0),
        (zf, zr, 0, 0, 1),
        (zf.at[high], zx.at[low], 1, 0, 1),
        (zf.at[low], zx.at[high], -1, 0, 1),
        (zf, zy.at[0], 0, 1, 1),
        (zf, zy.at[1], 0, -1, 1),
        (corner.at[0], cr.at[0], 1, 1, 0),
        (corner.at[1], cr.at[1], -1, -1, 0),
        (corner.at[2], cr.at[2], 1, -1, 0),
        (corner.at[3], cr.at[3], -1, 1, 0),
    ]


def partner(step_flow, step_cy, cross):
    flow, cy, cz = place()
    return (
        lax.rem(flow + FLOW + step_flow, FLOW),
        lax.rem(cy + CY + step_cy, CY),
        1 - cz if cross else cz,
    )


def faces_kernel(
    xf, yf, zf, corner, xo, yo, zo, zxo, zyo, co, xr, yr, zr, zx, zy, cr, send_sem, recv_sem
):
    messages = face_messages(xf, yf, zf, corner, xr, yr, zr, zx, zy, cr)
    barrier = pltpu.get_barrier_semaphore()
    for _, _, i, j, k in messages:
        pl.semaphore_signal(barrier, inc=1, device_id=partner(i, j, k), device_id_type=MESH)
    pl.semaphore_wait(barrier, len(messages))
    copies = []
    for n, (source, target, i, j, k) in enumerate(messages):
        copies.append(
            pltpu.make_async_remote_copy(
                src_ref=source,
                dst_ref=target,
                send_sem=send_sem.at[n],
                recv_sem=recv_sem.at[n],
                device_id=partner(i, j, k),
                device_id_type=MESH,
            )
        )
        copies[-1].start()
    for copy in copies:
        copy.wait()
    for out, got in ((xo, xr), (yo, yr), (zo, zr), (zxo, zx), (zyo, zy), (co, cr)):
        out[...] = got[...]


def swap_faces(xf, yf, zf, corner):
    vmem = pl.BlockSpec(memory_space=pltpu.VMEM)
    shapes = [(14, 16, 128), (14, 16, 128), (32, 128), (32, 128), (2, 32, 128), (4, 8, 128)]
    return pl.pallas_call(
        faces_kernel,
        out_shape=[jax.ShapeDtypeStruct(s, f32) for s in shapes],
        in_specs=[vmem] * 4,
        out_specs=[vmem] * 6,
        scratch_shapes=[pltpu.VMEM(s, f32) for s in shapes]
        + [pltpu.SemaphoreType.DMA((13,)), pltpu.SemaphoreType.DMA((13,))],
        compiler_params=pltpu.CompilerParams(
            collective_id=1, has_side_effects=True, vmem_limit_bytes=8 << 20
        ),
        name="faces",
    )(xf, yf, zf, corner)


def run_population(q, load, xr, yr, zr, zx, zy, cr, store):
    ex, ey, ez = DIRS[q]
    lane = lax.broadcasted_iota(jnp.int32, (16, 128), 1)
    row = lax.broadcasted_iota(jnp.int32, (16, 128), 0)
    last_row, first_row = (15, 0) if ey == 1 else (0, 15)
    for x in range(16):
        xs = x - ex
        outside = xs < 0 or xs > 15
        if outside:
            plane = xr[FACE[0, ex].index(q) + (0 if ex == 1 else 7)]
        else:
            plane = load(xs)
        if ey:
            if outside:
                n = {7: 0, 8: 1, 9: 2, 10: 3}[q]
                tile = 7 if ey == 1 else 0
                line = cr[n, tile : tile + 1, :]
            else:
                line = yr[FACE[1, ey].index(q) + (0 if ey == 1 else 7), xs : xs + 1, :]
            plane = jnp.where(row == first_row, line, pltpu.roll(plane, ey % 16, 0))
        if ez:
            face = FACE[2, ez].index(q)
            if outside:
                edge = zx[0:16, :] if ex == 1 else zx[16:32, :]
                block = 7 if ex == 1 else 0
            else:
                edge = zr[16 * (xs % 2) : 16 * (xs % 2) + 16, :]
                block = xs // 2
            at = 16 * block + 2 * face + (0 if ez == 1 else 1)
            if ey:
                beyond = zy[0 if ey == 1 else 1, 16 * (xs % 2) : 16 * (xs % 2) + 16, :]
                edge = pltpu.roll(jnp.where(row == last_row, beyond, edge), ey % 16, 0)
            goal = 0 if ez == 1 else 127
            moved = pltpu.roll(edge, (goal - at) % 128, 1) if (goal - at) % 128 else edge
            plane = jnp.where(lane == goal, moved, pltpu.roll(plane, ez % 128, 1))
        store(x, plane)


def running_kernel(post, xr, yr, zr, zx, zy, cr, flow_out, pos_out, neg_out, got, moved, in_sem, out_sem):
    def output(q):
        if q < 19:
            return flow_out.at[q]
        return pos_out.at[q - 19] if q < 26 else neg_out.at[q - 26]

    reads = [pltpu.make_async_copy(post.at[q], got.at[q], in_sem.at[q]) for q in range(33)]
    writes = []
    for copy in reads:
        copy.start()
    for q in range(33):
        reads[q].wait()
        if q in (0, 19, 26):
            writes.append(pltpu.make_async_copy(got.at[q], output(q), out_sem.at[q]))
        else:

            def load(x, q=q):
                return got[q, 16 * x : 16 * x + 16, :]

            def store(x, plane, q=q):
                moved[q, 16 * x : 16 * x + 16, :] = plane

            run_population(q, load, xr, yr, zr, zx, zy, cr, store)
            writes.append(pltpu.make_async_copy(moved.at[q], output(q), out_sem.at[q]))
        writes[-1].start()
    for copy in writes:
        copy.wait()


def run_all(post, faces):
    vmem = pl.BlockSpec(memory_space=pltpu.VMEM)
    anywhere = pl.BlockSpec(memory_space=pl.ANY)
    return pl.pallas_call(
        running_kernel,
        out_shape=[jax.ShapeDtypeStruct((n, 256, 128), f32) for n in (19, 7, 7)],
        in_specs=[anywhere] + [vmem] * 6,
        out_specs=[anywhere] * 3,
        scratch_shapes=[
            pltpu.VMEM((33, 256, 128), f32),
            pltpu.VMEM((33, 256, 128), f32),
            pltpu.SemaphoreType.DMA((33,)),
            pltpu.SemaphoreType.DMA((33,)),
        ],
        compiler_params=pltpu.CompilerParams(vmem_limit_bytes=40 << 20),
        name="running",
    )(post, *faces)


def shards(flow_pops, ion_pos, ion_neg, gray_class, fraction_table):
    extent = gray_class.shape
    flow_pops = flow_pops.reshape(19, 256, 128)
    ion_pos = ion_pos.reshape(7, 256, 128)
    ion_neg = ion_neg.reshape(7, 256, 128)
    gray = gray_class.reshape(256, 128)
    _, phi, xh, yh, zh = solve_potential(ion_pos, ion_neg)
    post, *faces = collide_all(
        fraction_table, flow_pops, ion_pos, ion_neg, gray, phi, xh, yh, zh
    )
    flow_new, pos_new, neg_new = run_all(post, swap_faces(*faces))
    return (
        flow_new.reshape(19, *extent),
        pos_new.reshape(7, *extent),
        neg_new.reshape(7, *extent),
        phi.reshape(extent),
    )


def solution(mesh):
    in_specs = (
        P(None, "flow", "cy", "cz"),
        P(None, "flow", "cy", "cz"),
        P(None, "flow", "cy", "cz"),
        P("flow", "cy", "cz"),
        P(),
    )
    out_specs = (
        P(None, "flow", "cy", "cz"),
        P(None, "flow", "cy", "cz"),
        P(None, "flow", "cy", "cz"),
        P("flow", "cy", "cz"),
    )
    return jax.shard_map(shards, mesh=mesh, in_specs=in_specs, out_specs=out_specs, check_vma=False)
```

```python
import functools
import math

import jax
import jax.numpy as jnp
import numpy as np
from jax import lax
from jax.experimental import pallas as pl
from jax.experimental.pallas import tpu as pltpu
from jax.sharding import PartitionSpec as P

flow_dirs = (
    (0, 0, 0),
    (1, 0, 0),
    (-1, 0, 0),
    (0, 1, 0),
    (0, -1, 0),
    (0, 0, 1),
    (0, 0, -1),
    (1, 1, 0),
    (-1, -1, 0),
    (1, -1, 0),
    (-1, 1, 0),
    (1, 0, 1),
    (-1, 0, -1),
    (1, 0, -1),
    (-1, 0, 1),
    (0, 1, 1),
    (0, -1, -1),
    (0, 1, -1),
    (0, -1, 1),
)
flow_weights = (1.0 / 3.0,) + (1.0 / 18.0,) * 6 + (1.0 / 36.0,) * 12
ion_weights = (0.25,) + (0.125,) * 6
tau_flow = 0.8
tau_ion = 0.9
coupling = 2.0
mobility = 0.5
NX, NY, NZ = 256, 128, 256
FLOW, CY, CZ = 16, 8, 2
MESH = pl.DeviceIdType.MESH
f32 = jnp.float32
VMEM_LIMIT = 60 << 20

DIRS = flow_dirs + flow_dirs[:7] + flow_dirs[:7]
FACE = {
    (axis, sign): [q for q in range(33) if DIRS[q][axis] == sign]
    for axis in range(3)
    for sign in (1, -1)
}


def cas_table(points_k, points_n, length):
    product = (points_k[:, None].astype(np.int64) * points_n[None, :]) % length
    angle = product * (2.0 * math.pi / length)
    return (np.cos(angle) + np.sin(angle)).astype(np.float32)


def tables():
    order = np.array([16 * a + b for b in range(16) for a in range(16)])
    hx = cas_table(order, order, NX)
    hy = cas_table(np.arange(NY), np.arange(NY), NY)
    hz = cas_table(np.arange(NZ), np.arange(NZ), NZ)

    def lam(modes, length):
        return 4.0 * np.sin(np.pi * modes / length) ** 2

    rows = np.zeros((NX + NY + 8, 128))
    rows[:NX] = lam(order, NX)[:, None]
    rows[NX : NX + NY] = lam(np.arange(NY), NY)[:, None]
    rows[NX + NY : NX + NY + 2] = lam(np.arange(NZ), NZ).reshape(2, 128)
    return hx, hy, hz, rows.astype(np.float32)


def place():
    return lax.axis_index("flow"), lax.axis_index("cy"), lax.axis_index("cz")


def fdot(left, right):
    return jnp.dot(left, right, precision=lax.Precision.HIGHEST, preferred_element_type=f32)


def settle(ref, sem):
    pltpu.make_async_copy(ref, ref, sem).wait()


def column_mask(shape, index):
    return lax.broadcasted_iota(jnp.int32, shape, 1) == index


def row_mask(shape, index):
    return lax.broadcasted_iota(jnp.int32, shape, 0) == index


def swap_across_plane(source, target, send_sem, recv_sem):
    _, cy, cz = place()
    me = cz * CY + cy

    def step(k, carry):
        other = lax.rem(me + k, 16)
        pltpu.make_async_remote_copy(
            src_ref=source(other),
            dst_ref=target(me),
            send_sem=send_sem,
            recv_sem=recv_sem,
            device_id={"cy": lax.rem(other, CY), "cz": lax.div(other, CY)},
            device_id_type=MESH,
        ).start()
        return carry

    lax.fori_loop(1, 16, step, 0)
    pltpu.make_async_copy(source(me), target(me), recv_sem).start()


def swap_along_flow(source, target, send_sem, recv_sem):
    me, _, _ = place()

    def step(k, carry):
        other = lax.rem(me + k, 16)
        pltpu.make_async_remote_copy(
            src_ref=source(other),
            dst_ref=target(me),
            send_sem=send_sem,
            recv_sem=recv_sem,
            device_id={"flow": other},
            device_id_type=MESH,
        ).start()
        return carry

    lax.fori_loop(1, 16, step, 0)
    pltpu.make_async_copy(source(me), target(me), recv_sem).start()


def rows_at(ref, start, count):
    return ref.at[pl.ds(pl.multiple_of(start, count), count), :]


def halves_at(ref, start, count):
    return ref.at[:, pl.ds(pl.multiple_of(start, count), count), :]


def pick_solid(gray, table_ref):
    bits = [(gray & (1 << n)) != 0 for n in range(4)]
    level = [table_ref[n] for n in range(16)]
    values = [jnp.where(bits[0], level[n + 1], level[n]) for n in range(0, 16, 2)]
    for n in range(1, 4):
        values = [
            jnp.where(bits[n], values[m + 1], values[m]) for m in range(0, len(values), 2)
        ]
    return values[0]


def fill_fields(phi, xh, yh, zh, field):
    lane = lax.broadcasted_iota(jnp.int32, (16, 128), 1)
    row = lax.broadcasted_iota(jnp.int32, (16, 128), 0)
    for x in range(16):
        here = phi[16 * x : 16 * x + 16, :]
        low = xh[0:16, :] if x == 0 else phi[16 * x - 16 : 16 * x, :]
        high = xh[16:32, :] if x == 15 else phi[16 * x + 16 : 16 * x + 32, :]
        field[0, 16 * x : 16 * x + 16, :] = -0.5 * (high - low)
        low = jnp.where(row == 0, yh[x : x + 1, :], pltpu.roll(here, 1, 0))
        high = jnp.where(row == 15, yh[16 + x : 17 + x, :], pltpu.roll(here, 15, 0))
        field[1, 16 * x : 16 * x + 16, :] = -0.5 * (high - low)
        edge = zh[16 * (x % 2) : 16 * (x % 2) + 16, :]
        at = 16 * (x // 2)
        low = jnp.where(lane == 0, pltpu.roll(edge, (128 - at) % 128, 1), pltpu.roll(here, 1, 1))
        high = jnp.where(
            lane == 127, pltpu.roll(edge, (127 - at - 1) % 128, 1), pltpu.roll(here, 127, 1)
        )
        field[2, 16 * x : 16 * x + 16, :] = -0.5 * (high - low)


def prepare(pops, charge, gray, table_ref, aux):
    def block(i, carry):
        at = pl.ds(pl.multiple_of(8 * i, 8), 8)
        f = [pops[q, at, :] for q in range(33)]
        solid = pick_solid(gray[at, :], table_ref)
        density = sum(f[1:19], f[0])
        inverse = 1.0 / density
        for axis in range(3):
            plus = [f[q] for q in range(19) if flow_dirs[q][axis] == 1]
            minus = [f[q] for q in range(19) if flow_dirs[q][axis] == -1]
            aux[axis, at, :] = (sum(plus[1:], plus[0]) - sum(minus[1:], minus[0])) * inverse
        aux[3, at, :] = (tau_flow * charge[at, :]) * inverse
        omega = (1.0 - solid) * (1.0 / tau_flow)
        keep = 1.0 - omega - solid
        aux[4, at, :] = omega * density
        pops[0, at, :] = (keep + solid) * f[0]
        for q in range(1, 19, 2):
            pops[q, at, :] = keep * f[q] + solid * f[q + 1]
            pops[q + 1, at, :] = keep * f[q + 1] + solid * f[q]
        omega = (1.0 - solid) * (1.0 / tau_ion)
        keep = 1.0 - omega - solid
        for n, start in enumerate((19, 26)):
            g = f[start : start + 7]
            aux[5 + n, at, :] = omega * sum(g[1:], g[0])
            pops[start, at, :] = (keep + solid) * g[0]
            for q in range(1, 7, 2):
                pops[start + q, at, :] = keep * g[q] + solid * g[q + 1]
                pops[start + q + 1, at, :] = keep * g[q + 1] + solid * g[q]
        return carry

    lax.fori_loop(0, 32, block, 0)


def finish(pops, aux, field, post):
    def block(i, carry):
        at = pl.ds(pl.multiple_of(8 * i, 8), 8)
        velocity = [aux[d, at, :] for d in range(3)]
        electric = [field[d, at, :] for d in range(3)]
        push = aux[3, at, :]
        drift = [velocity[d] + push * electric[d] for d in range(3)]
        square = drift[0] * drift[0] + drift[1] * drift[1] + drift[2] * drift[2]
        mass = aux[4, at, :]
        base = 1.0 - 1.5 * square
        post[0, at, :] = pops[0, at, :] + (mass * flow_weights[0]) * base
        for q in range(1, 19, 2):
            along = None
            for d in range(3):
                if flow_dirs[q][d] and along is None:
                    along = drift[d] if flow_dirs[q][d] == 1 else -drift[d]
                elif flow_dirs[q][d]:
                    along = along + drift[d] if flow_dirs[q][d] == 1 else along - drift[d]
            scaled = mass * flow_weights[q]
            even = scaled * (base + 4.5 * along * along)
            odd = (3.0 * scaled) * along
            post[q, at, :] = pops[q, at, :] + (even + odd)
            post[q + 1, at, :] = pops[q + 1, at, :] + (even - odd)
        for start, n, sign in ((19, 5, mobility), (26, 6, -mobility)):
            mass = aux[n, at, :]
            post[start, at, :] = pops[start, at, :] + ion_weights[0] * mass
            even = ion_weights[1] * mass
            for d in range(3):
                q = start + 1 + 2 * d
                odd = (4.0 * even) * (velocity[d] + sign * electric[d])
                post[q, at, :] = pops[q, at, :] + (even + odd)
                post[q + 1, at, :] = pops[q + 1, at, :] + (even - odd)
        return carry

    lax.fori_loop(0, 32, block, 0)


def gather_faces(post, xf, yf, zf, corner):
    for n, q in enumerate(FACE[0, 1]):
        xf[n] = post[q, 240:256, :]
    for n, q in enumerate(FACE[0, -1]):
        xf[7 + n] = post[q, 0:16, :]
    for n, q in enumerate(FACE[1, 1]):
        yf[n] = post[q, pl.ds(15, 16, stride=16), :]
    for n, q in enumerate(FACE[1, -1]):
        yf[7 + n] = post[q, pl.ds(0, 16, stride=16), :]
    lane = lax.broadcasted_iota(jnp.int32, (16, 128), 1)
    packed = [jnp.zeros((16, 128), f32), jnp.zeros((16, 128), f32)]
    for n, (up, down) in enumerate(zip(FACE[2, 1], FACE[2, -1])):
        for x in range(16):
            both = jnp.where(
                lane == 127, post[up, 16 * x : 16 * x + 16, :], post[down, 16 * x : 16 * x + 16, :]
            )
            at = 16 * (x // 2) + 2 * n
            moved = pltpu.roll(both, (at + 1) % 128, 1)
            packed[x % 2] = jnp.where((lane == at) | (lane == at + 1), moved, packed[x % 2])
    zf[0:16, :] = packed[0]
    zf[16:32, :] = packed[1]
    corner[0] = post[7, 248:256, :]
    corner[1] = post[8, 0:8, :]
    corner[2] = post[9, 240:248, :]
    corner[3] = post[10, 8:16, :]


def face_messages(xf, yf, zf, corner, xr, yr, zr, zx, zy, cr):
    up, down = pl.ds(0, 7), pl.ds(7, 7)
    low, high = pl.ds(0, 16), pl.ds(16, 16)
    return [
        (xf.at[up], xr.at[up], 1, 0, 0),
        (xf.at[down], xr.at[down], -1, 0, 0),
        (yf.at[up], yr.at[up], 0, 1, 0),
        (yf.at[down], yr.at[down], 0, -1, 0),
        (zf, zr, 0, 0, 1),
        (zf.at[high], zx.at[low], 1, 0, 1),
        (zf.at[low], zx.at[high], -1, 0, 1),
        (zf, zy.at[0], 0, 1, 1),
        (zf, zy.at[1], 0, -1, 1),
        (corner.at[0], cr.at[0], 1, 1, 0),
        (corner.at[1], cr.at[1], -1, -1, 0),
        (corner.at[2], cr.at[2], 1, -1, 0),
        (corner.at[3], cr.at[3], -1, 1, 0),
    ]


def partner(step_flow, step_cy, cross):
    flow, cy, cz = place()
    return (
        lax.rem(flow + FLOW + step_flow, FLOW),
        lax.rem(cy + CY + step_cy, CY),
        1 - cz if cross else cz,
    )


FACE_SHAPES = [(14, 16, 128), (14, 16, 128), (32, 128), (32, 128), (2, 32, 128), (4, 8, 128)]


def main_kernel(
    table_ref, pos_hbm, neg_hbm, flow_hbm, gray_hbm, hx_hbm, hy_hbm, hz_hbm, lam_hbm,
    post_out, phi_out, xo, yo, zo, zxo, zyo, co,
    pops, post, gray, hx_ref, hy_ref, hz_ref, lam_ref, aux, field,
    s0, r0, s1, r1, s2, r2, s3, r3, s4, r4, s5, r5, ys, zs, xh, yh, zh,
    xf, yf, zf, corner, xr, yr, zr, zx, zy, cr,
    load_sem, send_sem, recv_sem, hsend_sem, hrecv_sem, fsend_sem, frecv_sem, store_sem,
):
    flow, cy, cz = place()
    loads = [
        pltpu.make_async_copy(source, target, load_sem.at[n])
        for n, (source, target) in enumerate(
            (
                (pos_hbm, pops.at[pl.ds(19, 7)]),
                (neg_hbm, pops.at[pl.ds(26, 7)]),
                (hy_hbm, hy_ref),
                (hz_hbm, hz_ref),
                (flow_hbm, pops.at[pl.ds(0, 19)]),
                (gray_hbm, gray),
                (hx_hbm, hx_ref),
                (lam_hbm, lam_ref),
            )
        )
    ]
    for copy in loads:
        copy.start()
    barrier = pltpu.get_barrier_semaphore()
    me = cz * CY + cy

    def greet(k, carry):
        other = lax.rem(me + k, 16)
        pl.semaphore_signal(
            barrier,
            inc=1,
            device_id={"cy": lax.rem(other, CY), "cz": lax.div(other, CY)},
            device_id_type=MESH,
        )
        pl.semaphore_signal(
            barrier, inc=1, device_id={"flow": lax.rem(flow + k, 16)}, device_id_type=MESH
        )
        return carry

    lax.fori_loop(1, 16, greet, 0)
    messages = face_messages(xf, yf, zf, corner, xr, yr, zr, zx, zy, cr)
    strangers = [m[2:] for m in messages if m[2] and (m[3] or m[4])]
    for i, j, k in strangers:
        pl.semaphore_signal(barrier, inc=1, device_id=partner(i, j, k), device_id_type=MESH)
    loads[0].wait()
    loads[1].wait()
    pos = pops[19]
    neg = pops[26]
    for q in range(1, 7):
        pos = pos + pops[19 + q]
        neg = neg + pops[26 + q]
    s0[...] = pos - neg
    pl.semaphore_wait(barrier, 30 + len(strangers))

    swap_across_plane(
        lambda b: rows_at(s0, 16 * b, 16),
        lambda b: rows_at(r0, 16 * b, 16),
        send_sem.at[0],
        recv_sem.at[0],
    )
    for copy in loads[2:]:
        copy.wait()
    prepare(pops, s0, gray, table_ref, aux)
    settle(r0, recv_sem.at[0])
    hy = hy_ref[...]
    half = [fdot(hy, r0[128 * c : 128 * c + 128, :]) for c in range(2)]
    spectrum = fdot(jnp.concatenate(half, axis=1), hz_ref[...])
    s1[0] = spectrum[:, :128]
    s1[1] = spectrum[:, 128:]
    swap_along_flow(
        lambda a: halves_at(s1, 8 * a, 8),
        lambda a: halves_at(r1, 8 * a, 8),
        send_sem.at[1],
        recv_sem.at[1],
    )
    settle(r1, recv_sem.at[1])
    for b in range(16):
        s2[16 * b : 16 * b + 16, :] = r1[b // CY, pl.ds(b % CY, 16, stride=8), :]
    swap_across_plane(
        lambda b: rows_at(s2, 16 * b, 16),
        lambda b: rows_at(r2, 16 * b, 16),
        send_sem.at[2],
        recv_sem.at[2],
    )
    total = (
        lam_ref[0:NX, :]
        + lam_ref[pl.ds(NX + CY * flow + cy, 1), :]
        + lam_ref[pl.ds(NX + NY + cz, 1), :]
    )
    scale = coupling / (NX * NY * NZ)
    green = jnp.where(total > 0.0, scale / jnp.where(total > 0.0, total, 1.0), 0.0)
    settle(r2, recv_sem.at[2])
    modes = green * fdot(hx_ref[...], r2[...])
    s3[...] = fdot(hx_ref[...], modes)
    swap_across_plane(
        lambda b: rows_at(s3, 16 * b, 16),
        lambda b: rows_at(r3, 16 * b, 16),
        send_sem.at[3],
        recv_sem.at[3],
    )
    settle(r3, recv_sem.at[3])
    for a in range(16):
        for c in range(2):
            s4[c, 8 * a : 8 * a + 8, :] = r3[pl.ds(128 * c + a, 8, stride=16), :]
    swap_along_flow(
        lambda a: halves_at(s4, 8 * a, 8),
        lambda a: halves_at(r4, 8 * a, 8),
        send_sem.at[4],
        recv_sem.at[4],
    )
    settle(r4, recv_sem.at[4])
    half = [fdot(hy, r4[c]) for c in range(2)]
    plane = fdot(jnp.concatenate(half, axis=1), hz_ref[...])
    s5[0:128, :] = plane[:, :128]
    s5[128:256, :] = plane[:, 128:]
    swap_across_plane(
        lambda b: rows_at(s5, 16 * b, 16),
        lambda b: rows_at(r5, 16 * b, 16),
        send_sem.at[5],
        recv_sem.at[5],
    )
    settle(r5, recv_sem.at[5])

    ahead, behind = lax.rem(flow + 1, FLOW), lax.rem(flow + FLOW - 1, FLOW)
    above, below = lax.rem(cy + 1, CY), lax.rem(cy + CY - 1, CY)
    copies = []

    def halo(n, source, target, device):
        copies.append(
            pltpu.make_async_remote_copy(
                src_ref=source,
                dst_ref=target,
                send_sem=hsend_sem.at[n],
                recv_sem=hrecv_sem.at[n],
                device_id=device,
                device_id_type=MESH,
            )
        )
        copies[-1].start()

    halo(0, r5.at[pl.ds(240, 16), :], xh.at[pl.ds(0, 16), :], {"flow": ahead})
    halo(1, r5.at[pl.ds(0, 16), :], xh.at[pl.ds(16, 16), :], {"flow": behind})
    ys[0:16, :] = r5[pl.ds(15, 16, stride=16), :]
    ys[16:32, :] = r5[pl.ds(0, 16, stride=16), :]
    halo(2, ys.at[pl.ds(0, 16), :], yh.at[pl.ds(0, 16), :], {"cy": above})
    halo(3, ys.at[pl.ds(16, 16), :], yh.at[pl.ds(16, 16), :], {"cy": below})
    packed = [jnp.zeros((16, 128), f32), jnp.zeros((16, 128), f32)]
    lane = lax.broadcasted_iota(jnp.int32, (16, 128), 1)
    for x in range(16):
        at = 16 * (x // 2)
        moved = pltpu.roll(r5[16 * x : 16 * x + 16, :], (at + 1) % 128, 1)
        packed[x % 2] = jnp.where((lane == at) | (lane == at + 1), moved, packed[x % 2])
    zs[0:16, :] = packed[0]
    zs[16:32, :] = packed[1]
    halo(4, zs, zh, {"cz": 1 - cz})
    for copy in copies:
        copy.wait()
    fill_fields(r5, xh, yh, zh, field)
    finish(pops, aux, field, post)
    stores = [
        pltpu.make_async_copy(post, post_out, store_sem.at[0]),
        pltpu.make_async_copy(r5, phi_out, store_sem.at[1]),
    ]
    for copy in stores:
        copy.start()
    gather_faces(post, xf, yf, zf, corner)
    copies = []
    for n, (source, target, i, j, k) in enumerate(messages):
        copies.append(
            pltpu.make_async_remote_copy(
                src_ref=source,
                dst_ref=target,
                send_sem=fsend_sem.at[n],
                recv_sem=frecv_sem.at[n],
                device_id=partner(i, j, k),
                device_id_type=MESH,
            )
        )
        copies[-1].start()
    for n, ref in enumerate((s0, s1, s2, s3, s4, s5)):
        if n in (1, 4):
            settle(ref.at[:, pl.ds(0, 120), :], send_sem.at[n])
        else:
            settle(ref.at[pl.ds(0, 240), :], send_sem.at[n])


    for copy in copies:
        copy.wait()
    for n, (out, got) in enumerate(
        ((xo, xr), (yo, yr), (zo, zr), (zxo, zx), (zyo, zy), (co, cr))
    ):
        stores.append(pltpu.make_async_copy(got, out, store_sem.at[2 + n]))
        stores[-1].start()
    for copy in stores:
        copy.wait()


def collide_all(table, flow_pops, ion_pos, ion_neg, gray):
    rows = (256, 128)
    halves = (2, 128, 128)
    anywhere = pl.BlockSpec(memory_space=pl.ANY)
    shapes = [(33, 256, 128), rows, *FACE_SHAPES]
    buffers = [(256, 256), (128, 128), (256, 256), (NX + NY + 8, 128), (7, 256, 128), (3, 256, 128)]
    buffers += [rows, rows, halves, halves, rows, rows, rows, rows, halves, halves, rows, rows]
    buffers += [(32, 128)] * 5
    buffers += [(14, 16, 128), (14, 16, 128), (32, 128), (4, 8, 128)] + FACE_SHAPES
    return pl.pallas_call(
        main_kernel,
        out_shape=[jax.ShapeDtypeStruct(s, f32) for s in shapes],
        in_specs=[pl.BlockSpec(memory_space=pltpu.SMEM)] + [anywhere] * 8,
        out_specs=[anywhere] * 8,
        scratch_shapes=[pltpu.VMEM((33, 256, 128), f32)] * 2
        + [pltpu.VMEM(rows, jnp.int32)]
        + [pltpu.VMEM(s, f32) for s in buffers]
        + [pltpu.SemaphoreType.DMA((n,)) for n in (8, 6, 6, 5, 5, 13, 13, 8)],
        compiler_params=pltpu.CompilerParams(
            collective_id=0, has_side_effects=True, vmem_limit_bytes=VMEM_LIMIT
        ),
        name="collision",
    )(table, ion_pos, ion_neg, flow_pops, gray, *(jnp.asarray(t) for t in tables()))


def run_population(q, load, xr, yr, zr, zx, zy, cr, store):
    ex, ey, ez = DIRS[q]
    lane = lax.broadcasted_iota(jnp.int32, (16, 128), 1)
    row = lax.broadcasted_iota(jnp.int32, (16, 128), 0)
    last_row, first_row = (15, 0) if ey == 1 else (0, 15)
    for x in range(16):
        xs = x - ex
        outside = xs < 0 or xs > 15
        if outside:
            plane = xr[FACE[0, ex].index(q) + (0 if ex == 1 else 7)]
        else:
            plane = load(xs)
        if ey:
            if outside:
                n = {7: 0, 8: 1, 9: 2, 10: 3}[q]
                tile = 7 if ey == 1 else 0
                line = cr[n, tile : tile + 1, :]
            else:
                line = yr[FACE[1, ey].index(q) + (0 if ey == 1 else 7), xs : xs + 1, :]
            plane = jnp.where(row == first_row, line, pltpu.roll(plane, ey % 16, 0))
        if ez:
            face = FACE[2, ez].index(q)
            if outside:
                edge = zx[0:16, :] if ex == 1 else zx[16:32, :]
                block = 7 if ex == 1 else 0
            else:
                edge = zr[16 * (xs % 2) : 16 * (xs % 2) + 16, :]
                block = xs // 2
            at = 16 * block + 2 * face + (0 if ez == 1 else 1)
            if ey:
                beyond = zy[0 if ey == 1 else 1, 16 * (xs % 2) : 16 * (xs % 2) + 16, :]
                edge = pltpu.roll(jnp.where(row == last_row, beyond, edge), ey % 16, 0)
            goal = 0 if ez == 1 else 127
            moved = pltpu.roll(edge, (goal - at) % 128, 1) if (goal - at) % 128 else edge
            plane = jnp.where(lane == goal, moved, pltpu.roll(plane, ez % 128, 1))
        store(x, plane)


def running_kernel(
    post_hbm, phi_hbm, x_hbm, y_hbm, z_hbm, zx_hbm, zy_hbm, c_hbm,
    flow_out, pos_out, neg_out, phi_out,
    post, moved, xr, yr, zr, zx, zy, cr, in_sem, out_sem, face_sem,
):
    def output(q):
        if q < 19:
            return flow_out.at[q]
        return pos_out.at[q - 19] if q < 26 else neg_out.at[q - 26]

    pairs = ((x_hbm, xr), (y_hbm, yr), (z_hbm, zr), (zx_hbm, zx), (zy_hbm, zy), (c_hbm, cr))
    faces = [pltpu.make_async_copy(a, b, face_sem.at[n]) for n, (a, b) in enumerate(pairs)]
    reads = [pltpu.make_async_copy(post_hbm.at[q], post.at[q], in_sem.at[q]) for q in range(33)]
    writes = []
    for q in range(33):
        source = post if DIRS[q] == (0, 0, 0) else moved
        writes.append(pltpu.make_async_copy(source.at[q], output(q), out_sem.at[q]))
    writes.append(pltpu.make_async_copy(phi_hbm, phi_out, out_sem.at[33]))
    for copy in (reads[0], *faces, *reads[1:], writes[33]):
        copy.start()
    for q in range(33):
        reads[q].wait()
        if q == 1:
            for copy in faces:
                copy.wait()
        if DIRS[q] != (0, 0, 0):

            def load(x, q=q):
                return post[q, 16 * x : 16 * x + 16, :]

            def store(x, plane, q=q):
                moved[q, 16 * x : 16 * x + 16, :] = plane

            run_population(q, load, xr, yr, zr, zx, zy, cr, store)
        writes[q].start()
    for copy in writes:
        copy.wait()


def run_all(post, phi, faces):
    anywhere = pl.BlockSpec(memory_space=pl.ANY)
    shapes = [(19, 256, 128), (7, 256, 128), (7, 256, 128), (256, 128)]
    return pl.pallas_call(
        running_kernel,
        out_shape=[jax.ShapeDtypeStruct(s, f32) for s in shapes],
        in_specs=[anywhere] * 8,
        out_specs=[anywhere] * 4,
        scratch_shapes=[pltpu.VMEM((33, 256, 128), f32)] * 2
        + [pltpu.VMEM(s, f32) for s in FACE_SHAPES]
        + [pltpu.SemaphoreType.DMA((n,)) for n in (33, 34, 6)],
        compiler_params=pltpu.CompilerParams(vmem_limit_bytes=VMEM_LIMIT),
        name="running",
    )(post, phi, *faces)


def shards(flow_pops, ion_pos, ion_neg, gray_class, fraction_table):
    extent = gray_class.shape
    flow_pops = flow_pops.reshape(19, 256, 128)
    ion_pos = ion_pos.reshape(7, 256, 128)
    ion_neg = ion_neg.reshape(7, 256, 128)
    gray = gray_class.reshape(256, 128)
    post, phi, *faces = collide_all(fraction_table, flow_pops, ion_pos, ion_neg, gray)
    flow_new, pos_new, neg_new, phi = run_all(post, phi, faces)
    return (
        flow_new.reshape(19, *extent),
        pos_new.reshape(7, *extent),
        neg_new.reshape(7, *extent),
        phi.reshape(extent),
    )


def solution(mesh):
    in_specs = (
        P(None, "flow", "cy", "cz"),
        P(None, "flow", "cy", "cz"),
        P(None, "flow", "cy", "cz"),
        P("flow", "cy", "cz"),
        P(),
    )
    out_specs = (
        P(None, "flow", "cy", "cz"),
        P(None, "flow", "cy", "cz"),
        P(None, "flow", "cy", "cz"),
        P("flow", "cy", "cz"),
    )
    return jax.shard_map(shards, mesh=mesh, in_specs=in_specs, out_specs=out_specs, check_vma=False)
```

```python
import functools
import math

import jax
import jax.numpy as jnp
import numpy as np
from jax import lax
from jax.experimental import pallas as pl
from jax.experimental.pallas import tpu as pltpu
from jax.sharding import PartitionSpec as P

flow_dirs = (
    (0, 0, 0),
    (1, 0, 0),
    (-1, 0, 0),
    (0, 1, 0),
    (0, -1, 0),
    (0, 0, 1),
    (0, 0, -1),
    (1, 1, 0),
    (-1, -1, 0),
    (1, -1, 0),
    (-1, 1, 0),
    (1, 0, 1),
    (-1, 0, -1),
    (1, 0, -1),
    (-1, 0, 1),
    (0, 1, 1),
    (0, -1, -1),
    (0, 1, -1),
    (0, -1, 1),
)
flow_weights = (1.0 / 3.0,) + (1.0 / 18.0,) * 6 + (1.0 / 36.0,) * 12
ion_weights = (0.25,) + (0.125,) * 6
tau_flow = 0.8
tau_ion = 0.9
coupling = 2.0
mobility = 0.5
NX, NY, NZ = 256, 128, 256
FLOW, CY, CZ = 16, 8, 2
MESH = pl.DeviceIdType.MESH
f32 = jnp.float32
VMEM_LIMIT = 60 << 20

DIRS = flow_dirs + flow_dirs[:7] + flow_dirs[:7]
FACE = {
    (axis, sign): [q for q in range(33) if DIRS[q][axis] == sign]
    for axis in range(3)
    for sign in (1, -1)
}


def cas_table64(points_k, points_n, length):
    product = (points_k[:, None].astype(np.int64) * points_n[None, :]) % length
    angle = product * (2.0 * math.pi / length)
    return np.cos(angle) + np.sin(angle)


def cas_table(points_k, points_n, length):
    return cas_table64(points_k, points_n, length).astype(np.float32)


def tables():
    hy = cas_table(np.arange(NY), np.arange(NY), NY)
    z = np.arange(NZ)
    hz = cas_table(z, z, NZ)
    wide = cas_table64(z, z, NZ)
    slope = -0.5 * (np.roll(wide, -1, 1) - np.roll(wide, 1, 1))
    back = [
        np.concatenate([wide[:, 128 * c : 128 * c + 128], slope[:, 128 * c : 128 * c + 128]], 1)
        for c in range(CZ)
    ]
    lam_y = 4.0 * np.sin(np.pi * np.arange(NY) / NY) ** 2
    lam_z = 4.0 * np.sin(np.pi * z / NZ) ** 2
    t = 1.0 + 0.5 * (lam_y[:, None] + lam_z[None, :])
    mu = 1.0 / (t + np.sqrt(t * t - 1.0))
    gap = 1.0 / mu - mu
    gap[0, 0] = 1.0
    scale = coupling / (NY * NZ) / gap
    mu[0, 0] = scale[0, 0] = 0.0
    window = np.arange(128) // 16
    per_rank = []
    for b in range(16):
        m = np.tile(mu[:, 16 * b : 16 * b + 16], (1, 8))
        c = np.tile(scale[:, 16 * b : 16 * b + 16], (1, 8))
        packed = mu[:, 16 * b : 16 * b + 16].reshape(2, 8, 8, 16).transpose(0, 2, 1, 3).reshape(16, 128)
        per_rank.append(
            np.concatenate(
                [m, m ** (window + 1), m ** (8 - window), m**8, c, packed**16, 1.0 / (1.0 - packed**256)]
            )
        )
    return (
        np.concatenate([hy, hy], 1),
        hz.reshape(CZ, 128, NZ),
        np.stack(back).astype(np.float32),
        np.stack(per_rank).astype(np.float32),
    )


def place():
    return lax.axis_index("flow"), lax.axis_index("cy"), lax.axis_index("cz")


def fdot(left, right):
    return jnp.dot(left, right, precision=lax.Precision.HIGHEST, preferred_element_type=f32)


def settle(ref, sem):
    pltpu.make_async_copy(ref, ref, sem).wait()


def column_mask(shape, index):
    return lax.broadcasted_iota(jnp.int32, shape, 1) == index


def row_mask(shape, index):
    return lax.broadcasted_iota(jnp.int32, shape, 0) == index


def swap_across_plane(source, target, send_sem, recv_sem):
    _, cy, cz = place()
    me = cz * CY + cy
    for step_cy in (4, 5, 3, 2, 6, 7, 1, 0):
        for step_cz in (1, 0):
            if step_cy or step_cz:
                to_cy, to_cz = lax.rem(cy + step_cy, CY), lax.rem(cz + step_cz, CZ)
                pltpu.make_async_remote_copy(
                    src_ref=source(to_cz * CY + to_cy),
                    dst_ref=target(me),
                    send_sem=send_sem,
                    recv_sem=recv_sem,
                    device_id={"cy": to_cy, "cz": to_cz},
                    device_id_type=MESH,
                ).start()
    pltpu.make_async_copy(source(me), target(me), recv_sem).start()


def swap_along_flow(source, target, send_sem, recv_sem):
    me, _, _ = place()

    def step(k, carry):
        other = lax.rem(me + k, 16)
        pltpu.make_async_remote_copy(
            src_ref=source(other),
            dst_ref=target(me),
            send_sem=send_sem,
            recv_sem=recv_sem,
            device_id={"flow": other},
            device_id_type=MESH,
        ).start()
        return carry

    lax.fori_loop(1, 16, step, 0)
    pltpu.make_async_copy(source(me), target(me), recv_sem).start()


def rows_at(ref, start, count):
    return ref.at[pl.ds(pl.multiple_of(start, count), count), :]


def window_of(shape):
    return lax.broadcasted_iota(jnp.int32, shape, 1) // 16


def swap_windows(blocks):
    window = window_of(blocks[0].shape)
    for s in (1, 2, 4):
        high = (window & s) != 0
        moved = list(blocks)
        for i in range(8):
            if not i & s:
                low_block, high_block = blocks[i], blocks[i + s]
                moved[i] = jnp.where(high, pltpu.roll(high_block, 16 * s, 1), low_block)
                moved[i + s] = jnp.where(high, high_block, pltpu.roll(low_block, 128 - 16 * s, 1))
        blocks = moved
    return blocks


def spread(values, j):
    values = jnp.where(window_of(values.shape) == j, values, 0.0)
    for s in (16, 32, 64):
        values = values + pltpu.roll(values, s, 1)
    return values


def pack_windows(values, j):
    window = window_of((8, 128))
    packed = []
    for half in range(2):
        both = jnp.zeros((8, 128), f32)
        for i in range(8):
            tile = values[64 * half + 8 * i : 64 * half + 8 * i + 8, :]
            shift = (16 * (i - j)) % 128
            both = jnp.where(window == i, pltpu.roll(tile, shift, 1) if shift else tile, both)
        packed.append(both)
    return jnp.concatenate(packed, axis=0)


def scan_up(values, factor):
    window = window_of(values.shape)
    for s in (1, 2, 4):
        moved = pltpu.roll(values, 16 * s, 1)
        if factor is not None:
            moved = factor * moved
            factor = factor * factor
        values = values + jnp.where(window >= s, moved, 0.0)
    return values


def scan_down(values, factor):
    window = window_of(values.shape)
    for s in (1, 2, 4):
        moved = factor * pltpu.roll(values, 128 - 16 * s, 1)
        factor = factor * factor
        values = values + jnp.where(window < 8 - s, moved, 0.0)
    return values


def total_of(values):
    return jnp.sum(jnp.sum(values, axis=0, keepdims=True), axis=1, keepdims=True)


def zero_mode_mask(cy, cz):
    row = lax.broadcasted_iota(jnp.int32, (8, 128), 0)
    lane = lax.broadcasted_iota(jnp.int32, (8, 128), 1)
    here = jnp.where(cy + cz == 0, 1.0, 0.0)
    return jnp.where((row == 0) & (lane % 16 == 0), here, 0.0)


def block_moments(rho, gtab, moments, partial, mask):
    mu, near, far, eighth = (gtab[128 * n : 128 * n + 128, :] for n in range(4))
    up = [scan_up(r, mu) for r in rho]
    down = [scan_down(r, mu) for r in rho]
    moments[0:16, :] = pack_windows(up[1] + eighth * up[0], 7)
    moments[16:32, :] = pack_windows(down[0] + eighth * down[1], 0)
    window = window_of((8, 128)).astype(f32)
    at = (window - 7.5, window + 0.5)
    zero = [rho[g][0:8, :] * mask for g in range(2)]
    row = lax.broadcasted_iota(jnp.int32, (8, 128), 0)
    tile = jnp.zeros((8, 128), f32)
    for n in range(3):
        weighted = zero[0] * at[0] ** n + zero[1] * at[1] ** n if n else zero[0] + zero[1]
        tile = jnp.where(row == n, total_of(weighted), tile)
    moments[32:40, :] = tile

    def rest():
        partial[0] = up[0] + (down[0] - rho[0]) + far * spread(down[1], 0)
        partial[1] = up[1] + (down[1] - rho[1]) + near * spread(up[0], 7)

    return rest


def gathered_potential(rho_first, gtab, gathered, partial, mask, flow, out):
    def packed(source, start):
        return gathered[pl.ds(pl.multiple_of(40 * source + start, 8), 16), :]

    ratio, image = gtab[640:656, :], gtab[656:672, :]
    left, right = packed(flow, 0), packed(flow, 16)
    for d in range(15, 0, -1):
        left = packed(lax.rem(flow + 16 - d, 16), 0) + ratio * left
        right = packed(lax.rem(flow + d, 16), 16) + ratio * right
    left, right = left * image, right * image
    for tile in range(16):
        rows = slice(8 * tile, 8 * tile + 8)
        half = 8 * (tile // 8)
        from_left = spread(left[half : half + 8, :], tile % 8)
        from_right = spread(right[half : half + 8, :], tile % 8)
        near, far, eighth, scale = (
            gtab[128 * n + 8 * tile : 128 * n + 8 * tile + 8, :] for n in range(1, 5)
        )
        out[rows, 0:128] = scale * (
            partial[0, rows, :] + near * from_left + (far * eighth) * from_right
        )
        out[rows, 128:256] = scale * (
            partial[1, rows, :] + (near * eighth) * from_left + far * from_right
        )

    def moment(block, n):
        return gathered[40 * block + 32 + n : 40 * block + 33 + n, :]

    mean = sum((moment(n, 0) for n in range(1, 16)), moment(0, 0)) * (1.0 / NX)
    first = second = left_sum = left_first = jnp.zeros((1, 128), f32)
    for block in range(16):
        centre = 16.0 * block - 120.0
        own = moment(block, 0) - 16.0 * mean
        own_first = centre * own + moment(block, 1)
        first = first + own_first
        second = second + (centre * own_first + centre * moment(block, 1))
        second = second + (moment(block, 2) - 340.0 * mean)
        before = jnp.where(block < flow, 1.0, 0.0)
        left_sum = left_sum + before * own
        left_first = left_first + before * own_first
    window = window_of((8, 128)).astype(f32)
    centre = 16.0 * flow.astype(f32) - 120.0
    for g in range(2):
        at = centre + (window - 7.5 + 8.0 * g)
        zero = (rho_first[g] - mean) * mask
        to_here, to_here_first = scan_up(zero, None), scan_up(zero * at, None)
        upto, upto_first = left_sum + to_here, left_first + to_here_first
        left_sum = left_sum + spread(to_here, 7)
        left_first = left_first + spread(to_here_first, 7)
        distance = 2.0 * (at * upto - upto_first) + first
        value = (second - 2.0 * at * first) * (0.5 / NX) - 0.5 * distance
        lanes = slice(128 * g, 128 * g + 128)
        out[0:8, lanes] = out[0:8, lanes] + (coupling / (NY * NZ)) * (mask * value)


def pick_solid(gray, table_ref):
    bits = [(gray & (1 << n)) != 0 for n in range(4)]
    level = [table_ref[n] for n in range(16)]
    values = [jnp.where(bits[0], level[n + 1], level[n]) for n in range(0, 16, 2)]
    for n in range(1, 4):
        values = [
            jnp.where(bits[n], values[m + 1], values[m]) for m in range(0, len(values), 2)
        ]
    return values[0]


def fill_fields(phi, xh, yh, field):
    row = lax.broadcasted_iota(jnp.int32, (16, 128), 0)
    for x in range(16):
        here = phi[16 * x : 16 * x + 16, :]
        low = xh[0:16, :] if x == 0 else phi[16 * x - 16 : 16 * x, :]
        high = xh[16:32, :] if x == 15 else phi[16 * x + 16 : 16 * x + 32, :]
        field[0, 16 * x : 16 * x + 16, :] = -0.5 * (high - low)
        low = jnp.where(row == 0, yh[x : x + 1, :], pltpu.roll(here, 1, 0))
        high = jnp.where(row == 15, yh[16 + x : 17 + x, :], pltpu.roll(here, 15, 0))
        field[1, 16 * x : 16 * x + 16, :] = -0.5 * (high - low)


def prepare(pops, charge, gray, table_ref, aux):
    def block(i, carry):
        at = pl.ds(pl.multiple_of(8 * i, 8), 8)
        f = [pops[q, at, :] for q in range(33)]
        solid = pick_solid(gray[at, :], table_ref)
        density = sum(f[1:19], f[0])
        inverse = 1.0 / density
        for axis in range(3):
            plus = [f[q] for q in range(19) if flow_dirs[q][axis] == 1]
            minus = [f[q] for q in range(19) if flow_dirs[q][axis] == -1]
            aux[axis, at, :] = (sum(plus[1:], plus[0]) - sum(minus[1:], minus[0])) * inverse
        aux[3, at, :] = (tau_flow * charge[at, :]) * inverse
        omega = (1.0 - solid) * (1.0 / tau_flow)
        keep = 1.0 - omega - solid
        aux[4, at, :] = omega * density
        pops[0, at, :] = (keep + solid) * f[0]
        for q in range(1, 19, 2):
            pops[q, at, :] = keep * f[q] + solid * f[q + 1]
            pops[q + 1, at, :] = keep * f[q + 1] + solid * f[q]
        omega = (1.0 - solid) * (1.0 / tau_ion)
        keep = 1.0 - omega - solid
        for n, start in enumerate((19, 26)):
            g = f[start : start + 7]
            aux[5 + n, at, :] = omega * sum(g[1:], g[0])
            pops[start, at, :] = (keep + solid) * g[0]
            for q in range(1, 7, 2):
                pops[start + q, at, :] = keep * g[q] + solid * g[q + 1]
                pops[start + q + 1, at, :] = keep * g[q + 1] + solid * g[q]
        return carry

    lax.fori_loop(0, 32, block, 0)


def finish(pops, aux, field, post):
    def block(i, carry):
        at = pl.ds(pl.multiple_of(8 * i, 8), 8)
        velocity = [aux[d, at, :] for d in range(3)]
        electric = [field[d, at, :] for d in range(3)]
        push = aux[3, at, :]
        drift = [velocity[d] + push * electric[d] for d in range(3)]
        square = drift[0] * drift[0] + drift[1] * drift[1] + drift[2] * drift[2]
        mass = aux[4, at, :]
        base = 1.0 - 1.5 * square
        post[0, at, :] = pops[0, at, :] + (mass * flow_weights[0]) * base
        for q in range(1, 19, 2):
            along = None
            for d in range(3):
                if flow_dirs[q][d] and along is None:
                    along = drift[d] if flow_dirs[q][d] == 1 else -drift[d]
                elif flow_dirs[q][d]:
                    along = along + drift[d] if flow_dirs[q][d] == 1 else along - drift[d]
            scaled = mass * flow_weights[q]
            even = scaled * (base + 4.5 * along * along)
            odd = (3.0 * scaled) * along
            post[q, at, :] = pops[q, at, :] + (even + odd)
            post[q + 1, at, :] = pops[q + 1, at, :] + (even - odd)
        for start, n, sign in ((19, 5, mobility), (26, 6, -mobility)):
            mass = aux[n, at, :]
            post[start, at, :] = pops[start, at, :] + ion_weights[0] * mass
            even = ion_weights[1] * mass
            for d in range(3):
                q = start + 1 + 2 * d
                odd = (4.0 * even) * (velocity[d] + sign * electric[d])
                post[q, at, :] = pops[q, at, :] + (even + odd)
                post[q + 1, at, :] = pops[q + 1, at, :] + (even - odd)
        return carry

    lax.fori_loop(0, 32, block, 0)


def gather_faces(post, xf, yf, zf, corner):
    for n, q in enumerate(FACE[0, 1]):
        xf[n] = post[q, 240:256, :]
    for n, q in enumerate(FACE[0, -1]):
        xf[7 + n] = post[q, 0:16, :]
    for n, q in enumerate(FACE[1, 1]):
        yf[n] = post[q, pl.ds(15, 16, stride=16), :]
    for n, q in enumerate(FACE[1, -1]):
        yf[7 + n] = post[q, pl.ds(0, 16, stride=16), :]
    lane = lax.broadcasted_iota(jnp.int32, (16, 128), 1)
    packed = [jnp.zeros((16, 128), f32), jnp.zeros((16, 128), f32)]
    for n, (up, down) in enumerate(zip(FACE[2, 1], FACE[2, -1])):
        for x in range(16):
            both = jnp.where(
                lane == 127, post[up, 16 * x : 16 * x + 16, :], post[down, 16 * x : 16 * x + 16, :]
            )
            at = 16 * (x // 2) + 2 * n
            moved = pltpu.roll(both, (at + 1) % 128, 1)
            packed[x % 2] = jnp.where((lane == at) | (lane == at + 1), moved, packed[x % 2])
    zf[0:16, :] = packed[0]
    zf[16:32, :] = packed[1]
    corner[0] = post[7, 248:256, :]
    corner[1] = post[8, 0:8, :]
    corner[2] = post[9, 240:248, :]
    corner[3] = post[10, 8:16, :]


def face_messages(xf, yf, zf, corner, xr, yr, zr, zx, zy, cr):
    up, down = pl.ds(0, 7), pl.ds(7, 7)
    low, high = pl.ds(0, 16), pl.ds(16, 16)
    return [
        (xf.at[up], xr.at[up], 1, 0, 0),
        (xf.at[down], xr.at[down], -1, 0, 0),
        (yf.at[up], yr.at[up], 0, 1, 0),
        (yf.at[down], yr.at[down], 0, -1, 0),
        (zf, zr, 0, 0, 1),
        (zf.at[high], zx.at[low], 1, 0, 1),
        (zf.at[low], zx.at[high], -1, 0, 1),
        (zf, zy.at[0], 0, 1, 1),
        (zf, zy.at[1], 0, -1, 1),
        (corner.at[0], cr.at[0], 1, 1, 0),
        (corner.at[1], cr.at[1], -1, -1, 0),
        (corner.at[2], cr.at[2], 1, -1, 0),
        (corner.at[3], cr.at[3], -1, 1, 0),
    ]


def partner(step_flow, step_cy, cross):
    flow, cy, cz = place()
    return (
        lax.rem(flow + FLOW + step_flow, FLOW),
        lax.rem(cy + CY + step_cy, CY),
        1 - cz if cross else cz,
    )


FACE_SHAPES = [(14, 16, 128), (14, 16, 128), (32, 128), (32, 128), (2, 32, 128), (4, 8, 128)]


def main_kernel(
    table_ref, pos_hbm, neg_hbm, flow_hbm, gray_hbm, hy_hbm, hz_hbm, back_hbm, gtab_hbm,
    post_out, phi_out, xo, yo, zo, zxo, zyo, co,
    pops, post, gray, hy_ref, hz_ref, back_ref, gtab, aux, field, charge,
    s0, r0, moments, gathered, partial, modes, s1, r1, joined, phi, ys, xh, yh,
    xf, yf, zf, corner, xr, yr, zr, zx, zy, cr,
    load_sem, send_sem, recv_sem, hsend_sem, hrecv_sem, fsend_sem, frecv_sem, store_sem,
):
    flow, cy, cz = place()
    me = cz * CY + cy
    loads = [
        pltpu.make_async_copy(source, target, load_sem.at[n])
        for n, (source, target) in enumerate(
            (
                (pos_hbm, pops.at[pl.ds(19, 7)]),
                (neg_hbm, pops.at[pl.ds(26, 7)]),
                (hz_hbm.at[cz], hz_ref),
                (flow_hbm, pops.at[pl.ds(0, 19)]),
                (gray_hbm, gray),
                (hy_hbm, hy_ref),
                (gtab_hbm.at[me], gtab),
                (back_hbm.at[cz], back_ref),
            )
        )
    ]
    for copy in loads:
        copy.start()
    barrier = pltpu.get_barrier_semaphore()

    def greet(k, carry):
        other = lax.rem(me + k, 16)
        pl.semaphore_signal(
            barrier,
            inc=1,
            device_id={"cy": lax.rem(other, CY), "cz": lax.div(other, CY)},
            device_id_type=MESH,
        )
        pl.semaphore_signal(
            barrier, inc=1, device_id={"flow": lax.rem(flow + k, 16)}, device_id_type=MESH
        )
        return carry

    lax.fori_loop(1, 16, greet, 0)
    messages = face_messages(xf, yf, zf, corner, xr, yr, zr, zx, zy, cr)
    strangers = [m[2:] for m in messages if m[2] and (m[3] or m[4])]
    for i, j, k in strangers:
        pl.semaphore_signal(barrier, inc=1, device_id=partner(i, j, k), device_id_type=MESH)
    for copy in loads[:3]:
        copy.wait()
    pos = pops[19]
    neg = pops[26]
    for q in range(1, 7):
        pos = pos + pops[19 + q]
        neg = neg + pops[26 + q]
    charge[...] = pos - neg

    spectrum = fdot(charge[...], hz_ref[...])
    for g in range(2):
        for c in range(2):
            blocks = [
                spectrum[128 * g + 16 * i : 128 * g + 16 * i + 16, 128 * c : 128 * c + 128]
                for i in range(8)
            ]
            for i, block in enumerate(swap_windows(blocks)):
                at = 16 * (8 * c + i)
                s0[at : at + 16, 128 * g : 128 * g + 128] = block
    pl.semaphore_wait(barrier, 30 + len(strangers))
    swap_across_plane(
        lambda b: rows_at(s0, 16 * b, 16),
        lambda b: rows_at(r0, 16 * b, 16),
        send_sem.at[0],
        recv_sem.at[0],
    )
    for copy in loads[3:]:
        copy.wait()
    prepare(pops, charge, gray, table_ref, aux)
    settle(r0, recv_sem.at[0])
    spectrum = fdot(hy_ref[...], r0[...])
    rho = [spectrum[:, :128], spectrum[:, 128:]]
    mask = zero_mode_mask(cy, cz)
    rest = block_moments(rho, gtab, moments, partial, mask)
    swap_along_flow(
        lambda a: moments,
        lambda a: gathered.at[pl.ds(pl.multiple_of(40 * a, 8), 40), :],
        send_sem.at[1],
        recv_sem.at[1],
    )
    rest()
    settle(gathered, recv_sem.at[1])
    gathered_potential(
        [r[0:8, :] for r in rho], gtab, gathered, partial, mask, flow, modes
    )
    s1[...] = fdot(hy_ref[:, 0:128], modes[...])
    swap_across_plane(
        lambda b: rows_at(s1, 16 * lax.rem(b, CY), 16),
        lambda b: rows_at(r1, 16 * b, 16),
        send_sem.at[2],
        recv_sem.at[2],
    )
    settle(r1, recv_sem.at[2])
    for g in range(2):
        for c in range(2):
            blocks = [
                r1[128 * c + 16 * i : 128 * c + 16 * i + 16, 128 * g : 128 * g + 128]
                for i in range(8)
            ]
            for i, block in enumerate(swap_windows(blocks)):
                at = 128 * g + 16 * i
                joined[at : at + 16, 128 * c : 128 * c + 128] = block
    both = fdot(joined[...], back_ref[...])
    phi[...] = both[:, :128]
    field[2] = both[:, 128:]

    ahead, behind = lax.rem(flow + 1, FLOW), lax.rem(flow + FLOW - 1, FLOW)
    above, below = lax.rem(cy + 1, CY), lax.rem(cy + CY - 1, CY)
    copies = []

    def halo(n, source, target, device):
        copies.append(
            pltpu.make_async_remote_copy(
                src_ref=source,
                dst_ref=target,
                send_sem=hsend_sem.at[n],
                recv_sem=hrecv_sem.at[n],
                device_id=device,
                device_id_type=MESH,
            )
        )
        copies[-1].start()

    halo(0, phi.at[pl.ds(240, 16), :], xh.at[pl.ds(0, 16), :], {"flow": ahead})
    halo(1, phi.at[pl.ds(0, 16), :], xh.at[pl.ds(16, 16), :], {"flow": behind})
    ys[0:16, :] = phi[pl.ds(15, 16, stride=16), :]
    ys[16:32, :] = phi[pl.ds(0, 16, stride=16), :]
    halo(2, ys.at[pl.ds(0, 16), :], yh.at[pl.ds(0, 16), :], {"cy": above})
    halo(3, ys.at[pl.ds(16, 16), :], yh.at[pl.ds(16, 16), :], {"cy": below})
    for copy in copies:
        copy.wait()
    fill_fields(phi, xh, yh, field)
    finish(pops, aux, field, post)
    stores = [
        pltpu.make_async_copy(post, post_out, store_sem.at[0]),
        pltpu.make_async_copy(phi, phi_out, store_sem.at[1]),
    ]
    for copy in stores:
        copy.start()
    gather_faces(post, xf, yf, zf, corner)
    copies = []
    for n, (source, target, i, j, k) in enumerate(messages):
        copies.append(
            pltpu.make_async_remote_copy(
                src_ref=source,
                dst_ref=target,
                send_sem=fsend_sem.at[n],
                recv_sem=frecv_sem.at[n],
                device_id=partner(i, j, k),
                device_id_type=MESH,
            )
        )
        copies[-1].start()
    settle(s0.at[pl.ds(0, 240), :], send_sem.at[0])
    settle(gathered.at[pl.ds(0, 600), :], send_sem.at[1])
    settle(s0.at[pl.ds(0, 240), :], send_sem.at[2])
    for copy in copies:
        copy.wait()
    for n, (out, got) in enumerate(
        ((xo, xr), (yo, yr), (zo, zr), (zxo, zx), (zyo, zy), (co, cr))
    ):
        stores.append(pltpu.make_async_copy(got, out, store_sem.at[2 + n]))
        stores[-1].start()
    for copy in stores:
        copy.wait()


def collide_all(table, flow_pops, ion_pos, ion_neg, gray):
    rows, square = (256, 128), (256, 256)
    anywhere = pl.BlockSpec(memory_space=pl.ANY)
    shapes = [(33, 256, 128), rows, *FACE_SHAPES]
    buffers = [(128, 256), (128, 256), square, (672, 128), (7, 256, 128), (3, 256, 128), rows]
    buffers += [square, square, (40, 128), (640, 128), (2, 128, 128), (128, 256), (128, 256), square, square]
    buffers += [rows, (32, 128), (32, 128), (32, 128)]
    buffers += [(14, 16, 128), (14, 16, 128), (32, 128), (4, 8, 128)] + FACE_SHAPES
    return pl.pallas_call(
        main_kernel,
        out_shape=[jax.ShapeDtypeStruct(s, f32) for s in shapes],
        in_specs=[pl.BlockSpec(memory_space=pltpu.SMEM)] + [anywhere] * 8,
        out_specs=[anywhere] * 8,
        scratch_shapes=[pltpu.VMEM((33, 256, 128), f32)] * 2
        + [pltpu.VMEM(rows, jnp.int32)]
        + [pltpu.VMEM(s, f32) for s in buffers]
        + [pltpu.SemaphoreType.DMA((n,)) for n in (8, 3, 3, 4, 4, 13, 13, 8)],
        compiler_params=pltpu.CompilerParams(
            collective_id=0, has_side_effects=True, vmem_limit_bytes=VMEM_LIMIT
        ),
        name="collision",
    )(table, ion_pos, ion_neg, flow_pops, gray, *(jnp.asarray(t) for t in tables()))


def run_population(q, load, xr, yr, zr, zx, zy, cr, store):
    ex, ey, ez = DIRS[q]
    lane = lax.broadcasted_iota(jnp.int32, (16, 128), 1)
    row = lax.broadcasted_iota(jnp.int32, (16, 128), 0)
    last_row, first_row = (15, 0) if ey == 1 else (0, 15)
    for x in range(16):
        xs = x - ex
        outside = xs < 0 or xs > 15
        if outside:
            plane = xr[FACE[0, ex].index(q) + (0 if ex == 1 else 7)]
        else:
            plane = load(xs)
        if ey:
            if outside:
                n = {7: 0, 8: 1, 9: 2, 10: 3}[q]
                tile = 7 if ey == 1 else 0
                line = cr[n, tile : tile + 1, :]
            else:
                line = yr[FACE[1, ey].index(q) + (0 if ey == 1 else 7), xs : xs + 1, :]
            plane = jnp.where(row == first_row, line, pltpu.roll(plane, ey % 16, 0))
        if ez:
            face = FACE[2, ez].index(q)
            if outside:
                edge = zx[0:16, :] if ex == 1 else zx[16:32, :]
                block = 7 if ex == 1 else 0
            else:
                edge = zr[16 * (xs % 2) : 16 * (xs % 2) + 16, :]
                block = xs // 2
            at = 16 * block + 2 * face + (0 if ez == 1 else 1)
            if ey:
                beyond = zy[0 if ey == 1 else 1, 16 * (xs % 2) : 16 * (xs % 2) + 16, :]
                edge = pltpu.roll(jnp.where(row == last_row, beyond, edge), ey % 16, 0)
            goal = 0 if ez == 1 else 127
            moved = pltpu.roll(edge, (goal - at) % 128, 1) if (goal - at) % 128 else edge
            plane = jnp.where(lane == goal, moved, pltpu.roll(plane, ez % 128, 1))
        store(x, plane)


def running_kernel(
    post_hbm, phi_hbm, x_hbm, y_hbm, z_hbm, zx_hbm, zy_hbm, c_hbm,
    flow_out, pos_out, neg_out, phi_out,
    post, moved, xr, yr, zr, zx, zy, cr, in_sem, out_sem, face_sem,
):
    def output(q):
        if q < 19:
            return flow_out.at[q]
        return pos_out.at[q - 19] if q < 26 else neg_out.at[q - 26]

    pairs = ((x_hbm, xr), (y_hbm, yr), (z_hbm, zr), (zx_hbm, zx), (zy_hbm, zy), (c_hbm, cr))
    faces = [pltpu.make_async_copy(a, b, face_sem.at[n]) for n, (a, b) in enumerate(pairs)]
    reads = [pltpu.make_async_copy(post_hbm.at[q], post.at[q], in_sem.at[q]) for q in range(33)]
    writes = []
    for q in range(33):
        source = post if DIRS[q] == (0, 0, 0) else moved
        writes.append(pltpu.make_async_copy(source.at[q], output(q), out_sem.at[q]))
    writes.append(pltpu.make_async_copy(phi_hbm, phi_out, out_sem.at[33]))
    for copy in (reads[0], *faces, *reads[1:], writes[33]):
        copy.start()
    for q in range(33):
        reads[q].wait()
        if q == 1:
            for copy in faces:
                copy.wait()
        if DIRS[q] != (0, 0, 0):

            def load(x, q=q):
                return post[q, 16 * x : 16 * x + 16, :]

            def store(x, plane, q=q):
                moved[q, 16 * x : 16 * x + 16, :] = plane

            run_population(q, load, xr, yr, zr, zx, zy, cr, store)
        writes[q].start()
    for copy in writes:
        copy.wait()


def run_all(post, phi, faces):
    anywhere = pl.BlockSpec(memory_space=pl.ANY)
    shapes = [(19, 256, 128), (7, 256, 128), (7, 256, 128), (256, 128)]
    return pl.pallas_call(
        running_kernel,
        out_shape=[jax.ShapeDtypeStruct(s, f32) for s in shapes],
        in_specs=[anywhere] * 8,
        out_specs=[anywhere] * 4,
        scratch_shapes=[pltpu.VMEM((33, 256, 128), f32)] * 2
        + [pltpu.VMEM(s, f32) for s in FACE_SHAPES]
        + [pltpu.SemaphoreType.DMA((n,)) for n in (33, 34, 6)],
        compiler_params=pltpu.CompilerParams(vmem_limit_bytes=VMEM_LIMIT),
        name="running",
    )(post, phi, *faces)


def shards(flow_pops, ion_pos, ion_neg, gray_class, fraction_table):
    extent = gray_class.shape
    flow_pops = flow_pops.reshape(19, 256, 128)
    ion_pos = ion_pos.reshape(7, 256, 128)
    ion_neg = ion_neg.reshape(7, 256, 128)
    gray = gray_class.reshape(256, 128)
    post, phi, *faces = collide_all(fraction_table, flow_pops, ion_pos, ion_neg, gray)
    flow_new, pos_new, neg_new, phi = run_all(post, phi, faces)
    return (
        flow_new.reshape(19, *extent),
        pos_new.reshape(7, *extent),
        neg_new.reshape(7, *extent),
        phi.reshape(extent),
    )


def solution(mesh):
    in_specs = (
        P(None, "flow", "cy", "cz"),
        P(None, "flow", "cy", "cz"),
        P(None, "flow", "cy", "cz"),
        P("flow", "cy", "cz"),
        P(),
    )
    out_specs = (
        P(None, "flow", "cy", "cz"),
        P(None, "flow", "cy", "cz"),
        P(None, "flow", "cy", "cz"),
        P("flow", "cy", "cz"),
    )
    return jax.shard_map(shards, mesh=mesh, in_specs=in_specs, out_specs=out_specs, check_vma=False)
```

```python
import functools
import math

import jax
import jax.numpy as jnp
import numpy as np
from jax import lax
from jax.experimental import pallas as pl
from jax.experimental.pallas import tpu as pltpu
from jax.sharding import PartitionSpec as P

flow_dirs = (
    (0, 0, 0),
    (1, 0, 0),
    (-1, 0, 0),
    (0, 1, 0),
    (0, -1, 0),
    (0, 0, 1),
    (0, 0, -1),
    (1, 1, 0),
    (-1, -1, 0),
    (1, -1, 0),
    (-1, 1, 0),
    (1, 0, 1),
    (-1, 0, -1),
    (1, 0, -1),
    (-1, 0, 1),
    (0, 1, 1),
    (0, -1, -1),
    (0, 1, -1),
    (0, -1, 1),
)
flow_weights = (1.0 / 3.0,) + (1.0 / 18.0,) * 6 + (1.0 / 36.0,) * 12
ion_weights = (0.25,) + (0.125,) * 6
tau_flow = 0.8
tau_ion = 0.9
coupling = 2.0
mobility = 0.5
NX, NY, NZ = 256, 128, 256
FLOW, CY, CZ = 16, 8, 2
MESH = pl.DeviceIdType.MESH
f32 = jnp.float32
VMEM_LIMIT = 55 << 20

DIRS = flow_dirs + flow_dirs[:7] + flow_dirs[:7]
FACE = {
    (axis, sign): [q for q in range(33) if DIRS[q][axis] == sign]
    for axis in range(3)
    for sign in (1, -1)
}


def cas_table64(points_k, points_n, length):
    product = (points_k[:, None].astype(np.int64) * points_n[None, :]) % length
    angle = product * (2.0 * math.pi / length)
    return np.cos(angle) + np.sin(angle)


def cas_table(points_k, points_n, length):
    return cas_table64(points_k, points_n, length).astype(np.float32)


def tables():
    hy = cas_table(np.arange(NY), np.arange(NY), NY)
    z = np.arange(NZ)
    hz = cas_table(z, z, NZ)
    wide = cas_table64(z, z, NZ)
    slope = -0.5 * (np.roll(wide, -1, 1) - np.roll(wide, 1, 1))
    back = [
        np.concatenate([wide[:, 128 * c : 128 * c + 128], slope[:, 128 * c : 128 * c + 128]], 1)
        for c in range(CZ)
    ]
    lam_y = 4.0 * np.sin(np.pi * np.arange(NY) / NY) ** 2
    lam_z = 4.0 * np.sin(np.pi * z / NZ) ** 2
    t = 1.0 + 0.5 * (lam_y[:, None] + lam_z[None, :])
    mu = 1.0 / (t + np.sqrt(t * t - 1.0))
    gap = 1.0 / mu - mu
    gap[0, 0] = 1.0
    scale = coupling / (NY * NZ) / gap
    mu[0, 0] = scale[0, 0] = 0.0
    window = np.arange(128) // 16
    per_rank = []
    for b in range(16):
        m = np.tile(mu[:, 16 * b : 16 * b + 16], (1, 8))
        c = np.tile(scale[:, 16 * b : 16 * b + 16], (1, 8))
        packed = mu[:, 16 * b : 16 * b + 16].reshape(2, 8, 8, 16).transpose(0, 2, 1, 3).reshape(16, 128)
        per_rank.append(
            np.concatenate(
                [m, m ** (window + 1), m ** (8 - window), m**8, c, packed**16, 1.0 / (1.0 - packed**256)]
            )
        )
    return (
        np.concatenate([hy, hy], 1),
        hz.reshape(CZ, 128, NZ),
        np.stack(back).astype(np.float32),
        np.stack(per_rank).astype(np.float32),
    )


def place():
    return lax.axis_index("flow"), lax.axis_index("cy"), lax.axis_index("cz")


def fdot(left, right):
    return jnp.dot(left, right, precision=lax.Precision.HIGHEST, preferred_element_type=f32)


def settle(ref, sem):
    pltpu.make_async_copy(ref, ref, sem).wait()


def column_mask(shape, index):
    return lax.broadcasted_iota(jnp.int32, shape, 1) == index


def row_mask(shape, index):
    return lax.broadcasted_iota(jnp.int32, shape, 0) == index


def swap_across_plane(source, target, send_sem, recv_sem):
    _, cy, cz = place()
    me = cz * CY + cy
    for step_cy in (4, 5, 3, 2, 6, 7, 1, 0):
        for step_cz in (1, 0):
            if step_cy or step_cz:
                to_cy, to_cz = lax.rem(cy + step_cy, CY), lax.rem(cz + step_cz, CZ)
                pltpu.make_async_remote_copy(
                    src_ref=source(to_cz * CY + to_cy),
                    dst_ref=target(me),
                    send_sem=send_sem,
                    recv_sem=recv_sem,
                    device_id={"cy": to_cy, "cz": to_cz},
                    device_id_type=MESH,
                ).start()
    pltpu.make_async_copy(source(me), target(me), recv_sem).start()


def swap_along_flow(source, target, send_sem, recv_sem):
    me, _, _ = place()

    def step(k, carry):
        other = lax.rem(me + k, 16)
        pltpu.make_async_remote_copy(
            src_ref=source(other),
            dst_ref=target(me),
            send_sem=send_sem,
            recv_sem=recv_sem,
            device_id={"flow": other},
            device_id_type=MESH,
        ).start()
        return carry

    lax.fori_loop(1, 16, step, 0)
    pltpu.make_async_copy(source(me), target(me), recv_sem).start()


def rows_at(ref, start, count):
    return ref.at[pl.ds(pl.multiple_of(start, count), count), :]


def window_of(shape):
    return lax.broadcasted_iota(jnp.int32, shape, 1) // 16


def swap_windows(blocks):
    window = window_of(blocks[0].shape)
    for s in (1, 2, 4):
        high = (window & s) != 0
        moved = list(blocks)
        for i in range(8):
            if not i & s:
                low_block, high_block = blocks[i], blocks[i + s]
                moved[i] = jnp.where(high, pltpu.roll(high_block, 16 * s, 1), low_block)
                moved[i + s] = jnp.where(high, high_block, pltpu.roll(low_block, 128 - 16 * s, 1))
        blocks = moved
    return blocks


def spread(values, j):
    values = jnp.where(window_of(values.shape) == j, values, 0.0)
    for s in (16, 32, 64):
        values = values + pltpu.roll(values, s, 1)
    return values


def pack_windows(values, j):
    window = window_of((8, 128))
    packed = []
    for half in range(2):
        both = jnp.zeros((8, 128), f32)
        for i in range(8):
            tile = values[64 * half + 8 * i : 64 * half + 8 * i + 8, :]
            shift = (16 * (i - j)) % 128
            both = jnp.where(window == i, pltpu.roll(tile, shift, 1) if shift else tile, both)
        packed.append(both)
    return jnp.concatenate(packed, axis=0)


def scan_up(values, factor):
    window = window_of(values.shape)
    for s in (1, 2, 4):
        moved = pltpu.roll(values, 16 * s, 1)
        if factor is not None:
            moved = factor * moved
            factor = factor * factor
        values = values + jnp.where(window >= s, moved, 0.0)
    return values


def scan_down(values, factor):
    window = window_of(values.shape)
    for s in (1, 2, 4):
        moved = factor * pltpu.roll(values, 128 - 16 * s, 1)
        factor = factor * factor
        values = values + jnp.where(window < 8 - s, moved, 0.0)
    return values


def total_of(values):
    return jnp.sum(jnp.sum(values, axis=0, keepdims=True), axis=1, keepdims=True)


def zero_mode_mask(cy, cz):
    row = lax.broadcasted_iota(jnp.int32, (8, 128), 0)
    lane = lax.broadcasted_iota(jnp.int32, (8, 128), 1)
    here = jnp.where(cy + cz == 0, 1.0, 0.0)
    return jnp.where((row == 0) & (lane % 16 == 0), here, 0.0)


def block_moments(rho, gtab, moments, partial, mask):
    mu, near, far, eighth = (gtab[128 * n : 128 * n + 128, :] for n in range(4))
    up = [scan_up(r, mu) for r in rho]
    down = [scan_down(r, mu) for r in rho]
    moments[0:16, :] = pack_windows(up[1] + eighth * up[0], 7)
    moments[16:32, :] = pack_windows(down[0] + eighth * down[1], 0)
    window = window_of((8, 128)).astype(f32)
    at = (window - 7.5, window + 0.5)
    zero = [rho[g][0:8, :] * mask for g in range(2)]
    row = lax.broadcasted_iota(jnp.int32, (8, 128), 0)
    tile = jnp.zeros((8, 128), f32)
    for n in range(3):
        weighted = zero[0] * at[0] ** n + zero[1] * at[1] ** n if n else zero[0] + zero[1]
        tile = jnp.where(row == n, total_of(weighted), tile)
    moments[32:40, :] = tile

    def rest():
        partial[0] = up[0] + (down[0] - rho[0]) + far * spread(down[1], 0)
        partial[1] = up[1] + (down[1] - rho[1]) + near * spread(up[0], 7)

    return rest


def gathered_potential(rho_first, gtab, gathered, partial, mask, flow, out):
    def packed(source, start):
        return gathered[pl.ds(pl.multiple_of(40 * source + start, 8), 16), :]

    ratio, image = gtab[640:656, :], gtab[656:672, :]
    left, right = packed(flow, 0), packed(flow, 16)
    for d in range(15, 0, -1):
        left = packed(lax.rem(flow + 16 - d, 16), 0) + ratio * left
        right = packed(lax.rem(flow + d, 16), 16) + ratio * right
    left, right = left * image, right * image
    for tile in range(16):
        rows = slice(8 * tile, 8 * tile + 8)
        half = 8 * (tile // 8)
        from_left = spread(left[half : half + 8, :], tile % 8)
        from_right = spread(right[half : half + 8, :], tile % 8)
        near, far, eighth, scale = (
            gtab[128 * n + 8 * tile : 128 * n + 8 * tile + 8, :] for n in range(1, 5)
        )
        out[rows, 0:128] = scale * (
            partial[0, rows, :] + near * from_left + (far * eighth) * from_right
        )
        out[rows, 128:256] = scale * (
            partial[1, rows, :] + (near * eighth) * from_left + far * from_right
        )

    def moment(block, n):
        return gathered[40 * block + 32 + n : 40 * block + 33 + n, :]

    mean = sum((moment(n, 0) for n in range(1, 16)), moment(0, 0)) * (1.0 / NX)
    first = second = left_sum = left_first = jnp.zeros((1, 128), f32)
    for block in range(16):
        centre = 16.0 * block - 120.0
        own = moment(block, 0) - 16.0 * mean
        own_first = centre * own + moment(block, 1)
        first = first + own_first
        second = second + (centre * own_first + centre * moment(block, 1))
        second = second + (moment(block, 2) - 340.0 * mean)
        before = jnp.where(block < flow, 1.0, 0.0)
        left_sum = left_sum + before * own
        left_first = left_first + before * own_first
    window = window_of((8, 128)).astype(f32)
    centre = 16.0 * flow.astype(f32) - 120.0
    for g in range(2):
        at = centre + (window - 7.5 + 8.0 * g)
        zero = (rho_first[g] - mean) * mask
        to_here, to_here_first = scan_up(zero, None), scan_up(zero * at, None)
        upto, upto_first = left_sum + to_here, left_first + to_here_first
        left_sum = left_sum + spread(to_here, 7)
        left_first = left_first + spread(to_here_first, 7)
        distance = 2.0 * (at * upto - upto_first) + first
        value = (second - 2.0 * at * first) * (0.5 / NX) - 0.5 * distance
        lanes = slice(128 * g, 128 * g + 128)
        out[0:8, lanes] = out[0:8, lanes] + (coupling / (NY * NZ)) * (mask * value)


def pick_solid(gray, table_ref):
    bits = [(gray & (1 << n)) != 0 for n in range(4)]
    level = [table_ref[n] for n in range(16)]
    values = [jnp.where(bits[0], level[n + 1], level[n]) for n in range(0, 16, 2)]
    for n in range(1, 4):
        values = [
            jnp.where(bits[n], values[m + 1], values[m]) for m in range(0, len(values), 2)
        ]
    return values[0]


def fill_fields(phi, xh, yh, field):
    row = lax.broadcasted_iota(jnp.int32, (16, 128), 0)
    for x in range(16):
        here = phi[16 * x : 16 * x + 16, :]
        low = xh[0:16, :] if x == 0 else phi[16 * x - 16 : 16 * x, :]
        high = xh[16:32, :] if x == 15 else phi[16 * x + 16 : 16 * x + 32, :]
        field[0, 16 * x : 16 * x + 16, :] = -0.5 * (high - low)
        low = jnp.where(row == 0, yh[x : x + 1, :], pltpu.roll(here, 1, 0))
        high = jnp.where(row == 15, yh[16 + x : 17 + x, :], pltpu.roll(here, 15, 0))
        field[1, 16 * x : 16 * x + 16, :] = -0.5 * (high - low)


def prepare(pops, charge, gray, table_ref, aux):
    def block(i, carry):
        at = pl.ds(pl.multiple_of(8 * i, 8), 8)
        f = [pops[q, at, :] for q in range(33)]
        solid = pick_solid(gray[at, :], table_ref)
        density = sum(f[1:19], f[0])
        inverse = 1.0 / density
        for axis in range(3):
            plus = [f[q] for q in range(19) if flow_dirs[q][axis] == 1]
            minus = [f[q] for q in range(19) if flow_dirs[q][axis] == -1]
            aux[axis, at, :] = (sum(plus[1:], plus[0]) - sum(minus[1:], minus[0])) * inverse
        aux[3, at, :] = (tau_flow * charge[at, :]) * inverse
        omega = (1.0 - solid) * (1.0 / tau_flow)
        keep = 1.0 - omega - solid
        aux[4, at, :] = omega * density
        pops[0, at, :] = (keep + solid) * f[0]
        for q in range(1, 19, 2):
            pops[q, at, :] = keep * f[q] + solid * f[q + 1]
            pops[q + 1, at, :] = keep * f[q + 1] + solid * f[q]
        omega = (1.0 - solid) * (1.0 / tau_ion)
        keep = 1.0 - omega - solid
        for n, start in enumerate((19, 26)):
            g = f[start : start + 7]
            aux[5 + n, at, :] = omega * sum(g[1:], g[0])
            pops[start, at, :] = (keep + solid) * g[0]
            for q in range(1, 7, 2):
                pops[start + q, at, :] = keep * g[q] + solid * g[q + 1]
                pops[start + q + 1, at, :] = keep * g[q + 1] + solid * g[q]
        return carry

    lax.fori_loop(0, 32, block, 0)


def finish(pops, aux, field, post):
    def block(i, carry):
        at = pl.ds(pl.multiple_of(8 * i, 8), 8)
        velocity = [aux[d, at, :] for d in range(3)]
        electric = [field[d, at, :] for d in range(3)]
        push = aux[3, at, :]
        drift = [velocity[d] + push * electric[d] for d in range(3)]
        square = drift[0] * drift[0] + drift[1] * drift[1] + drift[2] * drift[2]
        mass = aux[4, at, :]
        base = 1.0 - 1.5 * square
        post[0, at, :] = pops[0, at, :] + (mass * flow_weights[0]) * base
        for q in range(1, 19, 2):
            along = None
            for d in range(3):
                if flow_dirs[q][d] and along is None:
                    along = drift[d] if flow_dirs[q][d] == 1 else -drift[d]
                elif flow_dirs[q][d]:
                    along = along + drift[d] if flow_dirs[q][d] == 1 else along - drift[d]
            scaled = mass * flow_weights[q]
            even = scaled * (base + 4.5 * along * along)
            odd = (3.0 * scaled) * along
            post[q, at, :] = pops[q, at, :] + (even + odd)
            post[q + 1, at, :] = pops[q + 1, at, :] + (even - odd)
        for start, n, sign in ((19, 5, mobility), (26, 6, -mobility)):
            mass = aux[n, at, :]
            post[start, at, :] = pops[start, at, :] + ion_weights[0] * mass
            even = ion_weights[1] * mass
            for d in range(3):
                q = start + 1 + 2 * d
                odd = (4.0 * even) * (velocity[d] + sign * electric[d])
                post[q, at, :] = pops[q, at, :] + (even + odd)
                post[q + 1, at, :] = pops[q + 1, at, :] + (even - odd)
        return carry

    lax.fori_loop(0, 32, block, 0)


def gather_faces(post, xf, yf, zf, corner):
    for n, q in enumerate(FACE[0, 1]):
        xf[n] = post[q, 240:256, :]
    for n, q in enumerate(FACE[0, -1]):
        xf[7 + n] = post[q, 0:16, :]
    for n, q in enumerate(FACE[1, 1]):
        yf[n] = post[q, pl.ds(15, 16, stride=16), :]
    for n, q in enumerate(FACE[1, -1]):
        yf[7 + n] = post[q, pl.ds(0, 16, stride=16), :]
    lane = lax.broadcasted_iota(jnp.int32, (16, 128), 1)
    packed = [jnp.zeros((16, 128), f32), jnp.zeros((16, 128), f32)]
    for n, (up, down) in enumerate(zip(FACE[2, 1], FACE[2, -1])):
        for x in range(16):
            both = jnp.where(
                lane == 127, post[up, 16 * x : 16 * x + 16, :], post[down, 16 * x : 16 * x + 16, :]
            )
            at = 16 * (x // 2) + 2 * n
            moved = pltpu.roll(both, (at + 1) % 128, 1)
            packed[x % 2] = jnp.where((lane == at) | (lane == at + 1), moved, packed[x % 2])
    zf[0:16, :] = packed[0]
    zf[16:32, :] = packed[1]
    corner[0] = post[7, 248:256, :]
    corner[1] = post[8, 0:8, :]
    corner[2] = post[9, 240:248, :]
    corner[3] = post[10, 8:16, :]


def face_messages(xf, yf, zf, corner, xr, yr, zr, zx, zy, cr):
    up, down = pl.ds(0, 7), pl.ds(7, 7)
    low, high = pl.ds(0, 16), pl.ds(16, 16)
    return [
        (xf.at[up], xr.at[up], 1, 0, 0),
        (xf.at[down], xr.at[down], -1, 0, 0),
        (yf.at[up], yr.at[up], 0, 1, 0),
        (yf.at[down], yr.at[down], 0, -1, 0),
        (zf, zr, 0, 0, 1),
        (zf.at[high], zx.at[low], 1, 0, 1),
        (zf.at[low], zx.at[high], -1, 0, 1),
        (zf, zy.at[0], 0, 1, 1),
        (zf, zy.at[1], 0, -1, 1),
        (corner.at[0], cr.at[0], 1, 1, 0),
        (corner.at[1], cr.at[1], -1, -1, 0),
        (corner.at[2], cr.at[2], 1, -1, 0),
        (corner.at[3], cr.at[3], -1, 1, 0),
    ]


def partner(step_flow, step_cy, cross):
    flow, cy, cz = place()
    return (
        lax.rem(flow + FLOW + step_flow, FLOW),
        lax.rem(cy + CY + step_cy, CY),
        1 - cz if cross else cz,
    )


def run_inside(post, moved):
    for q in range(33):
        ex, ey, ez = DIRS[q]
        for x in range(16):
            if 0 <= x - ex <= 15:
                plane = post[q, 16 * (x - ex) : 16 * (x - ex) + 16, :]
                if ey:
                    plane = pltpu.roll(plane, ey % 16, 0)
                if ez:
                    plane = pltpu.roll(plane, ez % 128, 1)
                moved[q, 16 * x : 16 * x + 16, :] = plane


def run_edges(moved, xr, yr, zr, zx, zy, cr):
    lane = lax.broadcasted_iota(jnp.int32, (16, 128), 1)
    row = lax.broadcasted_iota(jnp.int32, (16, 128), 0)
    for q in range(1, 33):
        ex, ey, ez = DIRS[q]
        edge_x = 0 if ex == 1 else 15
        first_row, last_row = (0, 15) if ey == 1 else (15, 0)
        if ex:
            plane = xr[FACE[0, ex].index(q) + (0 if ex == 1 else 7)]
            if ey:
                plane = pltpu.roll(plane, ey % 16, 0)
            if ez:
                plane = pltpu.roll(plane, ez % 128, 1)
            moved[q, 16 * edge_x : 16 * edge_x + 16, :] = plane
        if ey:
            lines = yr[FACE[1, ey].index(q) + (0 if ey == 1 else 7)]
            if ex:
                n = {7: 0, 8: 1, 9: 2, 10: 3}[q]
                tile = 7 if ey == 1 else 0
                lines = jnp.where(row == edge_x, cr[n, tile : tile + 1, :], pltpu.roll(lines, ex % 16, 0))
            if ez:
                lines = pltpu.roll(lines, ez % 128, 1)
            moved[q, pl.ds(first_row, 16, stride=16), :] = lines
        if ez:
            face = FACE[2, ez].index(q)
            goal = 0 if ez == 1 else 127
            for x in range(16):
                xs = x - ex
                if 0 <= xs <= 15:
                    edge = zr[16 * (xs % 2) : 16 * (xs % 2) + 16, :]
                    block = xs // 2
                else:
                    edge = zx[0:16, :] if ex == 1 else zx[16:32, :]
                    block = 7 if ex == 1 else 0
                if ey:
                    beyond = zy[0 if ey == 1 else 1, 16 * (xs % 2) : 16 * (xs % 2) + 16, :]
                    edge = pltpu.roll(jnp.where(row == last_row, beyond, edge), ey % 16, 0)
                shift = (goal - (16 * block + 2 * face + (0 if ez == 1 else 1))) % 128
                column = pltpu.roll(edge, shift, 1) if shift else edge
                here = slice(16 * x, 16 * x + 16)
                moved[q, here, :] = jnp.where(lane == goal, column, moved[q, here, :])


FACE_SHAPES = [(14, 16, 128), (14, 16, 128), (32, 128), (32, 128), (2, 32, 128), (4, 8, 128)]


def main_kernel(
    table_ref, pos_hbm, neg_hbm, flow_hbm, gray_hbm, hy_hbm, hz_hbm, back_hbm, gtab_hbm,
    moved, phi,
    pops, post, gray, hy_ref, hz_ref, back_ref, gtab, aux, field, charge,
    s0, r0, moments, gathered, partial, modes, s1, r1, joined, ys, xh, yh,
    xf, yf, zf, corner, xr, yr, zr, zx, zy, cr,
    load_sem, send_sem, recv_sem, hsend_sem, hrecv_sem, fsend_sem, frecv_sem,
):
    flow, cy, cz = place()
    me = cz * CY + cy
    loads = [
        pltpu.make_async_copy(source, target, load_sem.at[n])
        for n, (source, target) in enumerate(
            (
                (pos_hbm, pops.at[pl.ds(19, 7)]),
                (neg_hbm, pops.at[pl.ds(26, 7)]),
                (hz_hbm.at[cz], hz_ref),
                (flow_hbm, pops.at[pl.ds(0, 19)]),
                (gray_hbm, gray),
                (hy_hbm, hy_ref),
                (gtab_hbm.at[me], gtab),
                (back_hbm.at[cz], back_ref),
            )
        )
    ]
    for copy in loads:
        copy.start()
    barrier = pltpu.get_barrier_semaphore()

    def greet(k, carry):
        other = lax.rem(me + k, 16)
        pl.semaphore_signal(
            barrier,
            inc=1,
            device_id={"cy": lax.rem(other, CY), "cz": lax.div(other, CY)},
            device_id_type=MESH,
        )
        pl.semaphore_signal(
            barrier, inc=1, device_id={"flow": lax.rem(flow + k, 16)}, device_id_type=MESH
        )
        return carry

    lax.fori_loop(1, 16, greet, 0)
    messages = face_messages(xf, yf, zf, corner, xr, yr, zr, zx, zy, cr)
    strangers = [m[2:] for m in messages if m[2] and (m[3] or m[4])]
    for i, j, k in strangers:
        pl.semaphore_signal(barrier, inc=1, device_id=partner(i, j, k), device_id_type=MESH)
    for copy in loads[:3]:
        copy.wait()
    pos = pops[19]
    neg = pops[26]
    for q in range(1, 7):
        pos = pos + pops[19 + q]
        neg = neg + pops[26 + q]
    charge[...] = pos - neg

    spectrum = fdot(charge[...], hz_ref[...])
    for g in range(2):
        for c in range(2):
            blocks = [
                spectrum[128 * g + 16 * i : 128 * g + 16 * i + 16, 128 * c : 128 * c + 128]
                for i in range(8)
            ]
            for i, block in enumerate(swap_windows(blocks)):
                at = 16 * (8 * c + i)
                s0[at : at + 16, 128 * g : 128 * g + 128] = block
    pl.semaphore_wait(barrier, 30 + len(strangers))
    swap_across_plane(
        lambda b: rows_at(s0, 16 * b, 16),
        lambda b: rows_at(r0, 16 * b, 16),
        send_sem.at[0],
        recv_sem.at[0],
    )
    for copy in loads[3:]:
        copy.wait()
    prepare(pops, charge, gray, table_ref, aux)
    settle(r0, recv_sem.at[0])
    spectrum = fdot(hy_ref[...], r0[...])
    rho = [spectrum[:, :128], spectrum[:, 128:]]
    mask = zero_mode_mask(cy, cz)
    rest = block_moments(rho, gtab, moments, partial, mask)
    swap_along_flow(
        lambda a: moments,
        lambda a: gathered.at[pl.ds(pl.multiple_of(40 * a, 8), 40), :],
        send_sem.at[1],
        recv_sem.at[1],
    )
    rest()
    settle(gathered, recv_sem.at[1])
    gathered_potential(
        [r[0:8, :] for r in rho], gtab, gathered, partial, mask, flow, modes
    )
    s1[...] = fdot(hy_ref[:, 0:128], modes[...])
    swap_across_plane(
        lambda b: rows_at(s1, 16 * lax.rem(b, CY), 16),
        lambda b: rows_at(r1, 16 * b, 16),
        send_sem.at[2],
        recv_sem.at[2],
    )
    settle(r1, recv_sem.at[2])
    for g in range(2):
        for c in range(2):
            blocks = [
                r1[128 * c + 16 * i : 128 * c + 16 * i + 16, 128 * g : 128 * g + 128]
                for i in range(8)
            ]
            for i, block in enumerate(swap_windows(blocks)):
                at = 128 * g + 16 * i
                joined[at : at + 16, 128 * c : 128 * c + 128] = block
    both = fdot(joined[...], back_ref[...])
    phi[...] = both[:, :128]
    field[2] = both[:, 128:]

    ahead, behind = lax.rem(flow + 1, FLOW), lax.rem(flow + FLOW - 1, FLOW)
    above, below = lax.rem(cy + 1, CY), lax.rem(cy + CY - 1, CY)
    copies = []

    def halo(n, source, target, device):
        copies.append(
            pltpu.make_async_remote_copy(
                src_ref=source,
                dst_ref=target,
                send_sem=hsend_sem.at[n],
                recv_sem=hrecv_sem.at[n],
                device_id=device,
                device_id_type=MESH,
            )
        )
        copies[-1].start()

    halo(0, phi.at[pl.ds(240, 16), :], xh.at[pl.ds(0, 16), :], {"flow": ahead})
    halo(1, phi.at[pl.ds(0, 16), :], xh.at[pl.ds(16, 16), :], {"flow": behind})
    ys[0:16, :] = phi[pl.ds(15, 16, stride=16), :]
    ys[16:32, :] = phi[pl.ds(0, 16, stride=16), :]
    halo(2, ys.at[pl.ds(0, 16), :], yh.at[pl.ds(0, 16), :], {"cy": above})
    halo(3, ys.at[pl.ds(16, 16), :], yh.at[pl.ds(16, 16), :], {"cy": below})
    for copy in copies:
        copy.wait()
    fill_fields(phi, xh, yh, field)
    finish(pops, aux, field, post)
    gather_faces(post, xf, yf, zf, corner)
    copies = []
    for n, (source, target, i, j, k) in enumerate(messages):
        copies.append(
            pltpu.make_async_remote_copy(
                src_ref=source,
                dst_ref=target,
                send_sem=fsend_sem.at[n],
                recv_sem=frecv_sem.at[n],
                device_id=partner(i, j, k),
                device_id_type=MESH,
            )
        )
        copies[-1].start()
    run_inside(post, moved)
    settle(s0.at[pl.ds(0, 240), :], send_sem.at[0])
    settle(gathered.at[pl.ds(0, 600), :], send_sem.at[1])
    settle(s0.at[pl.ds(0, 240), :], send_sem.at[2])
    for copy in copies:
        copy.wait()
    run_edges(moved, xr, yr, zr, zx, zy, cr)


def collide_all(table, flow_pops, ion_pos, ion_neg, gray):
    rows, square = (256, 128), (256, 256)
    anywhere = pl.BlockSpec(memory_space=pl.ANY)
    shapes = [(33, 256, 128), rows]
    buffers = [(128, 256), (128, 256), square, (672, 128), (7, 256, 128), (3, 256, 128), rows]
    buffers += [square, square, (40, 128), (640, 128), (2, 128, 128), (128, 256), (128, 256), square, square]
    buffers += [(32, 128), (32, 128), (32, 128)]
    buffers += [(14, 16, 128), (14, 16, 128), (32, 128), (4, 8, 128)] + FACE_SHAPES
    return pl.pallas_call(
        main_kernel,
        out_shape=[pltpu.VMEM(s, f32) for s in shapes],
        in_specs=[pl.BlockSpec(memory_space=pltpu.SMEM)] + [anywhere] * 8,
        out_specs=[pl.BlockSpec(memory_space=pltpu.VMEM)] * 2,
        scratch_shapes=[pltpu.VMEM((33, 256, 128), f32)] * 2
        + [pltpu.VMEM(rows, jnp.int32)]
        + [pltpu.VMEM(s, f32) for s in buffers]
        + [pltpu.SemaphoreType.DMA((n,)) for n in (8, 3, 3, 4, 4, 13, 13)],
        compiler_params=pltpu.CompilerParams(
            collective_id=0, has_side_effects=True, vmem_limit_bytes=VMEM_LIMIT
        ),
        name="collision",
    )(table, ion_pos, ion_neg, flow_pops, gray, *(jnp.asarray(t) for t in tables()))


def store_kernel(moved, phi, flow_out, pos_out, neg_out, phi_out, sem):
    copies = [pltpu.make_async_copy(phi, phi_out, sem.at[33])]
    for q in range(33):
        target = flow_out.at[q] if q < 19 else pos_out.at[q - 19] if q < 26 else neg_out.at[q - 26]
        copies.append(pltpu.make_async_copy(moved.at[q], target, sem.at[q]))
    for copy in copies:
        copy.start()
    for copy in copies:
        copy.wait()


def store_all(moved, phi):
    shapes = [(19, 256, 128), (7, 256, 128), (7, 256, 128), (256, 128)]
    return pl.pallas_call(
        store_kernel,
        out_shape=[jax.ShapeDtypeStruct(s, f32) for s in shapes],
        in_specs=[pl.BlockSpec(memory_space=pltpu.VMEM)] * 2,
        out_specs=[pl.BlockSpec(memory_space=pl.ANY)] * 4,
        scratch_shapes=[pltpu.SemaphoreType.DMA((34,))],
        compiler_params=pltpu.CompilerParams(vmem_limit_bytes=2 << 20),
        name="results",
    )(moved, phi)


def shards(flow_pops, ion_pos, ion_neg, gray_class, fraction_table):
    extent = gray_class.shape
    flow_pops = flow_pops.reshape(19, 256, 128)
    ion_pos = ion_pos.reshape(7, 256, 128)
    ion_neg = ion_neg.reshape(7, 256, 128)
    gray = gray_class.reshape(256, 128)
    moved, phi = collide_all(fraction_table, flow_pops, ion_pos, ion_neg, gray)
    flow_new, pos_new, neg_new, phi = store_all(moved, phi)
    return (
        flow_new.reshape(19, *extent),
        pos_new.reshape(7, *extent),
        neg_new.reshape(7, *extent),
        phi.reshape(extent),
    )


def solution(mesh):
    in_specs = (
        P(None, "flow", "cy", "cz"),
        P(None, "flow", "cy", "cz"),
        P(None, "flow", "cy", "cz"),
        P("flow", "cy", "cz"),
        P(),
    )
    out_specs = (
        P(None, "flow", "cy", "cz"),
        P(None, "flow", "cy", "cz"),
        P(None, "flow", "cy", "cz"),
        P("flow", "cy", "cz"),
    )
    return jax.shard_map(shards, mesh=mesh, in_specs=in_specs, out_specs=out_specs, check_vma=False)
```

```python
import functools
import math

import jax
import jax.numpy as jnp
import numpy as np
from jax import lax
from jax.experimental import pallas as pl
from jax.experimental.pallas import tpu as pltpu
from jax.sharding import PartitionSpec as P

flow_dirs = (
    (0, 0, 0),
    (1, 0, 0),
    (-1, 0, 0),
    (0, 1, 0),
    (0, -1, 0),
    (0, 0, 1),
    (0, 0, -1),
    (1, 1, 0),
    (-1, -1, 0),
    (1, -1, 0),
    (-1, 1, 0),
    (1, 0, 1),
    (-1, 0, -1),
    (1, 0, -1),
    (-1, 0, 1),
    (0, 1, 1),
    (0, -1, -1),
    (0, 1, -1),
    (0, -1, 1),
)
flow_weights = (1.0 / 3.0,) + (1.0 / 18.0,) * 6 + (1.0 / 36.0,) * 12
ion_weights = (0.25,) + (0.125,) * 6
tau_flow = 0.8
tau_ion = 0.9
coupling = 2.0
mobility = 0.5
NX, NY, NZ = 256, 128, 256
FLOW, CY, CZ = 16, 8, 2
MESH = pl.DeviceIdType.MESH
f32 = jnp.float32
VMEM_LIMIT = 55 << 20

DIRS = flow_dirs + flow_dirs[:7] + flow_dirs[:7]
FACE = {
    (axis, sign): [q for q in range(33) if DIRS[q][axis] == sign]
    for axis in range(3)
    for sign in (1, -1)
}


def cas_table64(points_k, points_n, length):
    product = (points_k[:, None].astype(np.int64) * points_n[None, :]) % length
    angle = product * (2.0 * math.pi / length)
    return np.cos(angle) + np.sin(angle)


def cas_table(points_k, points_n, length):
    return cas_table64(points_k, points_n, length).astype(np.float32)


def pack_rank(table, b):
    part = table[:, 16 * b : 16 * b + 16].reshape(2, 8, 8, 16)
    return part.transpose(0, 2, 1, 3).reshape(16, 128)


def tables():
    hy = cas_table(np.arange(NY), np.arange(NY), NY)
    z = np.arange(NZ)
    hz = cas_table(z, z, NZ)
    wide = cas_table64(z, z, NZ)
    slope = -0.5 * (np.roll(wide, -1, 1) - np.roll(wide, 1, 1))
    back = [
        np.concatenate([wide[:, 128 * c : 128 * c + 128], slope[:, 128 * c : 128 * c + 128]], 1)
        for c in range(CZ)
    ]
    lam_y = 4.0 * np.sin(np.pi * np.arange(NY) / NY) ** 2
    lam_z = 4.0 * np.sin(np.pi * z / NZ) ** 2
    t = 1.0 + 0.5 * (lam_y[:, None] + lam_z[None, :])
    mu = 1.0 / (t + np.sqrt(t * t - 1.0))
    gap = 1.0 / mu - mu
    gap[0, 0] = 1.0
    scale = coupling / (NY * NZ) / gap
    mu[0, 0] = scale[0, 0] = 0.0
    window = np.arange(128) // 16
    per_rank = []
    for b in range(16):
        m = np.tile(mu[:, 16 * b : 16 * b + 16], (1, 8))
        c = np.tile(scale[:, 16 * b : 16 * b + 16], (1, 8))
        packed = pack_rank(mu, b)
        per_rank.append(
            np.concatenate(
                [m, m ** (window + 1), m ** (8 - window), m**8, c]
                + [packed**16, 1.0 / (1.0 - packed**256), packed, pack_rank(scale, b)]
            )
        )
    return (
        np.concatenate([hy, hy], 1),
        hz.reshape(CZ, 128, NZ),
        np.stack(back).astype(np.float32),
        np.stack(per_rank).astype(np.float32),
    )


def place():
    return lax.axis_index("flow"), lax.axis_index("cy"), lax.axis_index("cz")


def fdot(left, right):
    return jnp.dot(left, right, precision=lax.Precision.HIGHEST, preferred_element_type=f32)


def settle(ref, sem):
    pltpu.make_async_copy(ref, ref, sem).wait()


def column_mask(shape, index):
    return lax.broadcasted_iota(jnp.int32, shape, 1) == index


def row_mask(shape, index):
    return lax.broadcasted_iota(jnp.int32, shape, 0) == index


def swap_across_plane(source, target, send_sem, recv_sem):
    _, cy, cz = place()
    me = cz * CY + cy
    for step_cy in (4, 5, 3, 2, 6, 7, 1, 0):
        for step_cz in (1, 0):
            if step_cy or step_cz:
                to_cy, to_cz = lax.rem(cy + step_cy, CY), lax.rem(cz + step_cz, CZ)
                pltpu.make_async_remote_copy(
                    src_ref=source(to_cz * CY + to_cy),
                    dst_ref=target(me),
                    send_sem=send_sem,
                    recv_sem=recv_sem,
                    device_id={"cy": to_cy, "cz": to_cz},
                    device_id_type=MESH,
                ).start()
    pltpu.make_async_copy(source(me), target(me), recv_sem).start()


def swap_along_flow(source, target, send_sem, recv_sem):
    me, _, _ = place()

    def step(k, carry):
        other = lax.rem(me + k, 16)
        pltpu.make_async_remote_copy(
            src_ref=source(other),
            dst_ref=target(me),
            send_sem=send_sem,
            recv_sem=recv_sem,
            device_id={"flow": other},
            device_id_type=MESH,
        ).start()
        return carry

    lax.fori_loop(1, 16, step, 0)
    pltpu.make_async_copy(source(me), target(me), recv_sem).start()


def rows_at(ref, start, count):
    return ref.at[pl.ds(pl.multiple_of(start, count), count), :]


def window_of(shape):
    return lax.broadcasted_iota(jnp.int32, shape, 1) // 16


def swap_windows(blocks):
    window = window_of(blocks[0].shape)
    for s in (1, 2, 4):
        high = (window & s) != 0
        moved = list(blocks)
        for i in range(8):
            if not i & s:
                low_block, high_block = blocks[i], blocks[i + s]
                moved[i] = jnp.where(high, pltpu.roll(high_block, 16 * s, 1), low_block)
                moved[i + s] = jnp.where(high, high_block, pltpu.roll(low_block, 128 - 16 * s, 1))
        blocks = moved
    return blocks


def spread(values, j):
    values = jnp.where(window_of(values.shape) == j, values, 0.0)
    for s in (16, 32, 64):
        values = values + pltpu.roll(values, s, 1)
    return values


def pack_windows(values, j):
    window = window_of((8, 128))
    packed = []
    for half in range(2):
        both = jnp.zeros((8, 128), f32)
        for i in range(8):
            tile = values[64 * half + 8 * i : 64 * half + 8 * i + 8, :]
            shift = (16 * (i - j)) % 128
            both = jnp.where(window == i, pltpu.roll(tile, shift, 1) if shift else tile, both)
        packed.append(both)
    return jnp.concatenate(packed, axis=0)


def scan_up(values, factor):
    window = window_of(values.shape)
    for s in (1, 2, 4):
        moved = pltpu.roll(values, 16 * s, 1)
        if factor is not None:
            moved = factor * moved
            factor = factor * factor
        values = values + jnp.where(window >= s, moved, 0.0)
    return values


def scan_down(values, factor):
    window = window_of(values.shape)
    for s in (1, 2, 4):
        moved = factor * pltpu.roll(values, 128 - 16 * s, 1)
        factor = factor * factor
        values = values + jnp.where(window < 8 - s, moved, 0.0)
    return values


def total_of(values):
    return jnp.sum(jnp.sum(values, axis=0, keepdims=True), axis=1, keepdims=True)


def zero_mode_mask(cy, cz):
    row = lax.broadcasted_iota(jnp.int32, (8, 128), 0)
    lane = lax.broadcasted_iota(jnp.int32, (8, 128), 1)
    here = jnp.where(cy + cz == 0, 1.0, 0.0)
    return jnp.where((row == 0) & (lane % 16 == 0), here, 0.0)


def block_moments(rho, gtab, moments, partial, mask):
    mu, near, far, eighth = (gtab[128 * n : 128 * n + 128, :] for n in range(4))
    up = [scan_up(r, mu) for r in rho]
    down = [scan_down(r, mu) for r in rho]
    moments[0:16, :] = pack_windows(up[1] + eighth * up[0], 7)
    moments[16:32, :] = pack_windows(down[0] + eighth * down[1], 0)
    window = window_of((8, 128)).astype(f32)
    at = (window - 7.5, window + 0.5)
    zero = [rho[g][0:8, :] * mask for g in range(2)]
    row = lax.broadcasted_iota(jnp.int32, (8, 128), 0)
    tile = jnp.zeros((8, 128), f32)
    for n in range(3):
        weighted = zero[0] * at[0] ** n + zero[1] * at[1] ** n if n else zero[0] + zero[1]
        tile = jnp.where(row == n, total_of(weighted), tile)
    moments[32:40, :] = tile

    def rest():
        partial[0] = up[0] + (down[0] - rho[0]) + far * spread(down[1], 0)
        partial[1] = up[1] + (down[1] - rho[1]) + near * spread(up[0], 7)

    return rest


def gathered_potential(rho_first, gtab, gathered, partial, mask, flow, out):
    def packed(source, start):
        return gathered[pl.ds(pl.multiple_of(40 * source + start, 8), 16), :]

    ratio, image = gtab[640:656, :], gtab[656:672, :]
    left, right = packed(flow, 0), packed(flow, 16)
    for d in range(15, 0, -1):
        left = packed(lax.rem(flow + 16 - d, 16), 0) + ratio * left
        right = packed(lax.rem(flow + d, 16), 16) + ratio * right
    left, right = left * image, right * image
    one, packed_scale = gtab[672:688, :], gtab[688:704, :]
    behind = packed_scale * (left + one * (packed(flow, 16) + ratio * right))
    ahead = packed_scale * (right + one * (packed(flow, 0) + ratio * left))
    small = window_of((8, 128))
    for tile in range(16):
        rows = slice(8 * tile, 8 * tile + 8)
        half = 8 * (tile // 8)
        from_left = spread(left[half : half + 8, :], tile % 8)
        from_right = spread(right[half : half + 8, :], tile % 8)
        part, j = slice(half, half + 8), tile % 8
        at_first, at_second = (-16 * j) % 128, (16 - 16 * j) % 128
        first = pltpu.roll(behind[part, :], at_first, 1) if at_first else behind[part, :]
        second = pltpu.roll(ahead[part, :], at_second, 1) if at_second else ahead[part, :]
        out[rows, 256:384] = jnp.where(small == 0, first, jnp.where(small == 1, second, 0.0))
        near, far, eighth, scale = (
            gtab[128 * n + 8 * tile : 128 * n + 8 * tile + 8, :] for n in range(1, 5)
        )
        out[rows, 0:128] = scale * (
            partial[0, rows, :] + near * from_left + (far * eighth) * from_right
        )
        out[rows, 128:256] = scale * (
            partial[1, rows, :] + (near * eighth) * from_left + far * from_right
        )

    def moment(block, n):
        return gathered[40 * block + 32 + n : 40 * block + 33 + n, :]

    mean = sum((moment(n, 0) for n in range(1, 16)), moment(0, 0)) * (1.0 / NX)
    moment_first = second_moment = left_sum = left_first = jnp.zeros((1, 128), f32)
    for block in range(16):
        centre = 16.0 * block - 120.0
        own = moment(block, 0) - 16.0 * mean
        own_first = centre * own + moment(block, 1)
        moment_first = moment_first + own_first
        second_moment = second_moment + (centre * own_first + centre * moment(block, 1))
        second_moment = second_moment + (moment(block, 2) - 340.0 * mean)
        before = jnp.where(block < flow, 1.0, 0.0)
        left_sum = left_sum + before * own
        left_first = left_first + before * own_first
    window = window_of((8, 128)).astype(f32)
    centre = 16.0 * flow.astype(f32) - 120.0
    start_sum, start_first = left_sum, left_first
    for g in range(2):
        at = centre + (window - 7.5 + 8.0 * g)
        zero = (rho_first[g] - mean) * mask
        to_here, to_here_first = scan_up(zero, None), scan_up(zero * at, None)
        upto, upto_first = left_sum + to_here, left_first + to_here_first
        left_sum = left_sum + spread(to_here, 7)
        left_first = left_first + spread(to_here_first, 7)
        distance = 2.0 * (at * upto - upto_first) + moment_first
        value = (second_moment - 2.0 * at * moment_first) * (0.5 / NX) - 0.5 * distance
        lanes = slice(128 * g, 128 * g + 128)
        out[0:8, lanes] = out[0:8, lanes] + (coupling / (NY * NZ)) * (mask * value)
    at = centre - 8.5 + 17.0 * window
    upto = jnp.where(small == 0, start_sum, left_sum)
    upto_first = jnp.where(small == 0, start_first, left_first)
    distance = 2.0 * (at * upto - upto_first) + moment_first
    value = (second_moment - 2.0 * at * moment_first) * (0.5 / NX) - 0.5 * distance
    value = jnp.where(small < 2, mask * value, 0.0)
    out[0:8, 256:384] = out[0:8, 256:384] + (coupling / (NY * NZ)) * value


def send_halo(modes_y, s1):
    window = window_of((8, 128))
    for pair in range(4):
        tile = jnp.zeros((8, 128), f32)
        for k in range(4):
            piece = modes_y[pl.ds(32 * pair + k, 8, stride=4), :]
            piece = pltpu.roll(piece, 32 * k, 1) if k else piece
            tile = jnp.where(window // 2 == k, piece, tile)
        for n in range(2):
            at = 40 * (2 * pair + n) + 32
            s1[at : at + 4, :] = tile[4 * n : 4 * n + 4, :]
    for block in range(CY):
        for side, (other, line) in enumerate((((block - 1) % CY, 15), ((block + 1) % CY, 0))):
            for g in range(2):
                to, at = 40 * block + 36 + 2 * side + g, 40 * other + 16 * g + line
                s1[to : to + 1, :] = s1[at : at + 1, :]


def receive_halo(rows, xh, yh):
    for side in range(2):
        for r in range(4):
            at = 16 * side + 4 * r
            xh[at : at + 4, :] = rows[pl.ds(8 * side + r, 4, stride=16), :]
        for g in range(2):
            at = 16 * side + 8 * g
            yh[at : at + 8, :] = rows[pl.ds(4 + 2 * side + g, 8, stride=8), :]


def pick_solid(gray, table_ref):
    bits = [(gray & (1 << n)) != 0 for n in range(4)]
    level = [table_ref[n] for n in range(16)]
    values = [jnp.where(bits[0], level[n + 1], level[n]) for n in range(0, 16, 2)]
    for n in range(1, 4):
        values = [
            jnp.where(bits[n], values[m + 1], values[m]) for m in range(0, len(values), 2)
        ]
    return values[0]


def fill_fields(phi, xh, yh, field):
    row = lax.broadcasted_iota(jnp.int32, (16, 128), 0)
    for x in range(16):
        here = phi[16 * x : 16 * x + 16, :]
        low = xh[0:16, :] if x == 0 else phi[16 * x - 16 : 16 * x, :]
        high = xh[16:32, :] if x == 15 else phi[16 * x + 16 : 16 * x + 32, :]
        field[0, 16 * x : 16 * x + 16, :] = -0.5 * (high - low)
        low = jnp.where(row == 0, yh[x : x + 1, :], pltpu.roll(here, 1, 0))
        high = jnp.where(row == 15, yh[16 + x : 17 + x, :], pltpu.roll(here, 15, 0))
        field[1, 16 * x : 16 * x + 16, :] = -0.5 * (high - low)


def prepare(pops, charge, gray, table_ref, aux):
    def block(i, carry):
        at = pl.ds(pl.multiple_of(8 * i, 8), 8)
        f = [pops[q, at, :] for q in range(33)]
        solid = pick_solid(gray[at, :], table_ref)
        density = sum(f[1:19], f[0])
        inverse = 1.0 / density
        for axis in range(3):
            plus = [f[q] for q in range(19) if flow_dirs[q][axis] == 1]
            minus = [f[q] for q in range(19) if flow_dirs[q][axis] == -1]
            aux[axis, at, :] = (sum(plus[1:], plus[0]) - sum(minus[1:], minus[0])) * inverse
        aux[3, at, :] = (tau_flow * charge[at, :]) * inverse
        omega = (1.0 - solid) * (1.0 / tau_flow)
        keep = 1.0 - omega - solid
        aux[4, at, :] = omega * density
        pops[0, at, :] = (keep + solid) * f[0]
        for q in range(1, 19, 2):
            pops[q, at, :] = keep * f[q] + solid * f[q + 1]
            pops[q + 1, at, :] = keep * f[q + 1] + solid * f[q]
        omega = (1.0 - solid) * (1.0 / tau_ion)
        keep = 1.0 - omega - solid
        for n, start in enumerate((19, 26)):
            g = f[start : start + 7]
            aux[5 + n, at, :] = omega * sum(g[1:], g[0])
            pops[start, at, :] = (keep + solid) * g[0]
            for q in range(1, 7, 2):
                pops[start + q, at, :] = keep * g[q] + solid * g[q + 1]
                pops[start + q + 1, at, :] = keep * g[q + 1] + solid * g[q]
        return carry

    lax.fori_loop(0, 32, block, 0)


def finish(pops, aux, field, post):
    def block(i, carry):
        at = pl.ds(pl.multiple_of(8 * i, 8), 8)
        velocity = [aux[d, at, :] for d in range(3)]
        electric = [field[d, at, :] for d in range(3)]
        push = aux[3, at, :]
        drift = [velocity[d] + push * electric[d] for d in range(3)]
        square = drift[0] * drift[0] + drift[1] * drift[1] + drift[2] * drift[2]
        mass = aux[4, at, :]
        base = 1.0 - 1.5 * square
        post[0, at, :] = pops[0, at, :] + (mass * flow_weights[0]) * base
        for q in range(1, 19, 2):
            along = None
            for d in range(3):
                if flow_dirs[q][d] and along is None:
                    along = drift[d] if flow_dirs[q][d] == 1 else -drift[d]
                elif flow_dirs[q][d]:
                    along = along + drift[d] if flow_dirs[q][d] == 1 else along - drift[d]
            scaled = mass * flow_weights[q]
            even = scaled * (base + 4.5 * along * along)
            odd = (3.0 * scaled) * along
            post[q, at, :] = pops[q, at, :] + (even + odd)
            post[q + 1, at, :] = pops[q + 1, at, :] + (even - odd)
        for start, n, sign in ((19, 5, mobility), (26, 6, -mobility)):
            mass = aux[n, at, :]
            post[start, at, :] = pops[start, at, :] + ion_weights[0] * mass
            even = ion_weights[1] * mass
            for d in range(3):
                q = start + 1 + 2 * d
                odd = (4.0 * even) * (velocity[d] + sign * electric[d])
                post[q, at, :] = pops[q, at, :] + (even + odd)
                post[q + 1, at, :] = pops[q + 1, at, :] + (even - odd)
        return carry

    lax.fori_loop(0, 32, block, 0)


def gather_corners(post, corner):
    corner[0] = post[7, 248:256, :]
    corner[1] = post[8, 0:8, :]
    corner[2] = post[9, 240:248, :]
    corner[3] = post[10, 8:16, :]


def gather_x_faces(post, xf):
    for n, q in enumerate(FACE[0, 1]):
        xf[n] = post[q, 240:256, :]
    for n, q in enumerate(FACE[0, -1]):
        xf[7 + n] = post[q, 0:16, :]


def gather_y_faces(post, yf):
    for n, q in enumerate(FACE[1, 1]):
        yf[n] = post[q, pl.ds(15, 16, stride=16), :]
    for n, q in enumerate(FACE[1, -1]):
        yf[7 + n] = post[q, pl.ds(0, 16, stride=16), :]


def gather_z_faces(post, zf):
    lane = lax.broadcasted_iota(jnp.int32, (16, 128), 1)
    packed = [jnp.zeros((16, 128), f32), jnp.zeros((16, 128), f32)]
    for n, (up, down) in enumerate(zip(FACE[2, 1], FACE[2, -1])):
        for x in range(16):
            both = jnp.where(
                lane == 127, post[up, 16 * x : 16 * x + 16, :], post[down, 16 * x : 16 * x + 16, :]
            )
            at = 16 * (x // 2) + 2 * n
            moved = pltpu.roll(both, (at + 1) % 128, 1)
            packed[x % 2] = jnp.where((lane == at) | (lane == at + 1), moved, packed[x % 2])
    zf[0:16, :] = packed[0]
    zf[16:32, :] = packed[1]


def face_messages(xf, yf, zf, corner, xr, yr, zr, zx, zy, cr):
    up, down = pl.ds(0, 7), pl.ds(7, 7)
    low, high = pl.ds(0, 16), pl.ds(16, 16)
    return [
        (xf.at[up], xr.at[up], 1, 0, 0),
        (xf.at[down], xr.at[down], -1, 0, 0),
        (yf.at[up], yr.at[up], 0, 1, 0),
        (yf.at[down], yr.at[down], 0, -1, 0),
        (zf, zr, 0, 0, 1),
        (zf.at[high], zx.at[low], 1, 0, 1),
        (zf.at[low], zx.at[high], -1, 0, 1),
        (zf, zy.at[0], 0, 1, 1),
        (zf, zy.at[1], 0, -1, 1),
        (corner.at[0], cr.at[0], 1, 1, 0),
        (corner.at[1], cr.at[1], -1, -1, 0),
        (corner.at[2], cr.at[2], 1, -1, 0),
        (corner.at[3], cr.at[3], -1, 1, 0),
    ]


def partner(step_flow, step_cy, cross):
    flow, cy, cz = place()
    return (
        lax.rem(flow + FLOW + step_flow, FLOW),
        lax.rem(cy + CY + step_cy, CY),
        1 - cz if cross else cz,
    )


def run_inside(post, moved):
    for q in range(33):
        ex, ey, ez = DIRS[q]
        for x in range(16):
            if 0 <= x - ex <= 15:
                plane = post[q, 16 * (x - ex) : 16 * (x - ex) + 16, :]
                if ey:
                    plane = pltpu.roll(plane, ey % 16, 0)
                if ez:
                    plane = pltpu.roll(plane, ez % 128, 1)
                moved[q, 16 * x : 16 * x + 16, :] = plane


def run_edges(moved, xr, yr, zr, zx, zy, cr):
    lane = lax.broadcasted_iota(jnp.int32, (16, 128), 1)
    row = lax.broadcasted_iota(jnp.int32, (16, 128), 0)
    for q in range(1, 33):
        ex, ey, ez = DIRS[q]
        edge_x = 0 if ex == 1 else 15
        first_row, last_row = (0, 15) if ey == 1 else (15, 0)
        if ex:
            plane = xr[FACE[0, ex].index(q) + (0 if ex == 1 else 7)]
            if ey:
                plane = pltpu.roll(plane, ey % 16, 0)
            if ez:
                plane = pltpu.roll(plane, ez % 128, 1)
            moved[q, 16 * edge_x : 16 * edge_x + 16, :] = plane
        if ey:
            lines = yr[FACE[1, ey].index(q) + (0 if ey == 1 else 7)]
            if ex:
                n = {7: 0, 8: 1, 9: 2, 10: 3}[q]
                tile = 7 if ey == 1 else 0
                lines = jnp.where(row == edge_x, cr[n, tile : tile + 1, :], pltpu.roll(lines, ex % 16, 0))
            if ez:
                lines = pltpu.roll(lines, ez % 128, 1)
            moved[q, pl.ds(first_row, 16, stride=16), :] = lines
        if ez:
            face = FACE[2, ez].index(q)
            goal = 0 if ez == 1 else 127
            for x in range(16):
                xs = x - ex
                if 0 <= xs <= 15:
                    edge = zr[16 * (xs % 2) : 16 * (xs % 2) + 16, :]
                    block = xs // 2
                else:
                    edge = zx[0:16, :] if ex == 1 else zx[16:32, :]
                    block = 7 if ex == 1 else 0
                if ey:
                    beyond = zy[0 if ey == 1 else 1, 16 * (xs % 2) : 16 * (xs % 2) + 16, :]
                    edge = pltpu.roll(jnp.where(row == last_row, beyond, edge), ey % 16, 0)
                shift = (goal - (16 * block + 2 * face + (0 if ez == 1 else 1))) % 128
                column = pltpu.roll(edge, shift, 1) if shift else edge
                here = slice(16 * x, 16 * x + 16)
                moved[q, here, :] = jnp.where(lane == goal, column, moved[q, here, :])


FACE_SHAPES = [(14, 16, 128), (14, 16, 128), (32, 128), (32, 128), (2, 32, 128), (4, 8, 128)]


def main_kernel(
    table_ref, pos_hbm, neg_hbm, flow_hbm, gray_hbm, hy_hbm, hz_hbm, back_hbm, gtab_hbm,
    moved, phi,
    pops, post, gray, hy_ref, hz_ref, back_ref, gtab, aux, field, charge,
    s0, r0, moments, gathered, partial, modes, beside, s1, r1, joined, halo, xh, yh,
    xf, yf, zf, corner, xr, yr, zr, zx, zy, cr,
    load_sem, send_sem, recv_sem, fsend_sem, frecv_sem,
):
    flow, cy, cz = place()
    me = cz * CY + cy
    loads = [
        pltpu.make_async_copy(source, target, load_sem.at[n])
        for n, (source, target) in enumerate(
            (
                (pos_hbm, pops.at[pl.ds(19, 7)]),
                (neg_hbm, pops.at[pl.ds(26, 7)]),
                (hz_hbm.at[cz], hz_ref),
                (flow_hbm, pops.at[pl.ds(0, 19)]),
                (gray_hbm, gray),
                (hy_hbm, hy_ref),
                (gtab_hbm.at[me], gtab),
                (back_hbm.at[cz], back_ref),
            )
        )
    ]
    for copy in loads[:3]:
        copy.start()
    barrier = pltpu.get_barrier_semaphore()

    def greet(k, carry):
        other = lax.rem(me + k, 16)
        pl.semaphore_signal(
            barrier,
            inc=1,
            device_id={"cy": lax.rem(other, CY), "cz": lax.div(other, CY)},
            device_id_type=MESH,
        )
        pl.semaphore_signal(
            barrier, inc=1, device_id={"flow": lax.rem(flow + k, 16)}, device_id_type=MESH
        )
        return carry

    lax.fori_loop(1, 16, greet, 0)
    messages = face_messages(xf, yf, zf, corner, xr, yr, zr, zx, zy, cr)
    strangers = [m[2:] for m in messages if m[2] and (m[3] or m[4])]
    for i, j, k in strangers:
        pl.semaphore_signal(barrier, inc=1, device_id=partner(i, j, k), device_id_type=MESH)
    for copy in loads[:3]:
        copy.wait()
    pos = pops[19]
    neg = pops[26]
    for q in range(1, 7):
        pos = pos + pops[19 + q]
        neg = neg + pops[26 + q]
    charge[...] = pos - neg
    for copy in loads[3:]:
        copy.start()

    spectrum = fdot(charge[...], hz_ref[...])
    for g in range(2):
        for c in range(2):
            blocks = [
                spectrum[128 * g + 16 * i : 128 * g + 16 * i + 16, 128 * c : 128 * c + 128]
                for i in range(8)
            ]
            for i, block in enumerate(swap_windows(blocks)):
                at = 16 * (8 * c + i)
                s0[at : at + 16, 128 * g : 128 * g + 128] = block
    pl.semaphore_wait(barrier, 30 + len(strangers))
    swap_across_plane(
        lambda b: rows_at(s0, 16 * b, 16),
        lambda b: rows_at(r0, 16 * b, 16),
        send_sem.at[0],
        recv_sem.at[0],
    )
    for copy in loads[3:]:
        copy.wait()
    prepare(pops, charge, gray, table_ref, aux)
    settle(r0, recv_sem.at[0])
    spectrum = fdot(hy_ref[...], r0[...])
    rho = [spectrum[:, :128], spectrum[:, 128:]]
    mask = zero_mode_mask(cy, cz)
    rest = block_moments(rho, gtab, moments, partial, mask)
    swap_along_flow(
        lambda a: moments,
        lambda a: gathered.at[pl.ds(pl.multiple_of(40 * a, 8), 40), :],
        send_sem.at[1],
        recv_sem.at[1],
    )
    rest()
    settle(gathered, recv_sem.at[1])
    gathered_potential(
        [r[0:8, :] for r in rho], gtab, gathered, partial, mask, flow, modes
    )
    spectrum = fdot(hy_ref[:, 0:128], modes[...])
    for block in range(CY):
        for g in range(2):
            at = 40 * block + 16 * g
            s1[at : at + 16, :] = spectrum[16 * block : 16 * block + 16, 128 * g : 128 * g + 128]
    beside[...] = spectrum[:, 256:384]
    send_halo(beside, s1)
    swap_across_plane(
        lambda b: s1.at[pl.ds(pl.multiple_of(40 * lax.rem(b, CY), 8), 40), :],
        lambda b: r1.at[pl.ds(pl.multiple_of(40 * b, 8), 40), :],
        send_sem.at[2],
        recv_sem.at[2],
    )
    settle(r1, recv_sem.at[2])
    for g in range(2):
        for c in range(2):
            blocks = []
            for i in range(8):
                at = 40 * (8 * c + i) + 16 * g
                blocks.append(r1[at : at + 16, :])
            for i, block in enumerate(swap_windows(blocks)):
                at = 128 * g + 16 * i
                joined[at : at + 16, 128 * c : 128 * c + 128] = block
    for c in range(2):
        blocks = []
        for i in range(8):
            at = 40 * (8 * c + i) + 32
            blocks.append(r1[at : at + 8, :])
        for i, block in enumerate(swap_windows(blocks)):
            joined[256 + 8 * i : 264 + 8 * i, 128 * c : 128 * c + 128] = block
    both = fdot(joined[0:256, :], back_ref[...])
    phi[...] = both[:, :128]
    field[2] = both[:, 128:]
    halo[...] = fdot(joined[256:320, :], back_ref[:, 0:128])
    receive_halo(halo, xh, yh)
    fill_fields(phi, xh, yh, field)
    finish(pops, aux, field, post)
    copies = []

    def send_faces(first, last):
        for n in range(first, last):
            source, target, i, j, k = messages[n]
            copies.append(
                pltpu.make_async_remote_copy(
                    src_ref=source,
                    dst_ref=target,
                    send_sem=fsend_sem.at[n],
                    recv_sem=frecv_sem.at[n],
                    device_id=partner(i, j, k),
                    device_id_type=MESH,
                )
            )
            copies[-1].start()

    gather_corners(post, corner)
    send_faces(9, 13)
    gather_x_faces(post, xf)
    send_faces(0, 2)
    gather_y_faces(post, yf)
    send_faces(2, 4)
    gather_z_faces(post, zf)
    send_faces(4, 9)
    run_inside(post, moved)
    settle(s0.at[pl.ds(0, 240), :], send_sem.at[0])
    settle(gathered.at[pl.ds(0, 600), :], send_sem.at[1])
    settle(gathered.at[pl.ds(0, 600), :], send_sem.at[2])
    for copy in copies:
        copy.wait()
    run_edges(moved, xr, yr, zr, zx, zy, cr)


def collide_all(table, flow_pops, ion_pos, ion_neg, gray):
    rows, square = (256, 128), (256, 256)
    anywhere = pl.BlockSpec(memory_space=pl.ANY)
    shapes = [(33, 256, 128), rows]
    buffers = [(128, 256), (128, 256), square, (704, 128), (7, 256, 128), (3, 256, 128), rows]
    buffers += [square, square, (40, 128), (640, 128), (2, 128, 128), (128, 384)]
    buffers += [(128, 128), (320, 128), (640, 128), (320, 256), (64, 128)]
    buffers += [(32, 128), (32, 128)]
    buffers += [(14, 16, 128), (14, 16, 128), (32, 128), (4, 8, 128)] + FACE_SHAPES
    return pl.pallas_call(
        main_kernel,
        out_shape=[pltpu.VMEM(s, f32) for s in shapes],
        in_specs=[pl.BlockSpec(memory_space=pltpu.SMEM)] + [anywhere] * 8,
        out_specs=[pl.BlockSpec(memory_space=pltpu.VMEM)] * 2,
        scratch_shapes=[pltpu.VMEM((33, 256, 128), f32)] * 2
        + [pltpu.VMEM(rows, jnp.int32)]
        + [pltpu.VMEM(s, f32) for s in buffers]
        + [pltpu.SemaphoreType.DMA((n,)) for n in (8, 3, 3, 13, 13)],
        compiler_params=pltpu.CompilerParams(
            collective_id=0, has_side_effects=True, vmem_limit_bytes=VMEM_LIMIT
        ),
        name="collision",
    )(table, ion_pos, ion_neg, flow_pops, gray, *(jnp.asarray(t) for t in tables()))


def store_kernel(moved, phi, flow_out, pos_out, neg_out, phi_out, sem):
    copies = [pltpu.make_async_copy(phi, phi_out, sem.at[33])]
    for q in range(33):
        target = flow_out.at[q] if q < 19 else pos_out.at[q - 19] if q < 26 else neg_out.at[q - 26]
        copies.append(pltpu.make_async_copy(moved.at[q], target, sem.at[q]))
    for copy in copies:
        copy.start()
    for copy in copies:
        copy.wait()


def store_all(moved, phi):
    shapes = [(19, 256, 128), (7, 256, 128), (7, 256, 128), (256, 128)]
    return pl.pallas_call(
        store_kernel,
        out_shape=[jax.ShapeDtypeStruct(s, f32) for s in shapes],
        in_specs=[pl.BlockSpec(memory_space=pltpu.VMEM)] * 2,
        out_specs=[pl.BlockSpec(memory_space=pl.ANY)] * 4,
        scratch_shapes=[pltpu.SemaphoreType.DMA((34,))],
        compiler_params=pltpu.CompilerParams(vmem_limit_bytes=2 << 20),
        name="results",
    )(moved, phi)


def shards(flow_pops, ion_pos, ion_neg, gray_class, fraction_table):
    extent = gray_class.shape
    flow_pops = flow_pops.reshape(19, 256, 128)
    ion_pos = ion_pos.reshape(7, 256, 128)
    ion_neg = ion_neg.reshape(7, 256, 128)
    gray = gray_class.reshape(256, 128)
    moved, phi = collide_all(fraction_table, flow_pops, ion_pos, ion_neg, gray)
    flow_new, pos_new, neg_new, phi = store_all(moved, phi)
    return (
        flow_new.reshape(19, *extent),
        pos_new.reshape(7, *extent),
        neg_new.reshape(7, *extent),
        phi.reshape(extent),
    )


def solution(mesh):
    in_specs = (
        P(None, "flow", "cy", "cz"),
        P(None, "flow", "cy", "cz"),
        P(None, "flow", "cy", "cz"),
        P("flow", "cy", "cz"),
        P(),
    )
    out_specs = (
        P(None, "flow", "cy", "cz"),
        P(None, "flow", "cy", "cz"),
        P(None, "flow", "cy", "cz"),
        P("flow", "cy", "cz"),
    )
    return jax.shard_map(shards, mesh=mesh, in_specs=in_specs, out_specs=out_specs, check_vma=False)
```

```python
import functools
import math

import jax
import jax.numpy as jnp
import numpy as np
from jax import lax
from jax.experimental import pallas as pl
from jax.experimental.pallas import tpu as pltpu
from jax.sharding import PartitionSpec as P

flow_dirs = (
    (0, 0, 0),
    (1, 0, 0),
    (-1, 0, 0),
    (0, 1, 0),
    (0, -1, 0),
    (0, 0, 1),
    (0, 0, -1),
    (1, 1, 0),
    (-1, -1, 0),
    (1, -1, 0),
    (-1, 1, 0),
    (1, 0, 1),
    (-1, 0, -1),
    (1, 0, -1),
    (-1, 0, 1),
    (0, 1, 1),
    (0, -1, -1),
    (0, 1, -1),
    (0, -1, 1),
)
flow_weights = (1.0 / 3.0,) + (1.0 / 18.0,) * 6 + (1.0 / 36.0,) * 12
ion_weights = (0.25,) + (0.125,) * 6
tau_flow = 0.8
tau_ion = 0.9
coupling = 2.0
mobility = 0.5
NX, NY, NZ = 256, 128, 256
FLOW, CY, CZ = 16, 8, 2
MESH = pl.DeviceIdType.MESH
f32 = jnp.float32
VMEM_LIMIT = 55 << 20

DIRS = flow_dirs + flow_dirs[:7] + flow_dirs[:7]
FACE = {
    (axis, sign): [q for q in range(33) if DIRS[q][axis] == sign]
    for axis in range(3)
    for sign in (1, -1)
}


def cas_table64(points_k, points_n, length):
    product = (points_k[:, None].astype(np.int64) * points_n[None, :]) % length
    angle = product * (2.0 * math.pi / length)
    return np.cos(angle) + np.sin(angle)


def cas_table(points_k, points_n, length):
    return cas_table64(points_k, points_n, length).astype(np.float32)


def pack_rank(table, b):
    part = table[:, 16 * b : 16 * b + 16].reshape(2, 8, 8, 16)
    return part.transpose(0, 2, 1, 3).reshape(16, 128)


def tables():
    hy = cas_table(np.arange(NY), np.arange(NY), NY)
    z = np.arange(NZ)
    hz = cas_table(z, z, NZ)
    wide = cas_table64(z, z, NZ)
    slope = -0.5 * (np.roll(wide, -1, 1) - np.roll(wide, 1, 1))
    back = [
        np.concatenate([wide[:, 128 * c : 128 * c + 128], slope[:, 128 * c : 128 * c + 128]], 1)
        for c in range(CZ)
    ]
    lam_y = 4.0 * np.sin(np.pi * np.arange(NY) / NY) ** 2
    lam_z = 4.0 * np.sin(np.pi * z / NZ) ** 2
    t = 1.0 + 0.5 * (lam_y[:, None] + lam_z[None, :])
    mu = 1.0 / (t + np.sqrt(t * t - 1.0))
    gap = 1.0 / mu - mu
    gap[0, 0] = 1.0
    scale = coupling / (NY * NZ) / gap
    mu[0, 0] = scale[0, 0] = 0.0
    window = np.arange(128) // 16
    per_rank = []
    for b in range(16):
        m = np.tile(mu[:, 16 * b : 16 * b + 16], (1, 8))
        c = np.tile(scale[:, 16 * b : 16 * b + 16], (1, 8))
        packed = pack_rank(mu, b)
        per_rank.append(
            np.concatenate(
                [m, m ** (window + 1), m ** (8 - window), m**8, c]
                + [packed**16, 1.0 / (1.0 - packed**256), packed, pack_rank(scale, b)]
            )
        )
    return (
        np.concatenate([hy, hy], 1),
        hz.reshape(CZ, 128, NZ),
        np.stack(back).astype(np.float32),
        np.stack(per_rank).astype(np.float32),
    )


def place():
    return lax.axis_index("flow"), lax.axis_index("cy"), lax.axis_index("cz")


def fdot(left, right):
    return jnp.dot(left, right, precision=lax.Precision.HIGHEST, preferred_element_type=f32)


def settle(ref, sem):
    pltpu.make_async_copy(ref, ref, sem).wait()


def column_mask(shape, index):
    return lax.broadcasted_iota(jnp.int32, shape, 1) == index


def row_mask(shape, index):
    return lax.broadcasted_iota(jnp.int32, shape, 0) == index


def swap_across_plane(source, target, send_sem, recv_sem):
    _, cy, cz = place()
    me = cz * CY + cy
    for step_cy in (4, 5, 3, 2, 6, 7, 1, 0):
        for step_cz in (1, 0):
            if step_cy or step_cz:
                to_cy, to_cz = lax.rem(cy + step_cy, CY), lax.rem(cz + step_cz, CZ)
                pltpu.make_async_remote_copy(
                    src_ref=source(to_cz * CY + to_cy),
                    dst_ref=target(me),
                    send_sem=send_sem,
                    recv_sem=recv_sem,
                    device_id={"cy": to_cy, "cz": to_cz},
                    device_id_type=MESH,
                ).start()
    pltpu.make_async_copy(source(me), target(me), recv_sem).start()


def swap_along_flow(source, target, send_sem, recv_sem):
    me, _, _ = place()

    def step(k, carry):
        other = lax.rem(me + k, 16)
        pltpu.make_async_remote_copy(
            src_ref=source(other),
            dst_ref=target(me),
            send_sem=send_sem,
            recv_sem=recv_sem,
            device_id={"flow": other},
            device_id_type=MESH,
        ).start()
        return carry

    lax.fori_loop(1, 16, step, 0)
    pltpu.make_async_copy(source(me), target(me), recv_sem).start()


def rows_at(ref, start, count):
    return ref.at[pl.ds(pl.multiple_of(start, count), count), :]


def window_of(shape):
    return lax.broadcasted_iota(jnp.int32, shape, 1) // 16


def swap_windows(blocks):
    window = window_of(blocks[0].shape)
    for s in (1, 2, 4):
        high = (window & s) != 0
        moved = list(blocks)
        for i in range(8):
            if not i & s:
                low_block, high_block = blocks[i], blocks[i + s]
                moved[i] = jnp.where(high, pltpu.roll(high_block, 16 * s, 1), low_block)
                moved[i + s] = jnp.where(high, high_block, pltpu.roll(low_block, 128 - 16 * s, 1))
        blocks = moved
    return blocks


def spread(values, j):
    values = jnp.where(window_of(values.shape) == j, values, 0.0)
    for s in (16, 32, 64):
        values = values + pltpu.roll(values, s, 1)
    return values


def pack_windows(values, j):
    window = window_of((8, 128))
    packed = []
    for half in range(2):
        both = jnp.zeros((8, 128), f32)
        for i in range(8):
            tile = values[64 * half + 8 * i : 64 * half + 8 * i + 8, :]
            shift = (16 * (i - j)) % 128
            both = jnp.where(window == i, pltpu.roll(tile, shift, 1) if shift else tile, both)
        packed.append(both)
    return jnp.concatenate(packed, axis=0)


def scan_up(values, factor):
    window = window_of(values.shape)
    for s in (1, 2, 4):
        moved = pltpu.roll(values, 16 * s, 1)
        if factor is not None:
            moved = factor * moved
            factor = factor * factor
        values = values + jnp.where(window >= s, moved, 0.0)
    return values


def scan_down(values, factor):
    window = window_of(values.shape)
    for s in (1, 2, 4):
        moved = factor * pltpu.roll(values, 128 - 16 * s, 1)
        factor = factor * factor
        values = values + jnp.where(window < 8 - s, moved, 0.0)
    return values


def total_of(values):
    return jnp.sum(jnp.sum(values, axis=0, keepdims=True), axis=1, keepdims=True)


def zero_mode_mask(cy, cz):
    row = lax.broadcasted_iota(jnp.int32, (8, 128), 0)
    lane = lax.broadcasted_iota(jnp.int32, (8, 128), 1)
    here = jnp.where(cy + cz == 0, 1.0, 0.0)
    return jnp.where((row == 0) & (lane % 16 == 0), here, 0.0)


def block_moments(rho, gtab, moments, partial, mask):
    mu, near, far, eighth = (gtab[128 * n : 128 * n + 128, :] for n in range(4))
    up = [scan_up(r, mu) for r in rho]
    down = [scan_down(r, mu) for r in rho]
    moments[0:16, :] = pack_windows(up[1] + eighth * up[0], 7)
    moments[16:32, :] = pack_windows(down[0] + eighth * down[1], 0)
    window = window_of((8, 128)).astype(f32)
    at = (window - 7.5, window + 0.5)
    zero = [rho[g][0:8, :] * mask for g in range(2)]
    row = lax.broadcasted_iota(jnp.int32, (8, 128), 0)
    tile = jnp.zeros((8, 128), f32)
    for n in range(3):
        weighted = zero[0] * at[0] ** n + zero[1] * at[1] ** n if n else zero[0] + zero[1]
        tile = jnp.where(row == n, total_of(weighted), tile)
    moments[32:40, :] = tile

    def rest():
        partial[0] = up[0] + (down[0] - rho[0]) + far * spread(down[1], 0)
        partial[1] = up[1] + (down[1] - rho[1]) + near * spread(up[0], 7)

    return rest


def gathered_potential(rho_first, gtab, gathered, partial, mask, flow, out):
    def packed(source, start):
        return gathered[pl.ds(pl.multiple_of(40 * source + start, 8), 16), :]

    ratio, image = gtab[640:656, :], gtab[656:672, :]
    left, right = packed(flow, 0), packed(flow, 16)
    for d in range(15, 0, -1):
        left = packed(lax.rem(flow + 16 - d, 16), 0) + ratio * left
        right = packed(lax.rem(flow + d, 16), 16) + ratio * right
    left, right = left * image, right * image
    one, packed_scale = gtab[672:688, :], gtab[688:704, :]
    behind = packed_scale * (left + one * (packed(flow, 16) + ratio * right))
    ahead = packed_scale * (right + one * (packed(flow, 0) + ratio * left))
    small = window_of((8, 128))
    for tile in range(16):
        rows = slice(8 * tile, 8 * tile + 8)
        half = 8 * (tile // 8)
        from_left = spread(left[half : half + 8, :], tile % 8)
        from_right = spread(right[half : half + 8, :], tile % 8)
        part, j = slice(half, half + 8), tile % 8
        at_first, at_second = (-16 * j) % 128, (16 - 16 * j) % 128
        first = pltpu.roll(behind[part, :], at_first, 1) if at_first else behind[part, :]
        second = pltpu.roll(ahead[part, :], at_second, 1) if at_second else ahead[part, :]
        out[rows, 256:384] = jnp.where(small == 0, first, jnp.where(small == 1, second, 0.0))
        near, far, eighth, scale = (
            gtab[128 * n + 8 * tile : 128 * n + 8 * tile + 8, :] for n in range(1, 5)
        )
        out[rows, 0:128] = scale * (
            partial[0, rows, :] + near * from_left + (far * eighth) * from_right
        )
        out[rows, 128:256] = scale * (
            partial[1, rows, :] + (near * eighth) * from_left + far * from_right
        )

    def moment(block, n):
        return gathered[40 * block + 32 + n : 40 * block + 33 + n, :]

    mean = sum((moment(n, 0) for n in range(1, 16)), moment(0, 0)) * (1.0 / NX)
    moment_first = second_moment = left_sum = left_first = jnp.zeros((1, 128), f32)
    for block in range(16):
        centre = 16.0 * block - 120.0
        own = moment(block, 0) - 16.0 * mean
        own_first = centre * own + moment(block, 1)
        moment_first = moment_first + own_first
        second_moment = second_moment + (centre * own_first + centre * moment(block, 1))
        second_moment = second_moment + (moment(block, 2) - 340.0 * mean)
        before = jnp.where(block < flow, 1.0, 0.0)
        left_sum = left_sum + before * own
        left_first = left_first + before * own_first
    window = window_of((8, 128)).astype(f32)
    centre = 16.0 * flow.astype(f32) - 120.0
    start_sum, start_first = left_sum, left_first
    for g in range(2):
        at = centre + (window - 7.5 + 8.0 * g)
        zero = (rho_first[g] - mean) * mask
        to_here, to_here_first = scan_up(zero, None), scan_up(zero * at, None)
        upto, upto_first = left_sum + to_here, left_first + to_here_first
        left_sum = left_sum + spread(to_here, 7)
        left_first = left_first + spread(to_here_first, 7)
        distance = 2.0 * (at * upto - upto_first) + moment_first
        value = (second_moment - 2.0 * at * moment_first) * (0.5 / NX) - 0.5 * distance
        lanes = slice(128 * g, 128 * g + 128)
        out[0:8, lanes] = out[0:8, lanes] + (coupling / (NY * NZ)) * (mask * value)
    at = centre - 8.5 + 17.0 * window
    upto = jnp.where(small == 0, start_sum, left_sum)
    upto_first = jnp.where(small == 0, start_first, left_first)
    distance = 2.0 * (at * upto - upto_first) + moment_first
    value = (second_moment - 2.0 * at * moment_first) * (0.5 / NX) - 0.5 * distance
    value = jnp.where(small < 2, mask * value, 0.0)
    out[0:8, 256:384] = out[0:8, 256:384] + (coupling / (NY * NZ)) * value


def send_halo(modes_y, s1):
    window = window_of((8, 128))
    for pair in range(4):
        tile = jnp.zeros((8, 128), f32)
        for k in range(4):
            piece = modes_y[pl.ds(32 * pair + k, 8, stride=4), :]
            piece = pltpu.roll(piece, 32 * k, 1) if k else piece
            tile = jnp.where(window // 2 == k, piece, tile)
        for n in range(2):
            at = 40 * (2 * pair + n) + 32
            s1[at : at + 4, :] = tile[4 * n : 4 * n + 4, :]
    for block in range(CY):
        for side, (other, line) in enumerate((((block - 1) % CY, 15), ((block + 1) % CY, 0))):
            for g in range(2):
                to, at = 40 * block + 36 + 2 * side + g, 40 * other + 16 * g + line
                s1[to : to + 1, :] = s1[at : at + 1, :]


def receive_halo(rows, xh, yh):
    for side in range(2):
        for r in range(4):
            at = 16 * side + 4 * r
            xh[at : at + 4, :] = rows[pl.ds(8 * side + r, 4, stride=16), :]
        for g in range(2):
            at = 16 * side + 8 * g
            yh[at : at + 8, :] = rows[pl.ds(4 + 2 * side + g, 8, stride=8), :]


def pick_solid(gray, table_ref):
    bits = [(gray & (1 << n)) != 0 for n in range(4)]
    level = [table_ref[n] for n in range(16)]
    values = [jnp.where(bits[0], level[n + 1], level[n]) for n in range(0, 16, 2)]
    for n in range(1, 4):
        values = [
            jnp.where(bits[n], values[m + 1], values[m]) for m in range(0, len(values), 2)
        ]
    return values[0]


def fill_fields(phi, xh, yh, field):
    row = lax.broadcasted_iota(jnp.int32, (16, 128), 0)
    for x in range(16):
        here = phi[16 * x : 16 * x + 16, :]
        low = xh[0:16, :] if x == 0 else phi[16 * x - 16 : 16 * x, :]
        high = xh[16:32, :] if x == 15 else phi[16 * x + 16 : 16 * x + 32, :]
        field[0, 16 * x : 16 * x + 16, :] = -0.5 * (high - low)
        low = jnp.where(row == 0, yh[x : x + 1, :], pltpu.roll(here, 1, 0))
        high = jnp.where(row == 15, yh[16 + x : 17 + x, :], pltpu.roll(here, 15, 0))
        field[1, 16 * x : 16 * x + 16, :] = -0.5 * (high - low)


def prepare(pops, charge, gray, table_ref, aux):
    def block(i, carry):
        at = pl.ds(pl.multiple_of(8 * i, 8), 8)
        f = [pops[q, at, :] for q in range(33)]
        solid = pick_solid(gray[at, :], table_ref)
        density = sum(f[1:19], f[0])
        inverse = 1.0 / density
        for axis in range(3):
            plus = [f[q] for q in range(19) if flow_dirs[q][axis] == 1]
            minus = [f[q] for q in range(19) if flow_dirs[q][axis] == -1]
            aux[axis, at, :] = (sum(plus[1:], plus[0]) - sum(minus[1:], minus[0])) * inverse
        aux[3, at, :] = (tau_flow * charge[at, :]) * inverse
        omega = (1.0 - solid) * (1.0 / tau_flow)
        keep = 1.0 - omega - solid
        aux[4, at, :] = omega * density
        pops[0, at, :] = (keep + solid) * f[0]
        for q in range(1, 19, 2):
            pops[q, at, :] = keep * f[q] + solid * f[q + 1]
            pops[q + 1, at, :] = keep * f[q + 1] + solid * f[q]
        omega = (1.0 - solid) * (1.0 / tau_ion)
        keep = 1.0 - omega - solid
        for n, start in enumerate((19, 26)):
            g = f[start : start + 7]
            aux[5 + n, at, :] = omega * sum(g[1:], g[0])
            pops[start, at, :] = (keep + solid) * g[0]
            for q in range(1, 7, 2):
                pops[start + q, at, :] = keep * g[q] + solid * g[q + 1]
                pops[start + q + 1, at, :] = keep * g[q + 1] + solid * g[q]
        return carry

    lax.fori_loop(0, 32, block, 0)


def drift_of(velocity, push, electric):
    drift = [velocity[d] + push * electric[d] for d in range(3)]
    return drift, 1.0 - 1.5 * (drift[0] * drift[0] + drift[1] * drift[1] + drift[2] * drift[2])


def along_of(direction, drift):
    along = None
    for d in range(3):
        if direction[d] and along is None:
            along = drift[d] if direction[d] == 1 else -drift[d]
        elif direction[d]:
            along = along + drift[d] if direction[d] == 1 else along - drift[d]
    return along


def fluid_terms(mass, weight, base, along):
    scaled = mass * weight
    return scaled * (base + 4.5 * along * along), (3.0 * scaled) * along


def finish_rows(at, pops, aux, field, post):
    velocity = [aux[d, at, :] for d in range(3)]
    electric = [field[d, at, :] for d in range(3)]
    drift, base = drift_of(velocity, aux[3, at, :], electric)
    mass = aux[4, at, :]
    post[0, at, :] = pops[0, at, :] + (mass * flow_weights[0]) * base
    for q in range(1, 19, 2):
        even, odd = fluid_terms(mass, flow_weights[q], base, along_of(flow_dirs[q], drift))
        post[q, at, :] = pops[q, at, :] + (even + odd)
        post[q + 1, at, :] = pops[q + 1, at, :] + (even - odd)
    for start, n, sign in ((19, 5, mobility), (26, 6, -mobility)):
        mass = aux[n, at, :]
        post[start, at, :] = pops[start, at, :] + ion_weights[0] * mass
        even = ion_weights[1] * mass
        for d in range(3):
            q = start + 1 + 2 * d
            odd = (4.0 * even) * (velocity[d] + sign * electric[d])
            post[q, at, :] = pops[q, at, :] + (even + odd)
            post[q + 1, at, :] = pops[q + 1, at, :] + (even - odd)


def pack_columns(planes):
    lane = lax.broadcasted_iota(jnp.int32, (16, 128), 1)
    packed = [jnp.zeros((16, 128), f32), jnp.zeros((16, 128), f32)]
    for x in range(16):
        up, down = planes(x, 0), planes(x, 1)
        both = up if down is up else jnp.where(lane == 127, up, down)
        moved = pltpu.roll(both, (16 * (x // 2) + 1) % 128, 1)
        packed[x % 2] = jnp.where(lane // 16 == x // 2, moved, packed[x % 2])
    return jnp.concatenate(packed, axis=0)


def plane_at(x):
    return slice(16 * x, 16 * x + 16)


def pack_prepared(pops, aux, edge):
    for n in range(7):
        cache = {}

        def planes(x, side, n=n, cache=cache):
            if x not in cache:
                cache[x] = aux[n, plane_at(x), :]
            return cache[x]

        edge[n] = pack_columns(planes)
    for n, pair in enumerate(zip(FACE[2, 1], FACE[2, -1])):
        edge[7 + n] = pack_columns(lambda x, side, pair=pair: pops[pair[side], plane_at(x), :])


def z_faces(edge, field, zf):
    lane = lax.broadcasted_iota(jnp.int32, (32, 128), 1)
    sign = jnp.where(lane % 2 == 0, 1.0, -1.0)
    electric = []
    for d in range(3):
        cache = {}

        def planes(x, side, d=d, cache=cache):
            if x not in cache:
                cache[x] = field[d, plane_at(x), :]
            return cache[x]

        electric.append(pack_columns(planes))
    velocity = [edge[d] for d in range(3)]
    drift, base = drift_of(velocity, edge[3], electric)
    out = jnp.zeros((32, 128), f32)
    for n, q in enumerate(FACE[2, 1]):
        if q < 19:
            even, odd = fluid_terms(edge[4], flow_weights[q], base, along_of(flow_dirs[q], drift))
        else:
            which = 0 if q < 26 else 1
            even = ion_weights[1] * edge[5 + which]
            odd = (4.0 * even) * (velocity[2] + (mobility, -mobility)[which] * electric[2])
        value = edge[7 + n] + (even + sign * odd)
        moved = pltpu.roll(value, 2 * n, 1) if n else value
        out = jnp.where((lane % 16) // 2 == n, moved, out)
    zf[...] = out


def gather_corners(post, corner):
    corner[0] = post[7, 248:256, :]
    corner[1] = post[8, 0:8, :]
    corner[2] = post[9, 240:248, :]
    corner[3] = post[10, 8:16, :]


def gather_x_faces(post, xf):
    for n, q in enumerate(FACE[0, 1]):
        xf[n] = post[q, 240:256, :]
    for n, q in enumerate(FACE[0, -1]):
        xf[7 + n] = post[q, 0:16, :]


def gather_y_faces(post, yf):
    for n, q in enumerate(FACE[1, 1]):
        yf[n] = post[q, pl.ds(15, 16, stride=16), :]
    for n, q in enumerate(FACE[1, -1]):
        yf[7 + n] = post[q, pl.ds(0, 16, stride=16), :]


def face_messages(xf, yf, zf, corner, xr, yr, zr, zx, zy, cr):
    up, down = pl.ds(0, 7), pl.ds(7, 7)
    low, high = pl.ds(0, 16), pl.ds(16, 16)
    return [
        (xf.at[up], xr.at[up], 1, 0, 0),
        (xf.at[down], xr.at[down], -1, 0, 0),
        (yf.at[up], yr.at[up], 0, 1, 0),
        (yf.at[down], yr.at[down], 0, -1, 0),
        (zf, zr, 0, 0, 1),
        (zf.at[high], zx.at[low], 1, 0, 1),
        (zf.at[low], zx.at[high], -1, 0, 1),
        (zf, zy.at[0], 0, 1, 1),
        (zf, zy.at[1], 0, -1, 1),
        (corner.at[0], cr.at[0], 1, 1, 0),
        (corner.at[1], cr.at[1], -1, -1, 0),
        (corner.at[2], cr.at[2], 1, -1, 0),
        (corner.at[3], cr.at[3], -1, 1, 0),
    ]


def partner(step_flow, step_cy, cross):
    flow, cy, cz = place()
    return (
        lax.rem(flow + FLOW + step_flow, FLOW),
        lax.rem(cy + CY + step_cy, CY),
        1 - cz if cross else cz,
    )


def run_inside(post, moved):
    for q in range(33):
        ex, ey, ez = DIRS[q]
        for x in range(16):
            if 0 <= x - ex <= 15:
                plane = post[q, 16 * (x - ex) : 16 * (x - ex) + 16, :]
                if ey:
                    plane = pltpu.roll(plane, ey % 16, 0)
                if ez:
                    plane = pltpu.roll(plane, ez % 128, 1)
                moved[q, 16 * x : 16 * x + 16, :] = plane


def run_edges(moved, xr, yr, zr, zx, zy, cr):
    lane = lax.broadcasted_iota(jnp.int32, (16, 128), 1)
    row = lax.broadcasted_iota(jnp.int32, (16, 128), 0)
    for q in range(1, 33):
        ex, ey, ez = DIRS[q]
        edge_x = 0 if ex == 1 else 15
        first_row, last_row = (0, 15) if ey == 1 else (15, 0)
        if ex:
            plane = xr[FACE[0, ex].index(q) + (0 if ex == 1 else 7)]
            if ey:
                plane = pltpu.roll(plane, ey % 16, 0)
            if ez:
                plane = pltpu.roll(plane, ez % 128, 1)
            moved[q, 16 * edge_x : 16 * edge_x + 16, :] = plane
        if ey:
            lines = yr[FACE[1, ey].index(q) + (0 if ey == 1 else 7)]
            if ex:
                n = {7: 0, 8: 1, 9: 2, 10: 3}[q]
                tile = 7 if ey == 1 else 0
                lines = jnp.where(row == edge_x, cr[n, tile : tile + 1, :], pltpu.roll(lines, ex % 16, 0))
            if ez:
                lines = pltpu.roll(lines, ez % 128, 1)
            moved[q, pl.ds(first_row, 16, stride=16), :] = lines
        if ez:
            face = FACE[2, ez].index(q)
            goal = 0 if ez == 1 else 127
            for x in range(16):
                xs = x - ex
                if 0 <= xs <= 15:
                    edge = zr[16 * (xs % 2) : 16 * (xs % 2) + 16, :]
                    block = xs // 2
                else:
                    edge = zx[0:16, :] if ex == 1 else zx[16:32, :]
                    block = 7 if ex == 1 else 0
                if ey:
                    beyond = zy[0 if ey == 1 else 1, 16 * (xs % 2) : 16 * (xs % 2) + 16, :]
                    edge = pltpu.roll(jnp.where(row == last_row, beyond, edge), ey % 16, 0)
                shift = (goal - (16 * block + 2 * face + (0 if ez == 1 else 1))) % 128
                column = pltpu.roll(edge, shift, 1) if shift else edge
                here = slice(16 * x, 16 * x + 16)
                moved[q, here, :] = jnp.where(lane == goal, column, moved[q, here, :])


FACE_SHAPES = [(14, 16, 128), (14, 16, 128), (32, 128), (32, 128), (2, 32, 128), (4, 8, 128)]


def main_kernel(
    table_ref, pos_hbm, neg_hbm, flow_hbm, gray_hbm, hy_hbm, hz_hbm, back_hbm, gtab_hbm,
    moved, phi,
    pops, post, gray, hy_ref, hz_ref, back_ref, gtab, aux, field, charge, edge,
    s0, r0, moments, gathered, partial, modes, beside, s1, r1, joined, halo, xh, yh,
    xf, yf, zf, corner, xr, yr, zr, zx, zy, cr,
    load_sem, send_sem, recv_sem, fsend_sem, frecv_sem,
):
    flow, cy, cz = place()
    me = cz * CY + cy
    loads = [
        pltpu.make_async_copy(source, target, load_sem.at[n])
        for n, (source, target) in enumerate(
            (
                (pos_hbm, pops.at[pl.ds(19, 7)]),
                (neg_hbm, pops.at[pl.ds(26, 7)]),
                (hz_hbm.at[cz], hz_ref),
                (flow_hbm, pops.at[pl.ds(0, 19)]),
                (gray_hbm, gray),
                (hy_hbm, hy_ref),
                (gtab_hbm.at[me], gtab),
                (back_hbm.at[cz], back_ref),
            )
        )
    ]
    for copy in loads[:3]:
        copy.start()
    barrier = pltpu.get_barrier_semaphore()

    messages = face_messages(xf, yf, zf, corner, xr, yr, zr, zx, zy, cr)
    strangers = [m[2:] for m in messages if m[2] and (m[3] or m[4])]
    friends = [(0, j, k) for j in (4, 5, 3, 2, 6, 7, 1, 0) for k in (1, 0) if j or k]
    friends += [(i, 0, 0) for i in (10, 6, 5, 11, 9, 7, 2, 14, 8, 3, 13, 12, 4, 15, 1)]
    for i, j, k in strangers + friends:
        pl.semaphore_signal(barrier, inc=1, device_id=partner(i, j, k), device_id_type=MESH)
    for copy in loads[:3]:
        copy.wait()
    pos = pops[19]
    neg = pops[26]
    for q in range(1, 7):
        pos = pos + pops[19 + q]
        neg = neg + pops[26 + q]
    charge[...] = pos - neg
    for copy in loads[3:]:
        copy.start()

    spectrum = fdot(charge[...], hz_ref[...])
    for g in range(2):
        for c in range(2):
            blocks = [
                spectrum[128 * g + 16 * i : 128 * g + 16 * i + 16, 128 * c : 128 * c + 128]
                for i in range(8)
            ]
            for i, block in enumerate(swap_windows(blocks)):
                at = 16 * (8 * c + i)
                s0[at : at + 16, 128 * g : 128 * g + 128] = block
    pl.semaphore_wait(barrier, 30 + len(strangers))
    swap_across_plane(
        lambda b: rows_at(s0, 16 * b, 16),
        lambda b: rows_at(r0, 16 * b, 16),
        send_sem.at[0],
        recv_sem.at[0],
    )
    for copy in loads[3:]:
        copy.wait()
    prepare(pops, charge, gray, table_ref, aux)
    pack_prepared(pops, aux, edge)
    settle(r0, recv_sem.at[0])
    spectrum = fdot(hy_ref[...], r0[...])
    rho = [spectrum[:, :128], spectrum[:, 128:]]
    mask = zero_mode_mask(cy, cz)
    rest = block_moments(rho, gtab, moments, partial, mask)
    swap_along_flow(
        lambda a: moments,
        lambda a: gathered.at[pl.ds(pl.multiple_of(40 * a, 8), 40), :],
        send_sem.at[1],
        recv_sem.at[1],
    )
    rest()
    settle(gathered, recv_sem.at[1])
    gathered_potential(
        [r[0:8, :] for r in rho], gtab, gathered, partial, mask, flow, modes
    )
    spectrum = fdot(hy_ref[:, 0:128], modes[...])
    for block in range(CY):
        for g in range(2):
            at = 40 * block + 16 * g
            s1[at : at + 16, :] = spectrum[16 * block : 16 * block + 16, 128 * g : 128 * g + 128]
    beside[...] = spectrum[:, 256:384]
    send_halo(beside, s1)
    swap_across_plane(
        lambda b: s1.at[pl.ds(pl.multiple_of(40 * lax.rem(b, CY), 8), 40), :],
        lambda b: r1.at[pl.ds(pl.multiple_of(40 * b, 8), 40), :],
        send_sem.at[2],
        recv_sem.at[2],
    )
    settle(r1, recv_sem.at[2])
    for g in range(2):
        for c in range(2):
            blocks = []
            for i in range(8):
                at = 40 * (8 * c + i) + 16 * g
                blocks.append(r1[at : at + 16, :])
            for i, block in enumerate(swap_windows(blocks)):
                at = 128 * g + 16 * i
                joined[at : at + 16, 128 * c : 128 * c + 128] = block
    for c in range(2):
        blocks = []
        for i in range(8):
            at = 40 * (8 * c + i) + 32
            blocks.append(r1[at : at + 8, :])
        for i, block in enumerate(swap_windows(blocks)):
            joined[256 + 8 * i : 264 + 8 * i, 128 * c : 128 * c + 128] = block
    both = fdot(joined[0:256, :], back_ref[...])
    phi[...] = both[:, :128]
    field[2] = both[:, 128:]
    halo[...] = fdot(joined[256:320, :], back_ref[:, 0:128])
    receive_halo(halo, xh, yh)
    fill_fields(phi, xh, yh, field)
    for start in (0, 8, 240, 248):
        finish_rows(pl.ds(start, 8), pops, aux, field, post)
    copies = []

    def send_faces(first, last):
        for n in range(first, last):
            source, target, i, j, k = messages[n]
            copies.append(
                pltpu.make_async_remote_copy(
                    src_ref=source,
                    dst_ref=target,
                    send_sem=fsend_sem.at[n],
                    recv_sem=frecv_sem.at[n],
                    device_id=partner(i, j, k),
                    device_id_type=MESH,
                )
            )
            copies[-1].start()

    gather_corners(post, corner)
    send_faces(9, 13)
    gather_x_faces(post, xf)
    send_faces(0, 2)
    for start in (0, 15, 128, 143):
        finish_rows(pl.ds(start, 8, stride=16), pops, aux, field, post)
    gather_y_faces(post, yf)
    send_faces(2, 4)
    z_faces(edge, field, zf)
    send_faces(4, 9)

    def finish_block(i, carry):
        finish_rows(pl.ds(pl.multiple_of(8 * i, 8), 8), pops, aux, field, post)
        return carry

    lax.fori_loop(2, 30, finish_block, 0)
    run_inside(post, moved)
    settle(s0.at[pl.ds(0, 240), :], send_sem.at[0])
    settle(gathered.at[pl.ds(0, 600), :], send_sem.at[1])
    settle(gathered.at[pl.ds(0, 600), :], send_sem.at[2])
    for copy in copies:
        copy.wait()
    run_edges(moved, xr, yr, zr, zx, zy, cr)


def collide_all(table, flow_pops, ion_pos, ion_neg, gray):
    rows, square = (256, 128), (256, 256)
    anywhere = pl.BlockSpec(memory_space=pl.ANY)
    shapes = [(33, 256, 128), rows]
    buffers = [(128, 256), (128, 256), square, (704, 128), (7, 256, 128), (3, 256, 128), rows]
    buffers += [(14, 32, 128)]
    buffers += [square, square, (40, 128), (640, 128), (2, 128, 128), (128, 384)]
    buffers += [(128, 128), (320, 128), (640, 128), (320, 256), (64, 128)]
    buffers += [(32, 128), (32, 128)]
    buffers += [(14, 16, 128), (14, 16, 128), (32, 128), (4, 8, 128)] + FACE_SHAPES
    return pl.pallas_call(
        main_kernel,
        out_shape=[pltpu.VMEM(s, f32) for s in shapes],
        in_specs=[pl.BlockSpec(memory_space=pltpu.SMEM)] + [anywhere] * 8,
        out_specs=[pl.BlockSpec(memory_space=pltpu.VMEM)] * 2,
        scratch_shapes=[pltpu.VMEM((33, 256, 128), f32)] * 2
        + [pltpu.VMEM(rows, jnp.int32)]
        + [pltpu.VMEM(s, f32) for s in buffers]
        + [pltpu.SemaphoreType.DMA((n,)) for n in (8, 3, 3, 13, 13)],
        compiler_params=pltpu.CompilerParams(
            collective_id=0, has_side_effects=True, vmem_limit_bytes=VMEM_LIMIT
        ),
        name="collision",
    )(table, ion_pos, ion_neg, flow_pops, gray, *(jnp.asarray(t) for t in tables()))


def store_kernel(moved, phi, flow_out, pos_out, neg_out, phi_out, sem):
    copies = [pltpu.make_async_copy(phi, phi_out, sem.at[33])]
    for q in range(33):
        target = flow_out.at[q] if q < 19 else pos_out.at[q - 19] if q < 26 else neg_out.at[q - 26]
        copies.append(pltpu.make_async_copy(moved.at[q], target, sem.at[q]))
    for copy in copies:
        copy.start()
    for copy in copies:
        copy.wait()


def store_all(moved, phi):
    shapes = [(19, 256, 128), (7, 256, 128), (7, 256, 128), (256, 128)]
    return pl.pallas_call(
        store_kernel,
        out_shape=[jax.ShapeDtypeStruct(s, f32) for s in shapes],
        in_specs=[pl.BlockSpec(memory_space=pltpu.VMEM)] * 2,
        out_specs=[pl.BlockSpec(memory_space=pl.ANY)] * 4,
        scratch_shapes=[pltpu.SemaphoreType.DMA((34,))],
        compiler_params=pltpu.CompilerParams(vmem_limit_bytes=2 << 20),
        name="results",
    )(moved, phi)


def shards(flow_pops, ion_pos, ion_neg, gray_class, fraction_table):
    extent = gray_class.shape
    flow_pops = flow_pops.reshape(19, 256, 128)
    ion_pos = ion_pos.reshape(7, 256, 128)
    ion_neg = ion_neg.reshape(7, 256, 128)
    gray = gray_class.reshape(256, 128)
    moved, phi = collide_all(fraction_table, flow_pops, ion_pos, ion_neg, gray)
    flow_new, pos_new, neg_new, phi = store_all(moved, phi)
    return (
        flow_new.reshape(19, *extent),
        pos_new.reshape(7, *extent),
        neg_new.reshape(7, *extent),
        phi.reshape(extent),
    )


def solution(mesh):
    in_specs = (
        P(None, "flow", "cy", "cz"),
        P(None, "flow", "cy", "cz"),
        P(None, "flow", "cy", "cz"),
        P("flow", "cy", "cz"),
        P(),
    )
    out_specs = (
        P(None, "flow", "cy", "cz"),
        P(None, "flow", "cy", "cz"),
        P(None, "flow", "cy", "cz"),
        P("flow", "cy", "cz"),
    )
    return jax.shard_map(shards, mesh=mesh, in_specs=in_specs, out_specs=out_specs, check_vma=False)
```

```python
import functools
import math

import jax
import jax.numpy as jnp
import numpy as np
from jax import lax
from jax.experimental import pallas as pl
from jax.experimental.pallas import tpu as pltpu
from jax.sharding import PartitionSpec as P

flow_dirs = (
    (0, 0, 0),
    (1, 0, 0),
    (-1, 0, 0),
    (0, 1, 0),
    (0, -1, 0),
    (0, 0, 1),
    (0, 0, -1),
    (1, 1, 0),
    (-1, -1, 0),
    (1, -1, 0),
    (-1, 1, 0),
    (1, 0, 1),
    (-1, 0, -1),
    (1, 0, -1),
    (-1, 0, 1),
    (0, 1, 1),
    (0, -1, -1),
    (0, 1, -1),
    (0, -1, 1),
)
flow_weights = (1.0 / 3.0,) + (1.0 / 18.0,) * 6 + (1.0 / 36.0,) * 12
ion_weights = (0.25,) + (0.125,) * 6
tau_flow = 0.8
tau_ion = 0.9
coupling = 2.0
mobility = 0.5
NX, NY, NZ = 256, 128, 256
FLOW, CY, CZ = 16, 8, 2
MESH = pl.DeviceIdType.MESH
f32 = jnp.float32
VMEM_LIMIT = 55 << 20

DIRS = flow_dirs + flow_dirs[:7] + flow_dirs[:7]
FACE = {
    (axis, sign): [q for q in range(33) if DIRS[q][axis] == sign]
    for axis in range(3)
    for sign in (1, -1)
}


def cas_table64(points_k, points_n, length):
    product = (points_k[:, None].astype(np.int64) * points_n[None, :]) % length
    angle = product * (2.0 * math.pi / length)
    return np.cos(angle) + np.sin(angle)


def cas_table(points_k, points_n, length):
    return cas_table64(points_k, points_n, length).astype(np.float32)


def pack_rank(table, b):
    part = table[:, 16 * b : 16 * b + 16].reshape(2, 8, 8, 16)
    return part.transpose(0, 2, 1, 3).reshape(16, 128)


def tables():
    hy = cas_table(np.arange(NY), np.arange(NY), NY)
    z = np.arange(NZ)
    hz = cas_table(z, z, NZ)
    wide = cas_table64(z, z, NZ)
    slope = -0.5 * (np.roll(wide, -1, 1) - np.roll(wide, 1, 1))
    back = [
        np.concatenate([wide[:, 128 * c : 128 * c + 128], slope[:, 128 * c : 128 * c + 128]], 1)
        for c in range(CZ)
    ]
    lam_y = 4.0 * np.sin(np.pi * np.arange(NY) / NY) ** 2
    lam_z = 4.0 * np.sin(np.pi * z / NZ) ** 2
    t = 1.0 + 0.5 * (lam_y[:, None] + lam_z[None, :])
    mu = 1.0 / (t + np.sqrt(t * t - 1.0))
    gap = 1.0 / mu - mu
    gap[0, 0] = 1.0
    scale = coupling / (NY * NZ) / gap
    mu[0, 0] = scale[0, 0] = 0.0
    window = np.arange(128) // 16
    per_rank = []
    for b in range(16):
        m = np.tile(mu[:, 16 * b : 16 * b + 16], (1, 8))
        c = np.tile(scale[:, 16 * b : 16 * b + 16], (1, 8))
        packed = pack_rank(mu, b)
        per_rank.append(
            np.concatenate(
                [m, m ** (window + 1), m ** (8 - window), m**8, c]
                + [packed**16, 1.0 / (1.0 - packed**256), packed, pack_rank(scale, b)]
            )
        )
    return (
        np.concatenate([hy, hy], 1),
        hz.reshape(CZ, 128, NZ),
        np.stack(back).astype(np.float32),
        np.stack(per_rank).astype(np.float32),
    )


def place():
    return lax.axis_index("flow"), lax.axis_index("cy"), lax.axis_index("cz")


def fdot(left, right):
    return jnp.dot(left, right, precision=lax.Precision.HIGHEST, preferred_element_type=f32)


def settle(ref, sem):
    pltpu.make_async_copy(ref, ref, sem).wait()


def column_mask(shape, index):
    return lax.broadcasted_iota(jnp.int32, shape, 1) == index


def row_mask(shape, index):
    return lax.broadcasted_iota(jnp.int32, shape, 0) == index


def swap_across_plane(source, target, send_sem, recv_sem):
    _, cy, cz = place()
    me = cz * CY + cy
    for step_cy in (4, 5, 3, 2, 6, 7, 1, 0):
        for step_cz in (1, 0):
            if step_cy or step_cz:
                to_cy, to_cz = lax.rem(cy + step_cy, CY), lax.rem(cz + step_cz, CZ)
                pltpu.make_async_remote_copy(
                    src_ref=source(to_cz * CY + to_cy),
                    dst_ref=target(me),
                    send_sem=send_sem,
                    recv_sem=recv_sem,
                    device_id={"cy": to_cy, "cz": to_cz},
                    device_id_type=MESH,
                ).start()
    pltpu.make_async_copy(source(me), target(me), recv_sem).start()


def swap_along_flow(source, target, send_sem, recv_sem):
    me, _, _ = place()

    def step(k, carry):
        other = lax.rem(me + k, 16)
        pltpu.make_async_remote_copy(
            src_ref=source(other),
            dst_ref=target(me),
            send_sem=send_sem,
            recv_sem=recv_sem,
            device_id={"flow": other},
            device_id_type=MESH,
        ).start()
        return carry

    lax.fori_loop(1, 16, step, 0)
    pltpu.make_async_copy(source(me), target(me), recv_sem).start()


def rows_at(ref, start, count):
    return ref.at[pl.ds(pl.multiple_of(start, count), count), :]


def window_of(shape):
    return lax.broadcasted_iota(jnp.int32, shape, 1) // 16


def swap_windows(blocks):
    window = window_of(blocks[0].shape)
    for s in (1, 2, 4):
        high = (window & s) != 0
        moved = list(blocks)
        for i in range(8):
            if not i & s:
                low_block, high_block = blocks[i], blocks[i + s]
                moved[i] = jnp.where(high, pltpu.roll(high_block, 16 * s, 1), low_block)
                moved[i + s] = jnp.where(high, high_block, pltpu.roll(low_block, 128 - 16 * s, 1))
        blocks = moved
    return blocks


def spread(values, j):
    values = jnp.where(window_of(values.shape) == j, values, 0.0)
    for s in (16, 32, 64):
        values = values + pltpu.roll(values, s, 1)
    return values


def pack_windows(values, j):
    window = window_of((8, 128))
    packed = []
    for half in range(2):
        both = jnp.zeros((8, 128), f32)
        for i in range(8):
            tile = values[64 * half + 8 * i : 64 * half + 8 * i + 8, :]
            shift = (16 * (i - j)) % 128
            both = jnp.where(window == i, pltpu.roll(tile, shift, 1) if shift else tile, both)
        packed.append(both)
    return jnp.concatenate(packed, axis=0)


def scan_up(values, factor):
    window = window_of(values.shape)
    for s in (1, 2, 4):
        moved = pltpu.roll(values, 16 * s, 1)
        if factor is not None:
            moved = factor * moved
            factor = factor * factor
        values = values + jnp.where(window >= s, moved, 0.0)
    return values


def scan_down(values, factor):
    window = window_of(values.shape)
    for s in (1, 2, 4):
        moved = factor * pltpu.roll(values, 128 - 16 * s, 1)
        factor = factor * factor
        values = values + jnp.where(window < 8 - s, moved, 0.0)
    return values


def total_of(values):
    return jnp.sum(jnp.sum(values, axis=0, keepdims=True), axis=1, keepdims=True)


def zero_mode_mask(cy, cz):
    row = lax.broadcasted_iota(jnp.int32, (8, 128), 0)
    lane = lax.broadcasted_iota(jnp.int32, (8, 128), 1)
    here = jnp.where(cy + cz == 0, 1.0, 0.0)
    return jnp.where((row == 0) & (lane % 16 == 0), here, 0.0)


def block_moments(rho, up, down, gtab, moments, partial, mask):
    near, far, eighth = (gtab[128 * n : 128 * n + 128, :] for n in range(1, 4))
    moments[0:16, :] = pack_windows(up[1] + eighth * up[0], 7)
    moments[16:32, :] = pack_windows(down[0] + eighth * down[1], 0)
    window = window_of((8, 128)).astype(f32)
    at = (window - 7.5, window + 0.5)
    zero = [rho[g][0:8, :] * mask for g in range(2)]
    row = lax.broadcasted_iota(jnp.int32, (8, 128), 0)
    tile = jnp.zeros((8, 128), f32)
    for n in range(3):
        weighted = zero[0] * at[0] ** n + zero[1] * at[1] ** n if n else zero[0] + zero[1]
        tile = jnp.where(row == n, total_of(weighted), tile)
    moments[32:40, :] = tile

    def rest():
        partial[0] = up[0] + (down[0] - rho[0]) + far * spread(down[1], 0)
        partial[1] = up[1] + (down[1] - rho[1]) + near * spread(up[0], 7)

    return rest


def gathered_potential(rho_first, gtab, gathered, partial, mask, flow, out):
    def packed(source, start):
        return gathered[pl.ds(pl.multiple_of(40 * source + start, 8), 16), :]

    ratio, image = gtab[640:656, :], gtab[656:672, :]
    left, right = packed(flow, 0), packed(flow, 16)
    for d in range(15, 0, -1):
        left = packed(lax.rem(flow + 16 - d, 16), 0) + ratio * left
        right = packed(lax.rem(flow + d, 16), 16) + ratio * right
    left, right = left * image, right * image
    one, packed_scale = gtab[672:688, :], gtab[688:704, :]
    behind = packed_scale * (left + one * (packed(flow, 16) + ratio * right))
    ahead = packed_scale * (right + one * (packed(flow, 0) + ratio * left))
    small = window_of((8, 128))
    for tile in range(16):
        rows = slice(8 * tile, 8 * tile + 8)
        half = 8 * (tile // 8)
        from_left = spread(left[half : half + 8, :], tile % 8)
        from_right = spread(right[half : half + 8, :], tile % 8)
        part, j = slice(half, half + 8), tile % 8
        at_first, at_second = (-16 * j) % 128, (16 - 16 * j) % 128
        first = pltpu.roll(behind[part, :], at_first, 1) if at_first else behind[part, :]
        second = pltpu.roll(ahead[part, :], at_second, 1) if at_second else ahead[part, :]
        out[rows, 256:384] = jnp.where(small == 0, first, jnp.where(small == 1, second, 0.0))
        near, far, eighth, scale = (
            gtab[128 * n + 8 * tile : 128 * n + 8 * tile + 8, :] for n in range(1, 5)
        )
        out[rows, 0:128] = scale * (
            partial[0, rows, :] + near * from_left + (far * eighth) * from_right
        )
        out[rows, 128:256] = scale * (
            partial[1, rows, :] + (near * eighth) * from_left + far * from_right
        )

    def moment(block, n):
        return gathered[40 * block + 32 + n : 40 * block + 33 + n, :]

    mean = sum((moment(n, 0) for n in range(1, 16)), moment(0, 0)) * (1.0 / NX)
    moment_first = second_moment = left_sum = left_first = jnp.zeros((1, 128), f32)
    for block in range(16):
        centre = 16.0 * block - 120.0
        own = moment(block, 0) - 16.0 * mean
        own_first = centre * own + moment(block, 1)
        moment_first = moment_first + own_first
        second_moment = second_moment + (centre * own_first + centre * moment(block, 1))
        second_moment = second_moment + (moment(block, 2) - 340.0 * mean)
        before = jnp.where(block < flow, 1.0, 0.0)
        left_sum = left_sum + before * own
        left_first = left_first + before * own_first
    window = window_of((8, 128)).astype(f32)
    centre = 16.0 * flow.astype(f32) - 120.0
    start_sum, start_first = left_sum, left_first
    for g in range(2):
        at = centre + (window - 7.5 + 8.0 * g)
        zero = (rho_first[g] - mean) * mask
        to_here, to_here_first = scan_up(zero, None), scan_up(zero * at, None)
        upto, upto_first = left_sum + to_here, left_first + to_here_first
        left_sum = left_sum + spread(to_here, 7)
        left_first = left_first + spread(to_here_first, 7)
        distance = 2.0 * (at * upto - upto_first) + moment_first
        value = (second_moment - 2.0 * at * moment_first) * (0.5 / NX) - 0.5 * distance
        lanes = slice(128 * g, 128 * g + 128)
        out[0:8, lanes] = out[0:8, lanes] + (coupling / (NY * NZ)) * (mask * value)
    at = centre - 8.5 + 17.0 * window
    upto = jnp.where(small == 0, start_sum, left_sum)
    upto_first = jnp.where(small == 0, start_first, left_first)
    distance = 2.0 * (at * upto - upto_first) + moment_first
    value = (second_moment - 2.0 * at * moment_first) * (0.5 / NX) - 0.5 * distance
    value = jnp.where(small < 2, mask * value, 0.0)
    out[0:8, 256:384] = out[0:8, 256:384] + (coupling / (NY * NZ)) * value


def send_halo(modes_y, s1, s2):
    window = window_of((8, 128))
    for pair in range(4):
        tile = jnp.zeros((8, 128), f32)
        for k in range(4):
            piece = modes_y[pl.ds(32 * pair + k, 8, stride=4), :]
            piece = pltpu.roll(piece, 32 * k, 1) if k else piece
            tile = jnp.where(window // 2 == k, piece, tile)
        for n in range(2):
            at = 24 * (2 * pair + n) + 16
            s2[at : at + 4, :] = tile[4 * n : 4 * n + 4, :]
    for block in range(CY):
        for side, (other, line) in enumerate((((block - 1) % CY, 15), ((block + 1) % CY, 0))):
            for g in range(2):
                source, at = (s1, 16 * other + line) if g == 0 else (s2, 24 * other + line)
                to = 24 * block + 20 + 2 * side + g
                s2[to : to + 1, :] = source[at : at + 1, :]


def receive_halo(rows, xh, yh):
    for side in range(2):
        for r in range(4):
            at = 16 * side + 4 * r
            xh[at : at + 4, :] = rows[pl.ds(8 * side + r, 4, stride=16), :]
        for g in range(2):
            at = 16 * side + 8 * g
            yh[at : at + 8, :] = rows[pl.ds(4 + 2 * side + g, 8, stride=8), :]


def pick_solid(gray, table_ref):
    bits = [(gray & (1 << n)) != 0 for n in range(4)]
    level = [table_ref[n] for n in range(16)]
    values = [jnp.where(bits[0], level[n + 1], level[n]) for n in range(0, 16, 2)]
    for n in range(1, 4):
        values = [
            jnp.where(bits[n], values[m + 1], values[m]) for m in range(0, len(values), 2)
        ]
    return values[0]


def fill_fields(phi, xh, yh, field):
    row = lax.broadcasted_iota(jnp.int32, (16, 128), 0)
    for x in range(16):
        here = phi[16 * x : 16 * x + 16, :]
        low = xh[0:16, :] if x == 0 else phi[16 * x - 16 : 16 * x, :]
        high = xh[16:32, :] if x == 15 else phi[16 * x + 16 : 16 * x + 32, :]
        field[0, 16 * x : 16 * x + 16, :] = -0.5 * (high - low)
        low = jnp.where(row == 0, yh[x : x + 1, :], pltpu.roll(here, 1, 0))
        high = jnp.where(row == 15, yh[16 + x : 17 + x, :], pltpu.roll(here, 15, 0))
        field[1, 16 * x : 16 * x + 16, :] = -0.5 * (high - low)


def prepare(pops, charge, gray, table_ref, aux):
    def block(i, carry):
        at = pl.ds(pl.multiple_of(8 * i, 8), 8)
        f = [pops[q, at, :] for q in range(33)]
        solid = pick_solid(gray[at, :], table_ref)
        density = sum(f[1:19], f[0])
        inverse = 1.0 / density
        for axis in range(3):
            plus = [f[q] for q in range(19) if flow_dirs[q][axis] == 1]
            minus = [f[q] for q in range(19) if flow_dirs[q][axis] == -1]
            aux[axis, at, :] = (sum(plus[1:], plus[0]) - sum(minus[1:], minus[0])) * inverse
        aux[3, at, :] = (tau_flow * charge[at, :]) * inverse
        omega = (1.0 - solid) * (1.0 / tau_flow)
        keep = 1.0 - omega - solid
        aux[4, at, :] = omega * density
        pops[0, at, :] = (keep + solid) * f[0]
        for q in range(1, 19, 2):
            pops[q, at, :] = keep * f[q] + solid * f[q + 1]
            pops[q + 1, at, :] = keep * f[q + 1] + solid * f[q]
        omega = (1.0 - solid) * (1.0 / tau_ion)
        keep = 1.0 - omega - solid
        for n, start in enumerate((19, 26)):
            g = f[start : start + 7]
            aux[5 + n, at, :] = omega * sum(g[1:], g[0])
            pops[start, at, :] = (keep + solid) * g[0]
            for q in range(1, 7, 2):
                pops[start + q, at, :] = keep * g[q] + solid * g[q + 1]
                pops[start + q + 1, at, :] = keep * g[q + 1] + solid * g[q]
        return carry

    lax.fori_loop(0, 32, block, 0)


def drift_of(velocity, push, electric):
    drift = [velocity[d] + push * electric[d] for d in range(3)]
    return drift, 1.0 - 1.5 * (drift[0] * drift[0] + drift[1] * drift[1] + drift[2] * drift[2])


def along_of(direction, drift):
    along = None
    for d in range(3):
        if direction[d] and along is None:
            along = drift[d] if direction[d] == 1 else -drift[d]
        elif direction[d]:
            along = along + drift[d] if direction[d] == 1 else along - drift[d]
    return along


def fluid_terms(mass, weight, base, along):
    scaled = mass * weight
    return scaled * (base + 4.5 * along * along), (3.0 * scaled) * along


def finish_rows(at, pops, aux, field, post):
    velocity = [aux[d, at, :] for d in range(3)]
    electric = [field[d, at, :] for d in range(3)]
    drift, base = drift_of(velocity, aux[3, at, :], electric)
    mass = aux[4, at, :]
    post[0, at, :] = pops[0, at, :] + (mass * flow_weights[0]) * base
    for q in range(1, 19, 2):
        even, odd = fluid_terms(mass, flow_weights[q], base, along_of(flow_dirs[q], drift))
        post[q, at, :] = pops[q, at, :] + (even + odd)
        post[q + 1, at, :] = pops[q + 1, at, :] + (even - odd)
    for start, n, sign in ((19, 5, mobility), (26, 6, -mobility)):
        mass = aux[n, at, :]
        post[start, at, :] = pops[start, at, :] + ion_weights[0] * mass
        even = ion_weights[1] * mass
        for d in range(3):
            q = start + 1 + 2 * d
            odd = (4.0 * even) * (velocity[d] + sign * electric[d])
            post[q, at, :] = pops[q, at, :] + (even + odd)
            post[q + 1, at, :] = pops[q + 1, at, :] + (even - odd)


def pack_columns(planes):
    lane = lax.broadcasted_iota(jnp.int32, (16, 128), 1)
    packed = [jnp.zeros((16, 128), f32), jnp.zeros((16, 128), f32)]
    for x in range(16):
        up, down = planes(x, 0), planes(x, 1)
        both = up if down is up else jnp.where(lane == 127, up, down)
        moved = pltpu.roll(both, (16 * (x // 2) + 1) % 128, 1)
        packed[x % 2] = jnp.where(lane // 16 == x // 2, moved, packed[x % 2])
    return jnp.concatenate(packed, axis=0)


def plane_at(x):
    return slice(16 * x, 16 * x + 16)


def pack_prepared(pops, aux, edge):
    for n in range(7):
        cache = {}

        def planes(x, side, n=n, cache=cache):
            if x not in cache:
                cache[x] = aux[n, plane_at(x), :]
            return cache[x]

        edge[n] = pack_columns(planes)
    for n, pair in enumerate(zip(FACE[2, 1], FACE[2, -1])):
        edge[7 + n] = pack_columns(lambda x, side, pair=pair: pops[pair[side], plane_at(x), :])


def z_faces(edge, field, zf):
    lane = lax.broadcasted_iota(jnp.int32, (32, 128), 1)
    sign = jnp.where(lane % 2 == 0, 1.0, -1.0)
    electric = []
    for d in range(3):
        cache = {}

        def planes(x, side, d=d, cache=cache):
            if x not in cache:
                cache[x] = field[d, plane_at(x), :]
            return cache[x]

        electric.append(pack_columns(planes))
    velocity = [edge[d] for d in range(3)]
    drift, base = drift_of(velocity, edge[3], electric)
    out = jnp.zeros((32, 128), f32)
    for n, q in enumerate(FACE[2, 1]):
        if q < 19:
            even, odd = fluid_terms(edge[4], flow_weights[q], base, along_of(flow_dirs[q], drift))
        else:
            which = 0 if q < 26 else 1
            even = ion_weights[1] * edge[5 + which]
            odd = (4.0 * even) * (velocity[2] + (mobility, -mobility)[which] * electric[2])
        value = edge[7 + n] + (even + sign * odd)
        moved = pltpu.roll(value, 2 * n, 1) if n else value
        out = jnp.where((lane % 16) // 2 == n, moved, out)
    zf[...] = out


def gather_corners(post, corner):
    corner[0] = post[7, 248:256, :]
    corner[1] = post[8, 0:8, :]
    corner[2] = post[9, 240:248, :]
    corner[3] = post[10, 8:16, :]


def gather_x_faces(post, xf):
    for n, q in enumerate(FACE[0, 1]):
        xf[n] = post[q, 240:256, :]
    for n, q in enumerate(FACE[0, -1]):
        xf[7 + n] = post[q, 0:16, :]


def gather_y_faces(post, yf):
    for n, q in enumerate(FACE[1, 1]):
        yf[n] = post[q, pl.ds(15, 16, stride=16), :]
    for n, q in enumerate(FACE[1, -1]):
        yf[7 + n] = post[q, pl.ds(0, 16, stride=16), :]


def face_messages(xf, yf, zf, corner, xr, yr, zr, zx, zy, cr):
    up, down = pl.ds(0, 7), pl.ds(7, 7)
    low, high = pl.ds(0, 16), pl.ds(16, 16)
    return [
        (xf.at[up], xr.at[up], 1, 0, 0),
        (xf.at[down], xr.at[down], -1, 0, 0),
        (yf.at[up], yr.at[up], 0, 1, 0),
        (yf.at[down], yr.at[down], 0, -1, 0),
        (zf, zr, 0, 0, 1),
        (zf.at[high], zx.at[low], 1, 0, 1),
        (zf.at[low], zx.at[high], -1, 0, 1),
        (zf, zy.at[0], 0, 1, 1),
        (zf, zy.at[1], 0, -1, 1),
        (corner.at[0], cr.at[0], 1, 1, 0),
        (corner.at[1], cr.at[1], -1, -1, 0),
        (corner.at[2], cr.at[2], 1, -1, 0),
        (corner.at[3], cr.at[3], -1, 1, 0),
    ]


def partner(step_flow, step_cy, cross):
    flow, cy, cz = place()
    return (
        lax.rem(flow + FLOW + step_flow, FLOW),
        lax.rem(cy + CY + step_cy, CY),
        1 - cz if cross else cz,
    )


def run_inside(post, moved):
    for q in range(33):
        ex, ey, ez = DIRS[q]
        for x in range(16):
            if 0 <= x - ex <= 15:
                plane = post[q, 16 * (x - ex) : 16 * (x - ex) + 16, :]
                if ey:
                    plane = pltpu.roll(plane, ey % 16, 0)
                if ez:
                    plane = pltpu.roll(plane, ez % 128, 1)
                moved[q, 16 * x : 16 * x + 16, :] = plane


def run_x_edges(moved, xr):
    for ex in (1, -1):
        edge_x = 0 if ex == 1 else 15
        for n, q in enumerate(FACE[0, ex]):
            _, ey, ez = DIRS[q]
            plane = xr[n + (0 if ex == 1 else 7)]
            if ey:
                plane = pltpu.roll(plane, ey % 16, 0)
            if ez:
                plane = pltpu.roll(plane, ez % 128, 1)
            moved[q, 16 * edge_x : 16 * edge_x + 16, :] = plane


def run_y_edges(moved, yr, cr):
    row = lax.broadcasted_iota(jnp.int32, (16, 128), 0)
    for ey in (1, -1):
        for n, q in enumerate(FACE[1, ey]):
            ex, _, ez = DIRS[q]
            lines = yr[n + (0 if ey == 1 else 7)]
            if ex:
                tile = 7 if ey == 1 else 0
                line = cr[q - 7, tile : tile + 1, :]
                lines = jnp.where(row == (0 if ex == 1 else 15), line, pltpu.roll(lines, ex % 16, 0))
            if ez:
                lines = pltpu.roll(lines, ez % 128, 1)
            moved[q, pl.ds(0 if ey == 1 else 15, 16, stride=16), :] = lines


def run_z_edges(moved, zr, zx, zy):
    lane = lax.broadcasted_iota(jnp.int32, (16, 128), 1)
    row = lax.broadcasted_iota(jnp.int32, (16, 128), 0)
    for ez in (1, -1):
        goal = 0 if ez == 1 else 127
        for face, q in enumerate(FACE[2, ez]):
            ex, ey, _ = DIRS[q]
            for x in range(16):
                xs = x - ex
                if 0 <= xs <= 15:
                    edge = zr[16 * (xs % 2) : 16 * (xs % 2) + 16, :]
                    block = xs // 2
                else:
                    edge = zx[0:16, :] if ex == 1 else zx[16:32, :]
                    block = 7 if ex == 1 else 0
                if ey:
                    beyond = zy[0 if ey == 1 else 1, 16 * (xs % 2) : 16 * (xs % 2) + 16, :]
                    last_row = 15 if ey == 1 else 0
                    edge = pltpu.roll(jnp.where(row == last_row, beyond, edge), ey % 16, 0)
                shift = (goal - (16 * block + 2 * face + (0 if ez == 1 else 1))) % 128
                column = pltpu.roll(edge, shift, 1) if shift else edge
                here = slice(16 * x, 16 * x + 16)
                moved[q, here, :] = jnp.where(lane == goal, column, moved[q, here, :])


FACE_SHAPES = [(14, 16, 128), (14, 16, 128), (32, 128), (32, 128), (2, 32, 128), (4, 8, 128)]


def main_kernel(
    table_ref, pos_hbm, neg_hbm, flow_hbm, gray_hbm, hy_hbm, hz_hbm, back_hbm, gtab_hbm,
    moved, phi,
    pops, post, gray, hy_ref, hz_ref, back_ref, gtab, aux, field, charge, edge,
    s0, r0, moments, gathered, partial, modes, beside, s1, r1, s2, r2, joined, halo, xh, yh,
    xf, yf, zf, corner, xr, yr, zr, zx, zy, cr,
    load_sem, send_sem, recv_sem, fsend_sem, frecv_sem,
):
    flow, cy, cz = place()
    me = cz * CY + cy
    loads = [
        pltpu.make_async_copy(source, target, load_sem.at[n])
        for n, (source, target) in enumerate(
            (
                (pos_hbm, pops.at[pl.ds(19, 7)]),
                (neg_hbm, pops.at[pl.ds(26, 7)]),
                (hz_hbm.at[cz], hz_ref),
                (flow_hbm, pops.at[pl.ds(0, 19)]),
                (gray_hbm, gray),
                (hy_hbm, hy_ref),
                (gtab_hbm.at[me], gtab),
                (back_hbm.at[cz], back_ref),
            )
        )
    ]
    for copy in loads[:3]:
        copy.start()
    barrier = pltpu.get_barrier_semaphore()

    messages = face_messages(xf, yf, zf, corner, xr, yr, zr, zx, zy, cr)
    strangers = [m[2:] for m in messages if m[2] and (m[3] or m[4])]
    friends = [(0, j, k) for j in (4, 5, 3, 2, 6, 7, 1, 0) for k in (1, 0) if j or k]
    friends += [(i, 0, 0) for i in (10, 6, 5, 11, 9, 7, 2, 14, 8, 3, 13, 12, 4, 15, 1)]
    for i, j, k in strangers + friends:
        pl.semaphore_signal(barrier, inc=1, device_id=partner(i, j, k), device_id_type=MESH)
    for copy in loads[:3]:
        copy.wait()
    pos = pops[19]
    neg = pops[26]
    for q in range(1, 7):
        pos = pos + pops[19 + q]
        neg = neg + pops[26 + q]
    charge[...] = pos - neg
    for copy in loads[3:]:
        copy.start()

    spectrum = fdot(charge[...], hz_ref[...])
    for g in range(2):
        for c in range(2):
            blocks = [
                spectrum[128 * g + 16 * i : 128 * g + 16 * i + 16, 128 * c : 128 * c + 128]
                for i in range(8)
            ]
            for i, block in enumerate(swap_windows(blocks)):
                at = 16 * (8 * c + i)
                s0[g, at : at + 16, :] = block
    pl.semaphore_wait(barrier, 30 + len(strangers))
    for g in range(2):
        swap_across_plane(
            lambda b, g=g: rows_at(s0.at[g], 16 * b, 16),
            lambda b, g=g: rows_at(r0.at[g], 16 * b, 16),
            send_sem.at[g],
            recv_sem.at[g],
        )
    for copy in loads[3:]:
        copy.wait()
    prepare(pops, charge, gray, table_ref, aux)
    pack_prepared(pops, aux, edge)
    rho, up, down = [], [], []
    for g in range(2):
        settle(r0.at[g], recv_sem.at[g])
        rho.append(fdot(hy_ref[...], r0[g]))
        up.append(scan_up(rho[g], gtab[0:128, :]))
        down.append(scan_down(rho[g], gtab[0:128, :]))
    mask = zero_mode_mask(cy, cz)
    rest = block_moments(rho, up, down, gtab, moments, partial, mask)
    swap_along_flow(
        lambda a: moments,
        lambda a: gathered.at[pl.ds(pl.multiple_of(40 * a, 8), 40), :],
        send_sem.at[2],
        recv_sem.at[2],
    )
    rest()
    settle(gathered, recv_sem.at[2])
    gathered_potential(
        [r[0:8, :] for r in rho], gtab, gathered, partial, mask, flow, modes
    )
    s1[...] = fdot(hy_ref[:, 0:128], modes[:, 0:128])
    swap_across_plane(
        lambda b: rows_at(s1, 16 * lax.rem(b, CY), 16),
        lambda b: rows_at(r1, 16 * b, 16),
        send_sem.at[3],
        recv_sem.at[3],
    )
    spectrum = fdot(hy_ref[:, 0:128], modes[:, 128:384])
    for block in range(CY):
        s2[24 * block : 24 * block + 16, :] = spectrum[16 * block : 16 * block + 16, 0:128]
    beside[...] = spectrum[:, 128:256]
    send_halo(beside, s1, s2)
    swap_across_plane(
        lambda b: s2.at[pl.ds(pl.multiple_of(24 * lax.rem(b, CY), 8), 24), :],
        lambda b: r2.at[pl.ds(pl.multiple_of(24 * b, 8), 24), :],
        send_sem.at[4],
        recv_sem.at[4],
    )
    for g, (ref, step) in enumerate(((r1, 16), (r2, 24))):
        settle(ref, recv_sem.at[3 + g])
        for c in range(2):
            blocks = []
            for i in range(8):
                at = step * (8 * c + i)
                blocks.append(ref[at : at + 16, :])
            for i, block in enumerate(swap_windows(blocks)):
                at = 128 * g + 16 * i
                joined[at : at + 16, 128 * c : 128 * c + 128] = block
        both = fdot(joined[128 * g : 128 * g + 128, :], back_ref[...])
        phi[128 * g : 128 * g + 128, :] = both[:, :128]
        field[2, 128 * g : 128 * g + 128, :] = both[:, 128:]
    for c in range(2):
        blocks = []
        for i in range(8):
            at = 24 * (8 * c + i) + 16
            blocks.append(r2[at : at + 8, :])
        for i, block in enumerate(swap_windows(blocks)):
            joined[256 + 8 * i : 264 + 8 * i, 128 * c : 128 * c + 128] = block
    halo[...] = fdot(joined[256:320, :], back_ref[:, 0:128])
    receive_halo(halo, xh, yh)
    fill_fields(phi, xh, yh, field)
    for start in (0, 8, 240, 248):
        finish_rows(pl.ds(start, 8), pops, aux, field, post)
    copies = {}

    def send_faces(first, last):
        for n in range(first, last):
            source, target, i, j, k = messages[n]
            copies[n] = pltpu.make_async_remote_copy(
                src_ref=source,
                dst_ref=target,
                send_sem=fsend_sem.at[n],
                recv_sem=frecv_sem.at[n],
                device_id=partner(i, j, k),
                device_id_type=MESH,
            )
            copies[n].start()

    gather_corners(post, corner)
    send_faces(9, 13)
    gather_x_faces(post, xf)
    send_faces(0, 2)
    for start in (0, 15, 128, 143):
        finish_rows(pl.ds(start, 8, stride=16), pops, aux, field, post)
    gather_y_faces(post, yf)
    send_faces(2, 4)
    z_faces(edge, field, zf)
    send_faces(4, 9)

    def finish_block(i, carry):
        finish_rows(pl.ds(pl.multiple_of(8 * i, 8), 8), pops, aux, field, post)
        return carry

    lax.fori_loop(2, 30, finish_block, 0)
    run_inside(post, moved)
    for n in range(2):
        settle(s0.at[n, pl.ds(0, 240), :], send_sem.at[n])
    settle(gathered.at[pl.ds(0, 600), :], send_sem.at[2])
    settle(gathered.at[pl.ds(0, 240), :], send_sem.at[3])
    settle(gathered.at[pl.ds(0, 360), :], send_sem.at[4])
    for n in (0, 1):
        copies[n].wait()
    run_x_edges(moved, xr)
    for n in (2, 3, 9, 10, 11, 12):
        copies[n].wait()
    run_y_edges(moved, yr, cr)
    for n in (4, 5, 6, 7, 8):
        copies[n].wait()
    run_z_edges(moved, zr, zx, zy)


def collide_all(table, flow_pops, ion_pos, ion_neg, gray):
    rows, square = (256, 128), (256, 256)
    anywhere = pl.BlockSpec(memory_space=pl.ANY)
    shapes = [(33, 256, 128), rows]
    buffers = [(128, 256), (128, 256), square, (704, 128), (7, 256, 128), (3, 256, 128), rows]
    buffers += [(14, 32, 128)]
    buffers += [(2, 256, 128), (2, 256, 128), (40, 128), (640, 128), (2, 128, 128), (128, 384)]
    buffers += [(128, 128), (128, 128), rows, (192, 128), (384, 128), (320, 256), (64, 128)]
    buffers += [(32, 128), (32, 128)]
    buffers += [(14, 16, 128), (14, 16, 128), (32, 128), (4, 8, 128)] + FACE_SHAPES
    return pl.pallas_call(
        main_kernel,
        out_shape=[pltpu.VMEM(s, f32) for s in shapes],
        in_specs=[pl.BlockSpec(memory_space=pltpu.SMEM)] + [anywhere] * 8,
        out_specs=[pl.BlockSpec(memory_space=pltpu.VMEM)] * 2,
        scratch_shapes=[pltpu.VMEM((33, 256, 128), f32)] * 2
        + [pltpu.VMEM(rows, jnp.int32)]
        + [pltpu.VMEM(s, f32) for s in buffers]
        + [pltpu.SemaphoreType.DMA((n,)) for n in (8, 5, 5, 13, 13)],
        compiler_params=pltpu.CompilerParams(
            collective_id=0, has_side_effects=True, vmem_limit_bytes=VMEM_LIMIT
        ),
        name="collision",
    )(table, ion_pos, ion_neg, flow_pops, gray, *(jnp.asarray(t) for t in tables()))


STORES = ((0, 4), (4, 4), (8, 4), (12, 4), (16, 3))


def store_kernel(moved, phi, flow_out, pos_out, neg_out, phi_out, sem):
    parts = [(moved.at[pl.ds(q, n)], flow_out.at[pl.ds(q, n)]) for q, n in STORES]
    parts += [(moved.at[pl.ds(19, 7)], pos_out), (moved.at[pl.ds(26, 7)], neg_out), (phi, phi_out)]
    copies = [pltpu.make_async_copy(a, b, sem.at[n]) for n, (a, b) in enumerate(parts)]
    for copy in copies:
        copy.start()
    for copy in copies:
        copy.wait()


def store_all(moved, phi):
    shapes = [(19, 256, 128), (7, 256, 128), (7, 256, 128), (256, 128)]
    return pl.pallas_call(
        store_kernel,
        out_shape=[jax.ShapeDtypeStruct(s, f32) for s in shapes],
        in_specs=[pl.BlockSpec(memory_space=pltpu.VMEM)] * 2,
        out_specs=[pl.BlockSpec(memory_space=pl.ANY)] * 4,
        scratch_shapes=[pltpu.SemaphoreType.DMA((8,))],
        compiler_params=pltpu.CompilerParams(vmem_limit_bytes=2 << 20),
        name="results",
    )(moved, phi)


def shards(flow_pops, ion_pos, ion_neg, gray_class, fraction_table):
    extent = gray_class.shape
    flow_pops = flow_pops.reshape(19, 256, 128)
    ion_pos = ion_pos.reshape(7, 256, 128)
    ion_neg = ion_neg.reshape(7, 256, 128)
    gray = gray_class.reshape(256, 128)
    moved, phi = collide_all(fraction_table, flow_pops, ion_pos, ion_neg, gray)
    flow_new, pos_new, neg_new, phi = store_all(moved, phi)
    return (
        flow_new.reshape(19, *extent),
        pos_new.reshape(7, *extent),
        neg_new.reshape(7, *extent),
        phi.reshape(extent),
    )


def solution(mesh):
    in_specs = (
        P(None, "flow", "cy", "cz"),
        P(None, "flow", "cy", "cz"),
        P(None, "flow", "cy", "cz"),
        P("flow", "cy", "cz"),
        P(),
    )
    out_specs = (
        P(None, "flow", "cy", "cz"),
        P(None, "flow", "cy", "cz"),
        P(None, "flow", "cy", "cz"),
        P("flow", "cy", "cz"),
    )
    return jax.shard_map(shards, mesh=mesh, in_specs=in_specs, out_specs=out_specs, check_vma=False)
```

```python
import functools
import math

import jax
import jax.numpy as jnp
import numpy as np
from jax import lax
from jax.experimental import pallas as pl
from jax.experimental.pallas import tpu as pltpu
from jax.sharding import PartitionSpec as P

flow_dirs = (
    (0, 0, 0),
    (1, 0, 0),
    (-1, 0, 0),
    (0, 1, 0),
    (0, -1, 0),
    (0, 0, 1),
    (0, 0, -1),
    (1, 1, 0),
    (-1, -1, 0),
    (1, -1, 0),
    (-1, 1, 0),
    (1, 0, 1),
    (-1, 0, -1),
    (1, 0, -1),
    (-1, 0, 1),
    (0, 1, 1),
    (0, -1, -1),
    (0, 1, -1),
    (0, -1, 1),
)
flow_weights = (1.0 / 3.0,) + (1.0 / 18.0,) * 6 + (1.0 / 36.0,) * 12
ion_weights = (0.25,) + (0.125,) * 6
tau_flow = 0.8
tau_ion = 0.9
coupling = 2.0
mobility = 0.5
NX, NY, NZ = 256, 128, 256
FLOW, CY, CZ = 16, 8, 2
MESH = pl.DeviceIdType.MESH
f32 = jnp.float32
VMEM_LIMIT = 55 << 20

DIRS = flow_dirs + flow_dirs[:7] + flow_dirs[:7]
FACE = {
    (axis, sign): [q for q in range(33) if DIRS[q][axis] == sign]
    for axis in range(3)
    for sign in (1, -1)
}


def cas_table64(points_k, points_n, length):
    product = (points_k[:, None].astype(np.int64) * points_n[None, :]) % length
    angle = product * (2.0 * math.pi / length)
    return np.cos(angle) + np.sin(angle)


def cas_table(points_k, points_n, length):
    return cas_table64(points_k, points_n, length).astype(np.float32)


def pack_rank(table, b):
    part = table[:, 16 * b : 16 * b + 16].reshape(2, 8, 8, 16)
    return part.transpose(0, 2, 1, 3).reshape(16, 128)


def tables():
    hy = cas_table(np.arange(NY), np.arange(NY), NY)
    z = np.arange(NZ)
    hz = cas_table(z, z, NZ)
    wide = cas_table64(z, z, NZ)
    slope = -0.5 * (np.roll(wide, -1, 1) - np.roll(wide, 1, 1))
    back = [
        np.concatenate([wide[:, 128 * c : 128 * c + 128], slope[:, 128 * c : 128 * c + 128]], 1)
        for c in range(CZ)
    ]
    lam_y = 4.0 * np.sin(np.pi * np.arange(NY) / NY) ** 2
    lam_z = 4.0 * np.sin(np.pi * z / NZ) ** 2
    t = 1.0 + 0.5 * (lam_y[:, None] + lam_z[None, :])
    mu = 1.0 / (t + np.sqrt(t * t - 1.0))
    gap = 1.0 / mu - mu
    gap[0, 0] = 1.0
    scale = coupling / (NY * NZ) / gap
    mu[0, 0] = scale[0, 0] = 0.0
    window = np.arange(128) // 16
    per_rank = []
    for b in range(16):
        m = np.tile(mu[:, 16 * b : 16 * b + 16], (1, 8))
        c = np.tile(scale[:, 16 * b : 16 * b + 16], (1, 8))
        packed = pack_rank(mu, b)
        per_rank.append(
            np.concatenate(
                [m, m ** (window + 1), m ** (8 - window), m**8, c]
                + [packed**16, 1.0 / (1.0 - packed**256), packed, pack_rank(scale, b)]
            )
        )
    return (
        np.concatenate([hy, hy], 1),
        hz.reshape(CZ, 128, NZ),
        np.stack(back).astype(np.float32),
        np.stack(per_rank).astype(np.float32),
    )


def place():
    return lax.axis_index("flow"), lax.axis_index("cy"), lax.axis_index("cz")


def fdot(left, right):
    return jnp.dot(left, right, precision=lax.Precision.HIGHEST, preferred_element_type=f32)


def settle(ref, sem):
    pltpu.make_async_copy(ref, ref, sem).wait()


def column_mask(shape, index):
    return lax.broadcasted_iota(jnp.int32, shape, 1) == index


def row_mask(shape, index):
    return lax.broadcasted_iota(jnp.int32, shape, 0) == index


def swap_across_plane(source, target, send_sem, recv_sem):
    _, cy, cz = place()
    me = cz * CY + cy
    for step_cy in (4, 5, 3, 2, 6, 7, 1, 0):
        for step_cz in (1, 0):
            if step_cy or step_cz:
                to_cy, to_cz = lax.rem(cy + step_cy, CY), lax.rem(cz + step_cz, CZ)
                pltpu.make_async_remote_copy(
                    src_ref=source(to_cz * CY + to_cy),
                    dst_ref=target(me),
                    send_sem=send_sem,
                    recv_sem=recv_sem,
                    device_id={"cy": to_cy, "cz": to_cz},
                    device_id_type=MESH,
                ).start()
    pltpu.make_async_copy(source(me), target(me), recv_sem).start()


FLOW_STEPS = (10, 6, 5, 11, 9, 7, 2, 14, 8, 3, 13, 12, 4, 15, 1)


def swap_along_flow(source, target, send_sem, recv_sem):
    me, _, _ = place()
    for step in FLOW_STEPS:
        other = lax.rem(me + step, FLOW)
        pltpu.make_async_remote_copy(
            src_ref=source(other),
            dst_ref=target(me),
            send_sem=send_sem,
            recv_sem=recv_sem,
            device_id={"flow": other},
            device_id_type=MESH,
        ).start()
    pltpu.make_async_copy(source(me), target(me), recv_sem).start()


def rows_at(ref, start, count):
    return ref.at[pl.ds(pl.multiple_of(start, count), count), :]


def window_of(shape):
    return lax.broadcasted_iota(jnp.int32, shape, 1) // 16


def swap_windows(blocks):
    window = window_of(blocks[0].shape)
    for s in (1, 2, 4):
        high = (window & s) != 0
        moved = list(blocks)
        for i in range(8):
            if not i & s:
                low_block, high_block = blocks[i], blocks[i + s]
                moved[i] = jnp.where(high, pltpu.roll(high_block, 16 * s, 1), low_block)
                moved[i + s] = jnp.where(high, high_block, pltpu.roll(low_block, 128 - 16 * s, 1))
        blocks = moved
    return blocks


def spread(values, j):
    values = jnp.where(window_of(values.shape) == j, values, 0.0)
    for s in (16, 32, 64):
        values = values + pltpu.roll(values, s, 1)
    return values


def pack_windows(values, j):
    window = window_of((8, 128))
    packed = []
    for half in range(2):
        both = jnp.zeros((8, 128), f32)
        for i in range(8):
            tile = values[64 * half + 8 * i : 64 * half + 8 * i + 8, :]
            shift = (16 * (i - j)) % 128
            both = jnp.where(window == i, pltpu.roll(tile, shift, 1) if shift else tile, both)
        packed.append(both)
    return jnp.concatenate(packed, axis=0)


def scan_up(values, factor):
    window = window_of(values.shape)
    for s in (1, 2, 4):
        moved = pltpu.roll(values, 16 * s, 1)
        if factor is not None:
            moved = factor * moved
            factor = factor * factor
        values = values + jnp.where(window >= s, moved, 0.0)
    return values


def scan_down(values, factor):
    window = window_of(values.shape)
    for s in (1, 2, 4):
        moved = factor * pltpu.roll(values, 128 - 16 * s, 1)
        factor = factor * factor
        values = values + jnp.where(window < 8 - s, moved, 0.0)
    return values


def total_of(values):
    return jnp.sum(jnp.sum(values, axis=0, keepdims=True), axis=1, keepdims=True)


def zero_mode_mask(cy, cz):
    row = lax.broadcasted_iota(jnp.int32, (8, 128), 0)
    lane = lax.broadcasted_iota(jnp.int32, (8, 128), 1)
    here = jnp.where(cy + cz == 0, 1.0, 0.0)
    return jnp.where((row == 0) & (lane % 16 == 0), here, 0.0)


def block_moments(rho, up, down, gtab, moments, partial, mask):
    near, far, eighth = (gtab[128 * n : 128 * n + 128, :] for n in range(1, 4))
    moments[0:16, :] = pack_windows(up[1] + eighth * up[0], 7)
    moments[16:32, :] = pack_windows(down[0] + eighth * down[1], 0)
    window = window_of((8, 128)).astype(f32)
    at = (window - 7.5, window + 0.5)
    zero = [rho[g][0:8, :] * mask for g in range(2)]
    row = lax.broadcasted_iota(jnp.int32, (8, 128), 0)
    tile = jnp.zeros((8, 128), f32)
    for n in range(3):
        weighted = zero[0] * at[0] ** n + zero[1] * at[1] ** n if n else zero[0] + zero[1]
        tile = jnp.where(row == n, total_of(weighted), tile)
    moments[32:40, :] = tile

    def rest():
        partial[0] = up[0] + (down[0] - rho[0]) + far * spread(down[1], 0)
        partial[1] = up[1] + (down[1] - rho[1]) + near * spread(up[0], 7)

    return rest


def gathered_potential(rho_first, gtab, gathered, partial, mask, flow, out):
    def packed(source, start):
        return gathered[pl.ds(pl.multiple_of(40 * source + start, 8), 16), :]

    ratio, image = gtab[640:656, :], gtab[656:672, :]
    left, right = packed(flow, 0), packed(flow, 16)
    for d in range(15, 0, -1):
        left = packed(lax.rem(flow + 16 - d, 16), 0) + ratio * left
        right = packed(lax.rem(flow + d, 16), 16) + ratio * right
    left, right = left * image, right * image
    one, packed_scale = gtab[672:688, :], gtab[688:704, :]
    behind = packed_scale * (left + one * (packed(flow, 16) + ratio * right))
    ahead = packed_scale * (right + one * (packed(flow, 0) + ratio * left))
    small = window_of((8, 128))
    for tile in range(16):
        rows = slice(8 * tile, 8 * tile + 8)
        half = 8 * (tile // 8)
        from_left = spread(left[half : half + 8, :], tile % 8)
        from_right = spread(right[half : half + 8, :], tile % 8)
        part, j = slice(half, half + 8), tile % 8
        at_first, at_second = (-16 * j) % 128, (16 - 16 * j) % 128
        first = pltpu.roll(behind[part, :], at_first, 1) if at_first else behind[part, :]
        second = pltpu.roll(ahead[part, :], at_second, 1) if at_second else ahead[part, :]
        out[rows, 256:384] = jnp.where(small == 0, first, jnp.where(small == 1, second, 0.0))
        near, far, eighth, scale = (
            gtab[128 * n + 8 * tile : 128 * n + 8 * tile + 8, :] for n in range(1, 5)
        )
        out[rows, 0:128] = scale * (
            partial[0, rows, :] + near * from_left + (far * eighth) * from_right
        )
        out[rows, 128:256] = scale * (
            partial[1, rows, :] + (near * eighth) * from_left + far * from_right
        )

    def moment(block, n):
        return gathered[40 * block + 32 + n : 40 * block + 33 + n, :]

    mean = sum((moment(n, 0) for n in range(1, 16)), moment(0, 0)) * (1.0 / NX)
    moment_first = second_moment = left_sum = left_first = jnp.zeros((1, 128), f32)
    for block in range(16):
        centre = 16.0 * block - 120.0
        own = moment(block, 0) - 16.0 * mean
        own_first = centre * own + moment(block, 1)
        moment_first = moment_first + own_first
        second_moment = second_moment + (centre * own_first + centre * moment(block, 1))
        second_moment = second_moment + (moment(block, 2) - 340.0 * mean)
        before = jnp.where(block < flow, 1.0, 0.0)
        left_sum = left_sum + before * own
        left_first = left_first + before * own_first
    window = window_of((8, 128)).astype(f32)
    centre = 16.0 * flow.astype(f32) - 120.0
    start_sum, start_first = left_sum, left_first
    for g in range(2):
        at = centre + (window - 7.5 + 8.0 * g)
        zero = (rho_first[g] - mean) * mask
        to_here, to_here_first = scan_up(zero, None), scan_up(zero * at, None)
        upto, upto_first = left_sum + to_here, left_first + to_here_first
        left_sum = left_sum + spread(to_here, 7)
        left_first = left_first + spread(to_here_first, 7)
        distance = 2.0 * (at * upto - upto_first) + moment_first
        value = (second_moment - 2.0 * at * moment_first) * (0.5 / NX) - 0.5 * distance
        lanes = slice(128 * g, 128 * g + 128)
        out[0:8, lanes] = out[0:8, lanes] + (coupling / (NY * NZ)) * (mask * value)
    at = centre - 8.5 + 17.0 * window
    upto = jnp.where(small == 0, start_sum, left_sum)
    upto_first = jnp.where(small == 0, start_first, left_first)
    distance = 2.0 * (at * upto - upto_first) + moment_first
    value = (second_moment - 2.0 * at * moment_first) * (0.5 / NX) - 0.5 * distance
    value = jnp.where(small < 2, mask * value, 0.0)
    out[0:8, 256:384] = out[0:8, 256:384] + (coupling / (NY * NZ)) * value


def send_halo(modes_y, s1, s2):
    window = window_of((8, 128))
    for pair in range(4):
        tile = jnp.zeros((8, 128), f32)
        for k in range(4):
            piece = modes_y[pl.ds(32 * pair + k, 8, stride=4), :]
            piece = pltpu.roll(piece, 32 * k, 1) if k else piece
            tile = jnp.where(window // 2 == k, piece, tile)
        for n in range(2):
            at = 24 * (2 * pair + n) + 16
            s2[at : at + 4, :] = tile[4 * n : 4 * n + 4, :]
    for block in range(CY):
        for side, (other, line) in enumerate((((block - 1) % CY, 15), ((block + 1) % CY, 0))):
            for g in range(2):
                source, at = (s1, 16 * other + line) if g == 0 else (s2, 24 * other + line)
                to = 24 * block + 20 + 2 * side + g
                s2[to : to + 1, :] = source[at : at + 1, :]


def receive_halo(rows, xh, yh):
    for side in range(2):
        for r in range(4):
            at = 16 * side + 4 * r
            xh[at : at + 4, :] = rows[pl.ds(8 * side + r, 4, stride=16), :]
        for g in range(2):
            at = 16 * side + 8 * g
            yh[at : at + 8, :] = rows[pl.ds(4 + 2 * side + g, 8, stride=8), :]


def pick_solid(gray, table_ref):
    bits = [(gray & (1 << n)) != 0 for n in range(4)]
    level = [table_ref[n] for n in range(16)]
    values = [jnp.where(bits[0], level[n + 1], level[n]) for n in range(0, 16, 2)]
    for n in range(1, 4):
        values = [
            jnp.where(bits[n], values[m + 1], values[m]) for m in range(0, len(values), 2)
        ]
    return values[0]


def fill_fields(phi, xh, yh, field):
    row = lax.broadcasted_iota(jnp.int32, (16, 128), 0)
    for x in range(16):
        here = phi[16 * x : 16 * x + 16, :]
        low = xh[0:16, :] if x == 0 else phi[16 * x - 16 : 16 * x, :]
        high = xh[16:32, :] if x == 15 else phi[16 * x + 16 : 16 * x + 32, :]
        field[0, 16 * x : 16 * x + 16, :] = -0.5 * (high - low)
        low = jnp.where(row == 0, yh[x : x + 1, :], pltpu.roll(here, 1, 0))
        high = jnp.where(row == 15, yh[16 + x : 17 + x, :], pltpu.roll(here, 15, 0))
        field[1, 16 * x : 16 * x + 16, :] = -0.5 * (high - low)


def prepare(pops, charge, gray, table_ref, aux):
    def block(i, carry):
        at = pl.ds(pl.multiple_of(8 * i, 8), 8)
        f = [pops[q, at, :] for q in range(33)]
        solid = pick_solid(gray[at, :], table_ref)
        density = sum(f[1:19], f[0])
        inverse = 1.0 / density
        for axis in range(3):
            plus = [f[q] for q in range(19) if flow_dirs[q][axis] == 1]
            minus = [f[q] for q in range(19) if flow_dirs[q][axis] == -1]
            aux[axis, at, :] = (sum(plus[1:], plus[0]) - sum(minus[1:], minus[0])) * inverse
        aux[3, at, :] = (tau_flow * charge[at, :]) * inverse
        omega = (1.0 - solid) * (1.0 / tau_flow)
        keep = 1.0 - omega - solid
        aux[4, at, :] = omega * density
        pops[0, at, :] = (keep + solid) * f[0]
        for q in range(1, 19, 2):
            pops[q, at, :] = keep * f[q] + solid * f[q + 1]
            pops[q + 1, at, :] = keep * f[q + 1] + solid * f[q]
        omega = (1.0 - solid) * (1.0 / tau_ion)
        keep = 1.0 - omega - solid
        for n, start in enumerate((19, 26)):
            g = f[start : start + 7]
            aux[5 + n, at, :] = omega * sum(g[1:], g[0])
            pops[start, at, :] = (keep + solid) * g[0]
            for q in range(1, 7, 2):
                pops[start + q, at, :] = keep * g[q] + solid * g[q + 1]
                pops[start + q + 1, at, :] = keep * g[q + 1] + solid * g[q]
        return carry

    lax.fori_loop(0, 32, block, 0)


def drift_of(velocity, push, electric):
    drift = [velocity[d] + push * electric[d] for d in range(3)]
    return drift, 1.0 - 1.5 * (drift[0] * drift[0] + drift[1] * drift[1] + drift[2] * drift[2])


def along_of(direction, drift):
    along = None
    for d in range(3):
        if direction[d] and along is None:
            along = drift[d] if direction[d] == 1 else -drift[d]
        elif direction[d]:
            along = along + drift[d] if direction[d] == 1 else along - drift[d]
    return along


def fluid_terms(mass, weight, base, along):
    scaled = mass * weight
    return scaled * (base + 4.5 * along * along), (3.0 * scaled) * along


def finish_rows(at, pops, aux, field, post):
    velocity = [aux[d, at, :] for d in range(3)]
    electric = [field[d, at, :] for d in range(3)]
    drift, base = drift_of(velocity, aux[3, at, :], electric)
    mass = aux[4, at, :]
    post[0, at, :] = pops[0, at, :] + (mass * flow_weights[0]) * base
    for q in range(1, 19, 2):
        even, odd = fluid_terms(mass, flow_weights[q], base, along_of(flow_dirs[q], drift))
        post[q, at, :] = pops[q, at, :] + (even + odd)
        post[q + 1, at, :] = pops[q + 1, at, :] + (even - odd)
    for start, n, sign in ((19, 5, mobility), (26, 6, -mobility)):
        mass = aux[n, at, :]
        post[start, at, :] = pops[start, at, :] + ion_weights[0] * mass
        even = ion_weights[1] * mass
        for d in range(3):
            q = start + 1 + 2 * d
            odd = (4.0 * even) * (velocity[d] + sign * electric[d])
            post[q, at, :] = pops[q, at, :] + (even + odd)
            post[q + 1, at, :] = pops[q + 1, at, :] + (even - odd)


def pack_columns(planes):
    lane = lax.broadcasted_iota(jnp.int32, (16, 128), 1)
    packed = [jnp.zeros((16, 128), f32), jnp.zeros((16, 128), f32)]
    for x in range(16):
        up, down = planes(x, 0), planes(x, 1)
        both = up if down is up else jnp.where(lane == 127, up, down)
        moved = pltpu.roll(both, (16 * (x // 2) + 1) % 128, 1)
        packed[x % 2] = jnp.where(lane // 16 == x // 2, moved, packed[x % 2])
    return jnp.concatenate(packed, axis=0)


def plane_at(x):
    return slice(16 * x, 16 * x + 16)


def pack_prepared(pops, aux, edge):
    for n in range(7):
        cache = {}

        def planes(x, side, n=n, cache=cache):
            if x not in cache:
                cache[x] = aux[n, plane_at(x), :]
            return cache[x]

        edge[n] = pack_columns(planes)
    for n, pair in enumerate(zip(FACE[2, 1], FACE[2, -1])):
        edge[7 + n] = pack_columns(lambda x, side, pair=pair: pops[pair[side], plane_at(x), :])


def z_faces(edge, field, zf):
    lane = lax.broadcasted_iota(jnp.int32, (32, 128), 1)
    sign = jnp.where(lane % 2 == 0, 1.0, -1.0)
    electric = []
    for d in range(3):
        cache = {}

        def planes(x, side, d=d, cache=cache):
            if x not in cache:
                cache[x] = field[d, plane_at(x), :]
            return cache[x]

        electric.append(pack_columns(planes))
    velocity = [edge[d] for d in range(3)]
    drift, base = drift_of(velocity, edge[3], electric)
    out = jnp.zeros((32, 128), f32)
    for n, q in enumerate(FACE[2, 1]):
        if q < 19:
            even, odd = fluid_terms(edge[4], flow_weights[q], base, along_of(flow_dirs[q], drift))
        else:
            which = 0 if q < 26 else 1
            even = ion_weights[1] * edge[5 + which]
            odd = (4.0 * even) * (velocity[2] + (mobility, -mobility)[which] * electric[2])
        value = edge[7 + n] + (even + sign * odd)
        moved = pltpu.roll(value, 2 * n, 1) if n else value
        out = jnp.where((lane % 16) // 2 == n, moved, out)
    zf[...] = out


def gather_corners(post, corner):
    corner[0] = post[7, 248:256, :]
    corner[1] = post[8, 0:8, :]
    corner[2] = post[9, 240:248, :]
    corner[3] = post[10, 8:16, :]


def gather_x_faces(post, xf):
    for n, q in enumerate(FACE[0, 1]):
        xf[n] = post[q, 240:256, :]
    for n, q in enumerate(FACE[0, -1]):
        xf[7 + n] = post[q, 0:16, :]


def gather_y_faces(post, yf):
    for n, q in enumerate(FACE[1, 1]):
        yf[n] = post[q, pl.ds(15, 16, stride=16), :]
    for n, q in enumerate(FACE[1, -1]):
        yf[7 + n] = post[q, pl.ds(0, 16, stride=16), :]


def face_messages(xf, yf, zf, corner, xr, yr, zr, zx, zy, cr):
    up, down = pl.ds(0, 7), pl.ds(7, 7)
    low, high = pl.ds(0, 16), pl.ds(16, 16)
    return [
        (xf.at[up], xr.at[up], 1, 0, 0),
        (xf.at[down], xr.at[down], -1, 0, 0),
        (yf.at[up], yr.at[up], 0, 1, 0),
        (yf.at[down], yr.at[down], 0, -1, 0),
        (zf, zr, 0, 0, 1),
        (zf.at[high], zx.at[low], 1, 0, 1),
        (zf.at[low], zx.at[high], -1, 0, 1),
        (zf, zy.at[0], 0, 1, 1),
        (zf, zy.at[1], 0, -1, 1),
        (corner.at[0], cr.at[0], 1, 1, 0),
        (corner.at[1], cr.at[1], -1, -1, 0),
        (corner.at[2], cr.at[2], 1, -1, 0),
        (corner.at[3], cr.at[3], -1, 1, 0),
    ]


def partner(step_flow, step_cy, cross):
    flow, cy, cz = place()
    return (
        lax.rem(flow + FLOW + step_flow, FLOW),
        lax.rem(cy + CY + step_cy, CY),
        1 - cz if cross else cz,
    )


def run_inside(post, moved):
    for q in range(33):
        ex, ey, ez = DIRS[q]
        for x in range(16):
            if 0 <= x - ex <= 15:
                plane = post[q, 16 * (x - ex) : 16 * (x - ex) + 16, :]
                if ey:
                    plane = pltpu.roll(plane, ey % 16, 0)
                if ez:
                    plane = pltpu.roll(plane, ez % 128, 1)
                moved[q, 16 * x : 16 * x + 16, :] = plane


def run_x_edges(moved, xr):
    for ex in (1, -1):
        edge_x = 0 if ex == 1 else 15
        for n, q in enumerate(FACE[0, ex]):
            _, ey, ez = DIRS[q]
            plane = xr[n + (0 if ex == 1 else 7)]
            if ey:
                plane = pltpu.roll(plane, ey % 16, 0)
            if ez:
                plane = pltpu.roll(plane, ez % 128, 1)
            moved[q, 16 * edge_x : 16 * edge_x + 16, :] = plane


def run_y_edges(moved, yr, cr):
    row = lax.broadcasted_iota(jnp.int32, (16, 128), 0)
    for ey in (1, -1):
        for n, q in enumerate(FACE[1, ey]):
            ex, _, ez = DIRS[q]
            lines = yr[n + (0 if ey == 1 else 7)]
            if ex:
                tile = 7 if ey == 1 else 0
                line = cr[q - 7, tile : tile + 1, :]
                lines = jnp.where(row == (0 if ex == 1 else 15), line, pltpu.roll(lines, ex % 16, 0))
            if ez:
                lines = pltpu.roll(lines, ez % 128, 1)
            moved[q, pl.ds(0 if ey == 1 else 15, 16, stride=16), :] = lines


def run_z_edges(moved, zr, zx, zy):
    lane = lax.broadcasted_iota(jnp.int32, (16, 128), 1)
    row = lax.broadcasted_iota(jnp.int32, (16, 128), 0)
    for ez in (1, -1):
        goal = 0 if ez == 1 else 127
        for face, q in enumerate(FACE[2, ez]):
            ex, ey, _ = DIRS[q]
            for x in range(16):
                xs = x - ex
                if 0 <= xs <= 15:
                    edge = zr[16 * (xs % 2) : 16 * (xs % 2) + 16, :]
                    block = xs // 2
                else:
                    edge = zx[0:16, :] if ex == 1 else zx[16:32, :]
                    block = 7 if ex == 1 else 0
                if ey:
                    beyond = zy[0 if ey == 1 else 1, 16 * (xs % 2) : 16 * (xs % 2) + 16, :]
                    last_row = 15 if ey == 1 else 0
                    edge = pltpu.roll(jnp.where(row == last_row, beyond, edge), ey % 16, 0)
                shift = (goal - (16 * block + 2 * face + (0 if ez == 1 else 1))) % 128
                column = pltpu.roll(edge, shift, 1) if shift else edge
                here = slice(16 * x, 16 * x + 16)
                moved[q, here, :] = jnp.where(lane == goal, column, moved[q, here, :])


FACE_SHAPES = [(14, 16, 128), (14, 16, 128), (32, 128), (32, 128), (2, 32, 128), (4, 8, 128)]


def main_kernel(
    table_ref, pos_hbm, neg_hbm, flow_hbm, gray_hbm, hy_hbm, hz_hbm, back_hbm, gtab_hbm,
    moved, phi,
    pops, post, gray, hy_ref, hz_ref, back_ref, gtab, aux, field, charge, edge,
    s0, r0, moments, gathered, partial, modes, beside, s1, r1, s2, r2, joined, halo, xh, yh,
    xf, yf, zf, corner, xr, yr, zr, zx, zy, cr,
    load_sem, send_sem, recv_sem, fsend_sem, frecv_sem,
):
    flow, cy, cz = place()
    me = cz * CY + cy
    loads = [
        pltpu.make_async_copy(source, target, load_sem.at[n])
        for n, (source, target) in enumerate(
            (
                (pos_hbm, pops.at[pl.ds(19, 7)]),
                (neg_hbm, pops.at[pl.ds(26, 7)]),
                (hz_hbm.at[cz], hz_ref),
                (flow_hbm, pops.at[pl.ds(0, 19)]),
                (gray_hbm, gray),
                (hy_hbm, hy_ref),
                (gtab_hbm.at[me], gtab),
                (back_hbm.at[cz], back_ref),
            )
        )
    ]
    for copy in loads[:3]:
        copy.start()
    barrier = pltpu.get_barrier_semaphore()

    messages = face_messages(xf, yf, zf, corner, xr, yr, zr, zx, zy, cr)
    strangers = [m[2:] for m in messages if m[2] and (m[3] or m[4])]
    friends = [(0, j, k) for j in (4, 5, 3, 2, 6, 7, 1, 0) for k in (1, 0) if j or k]
    friends += [(i, 0, 0) for i in FLOW_STEPS]
    for i, j, k in strangers + friends:
        pl.semaphore_signal(barrier, inc=1, device_id=partner(i, j, k), device_id_type=MESH)
    for copy in loads[:3]:
        copy.wait()
    pos = pops[19]
    neg = pops[26]
    for q in range(1, 7):
        pos = pos + pops[19 + q]
        neg = neg + pops[26 + q]
    charge[...] = pos - neg
    for copy in loads[3:]:
        copy.start()

    spectrum = fdot(charge[...], hz_ref[...])
    for g in range(2):
        for c in range(2):
            blocks = [
                spectrum[128 * g + 16 * i : 128 * g + 16 * i + 16, 128 * c : 128 * c + 128]
                for i in range(8)
            ]
            for i, block in enumerate(swap_windows(blocks)):
                at = 16 * (8 * c + i)
                s0[g, at : at + 16, :] = block
    pl.semaphore_wait(barrier, 30 + len(strangers))
    swap_across_plane(
        lambda b: s0.at[:, pl.ds(pl.multiple_of(16 * b, 16), 16), :],
        lambda b: r0.at[:, pl.ds(pl.multiple_of(16 * b, 16), 16), :],
        send_sem.at[0],
        recv_sem.at[0],
    )
    for copy in loads[3:]:
        copy.wait()
    prepare(pops, charge, gray, table_ref, aux)
    pack_prepared(pops, aux, edge)
    rho, up, down = [], [], []
    settle(r0, recv_sem.at[0])
    for g in range(2):
        rho.append(fdot(hy_ref[...], r0[g]))
        up.append(scan_up(rho[g], gtab[0:128, :]))
        down.append(scan_down(rho[g], gtab[0:128, :]))
    mask = zero_mode_mask(cy, cz)
    rest = block_moments(rho, up, down, gtab, moments, partial, mask)
    swap_along_flow(
        lambda a: moments,
        lambda a: gathered.at[pl.ds(pl.multiple_of(40 * a, 8), 40), :],
        send_sem.at[1],
        recv_sem.at[1],
    )
    rest()
    settle(gathered, recv_sem.at[1])
    gathered_potential(
        [r[0:8, :] for r in rho], gtab, gathered, partial, mask, flow, modes
    )
    s1[...] = fdot(hy_ref[:, 0:128], modes[:, 0:128])
    swap_across_plane(
        lambda b: rows_at(s1, 16 * lax.rem(b, CY), 16),
        lambda b: rows_at(r1, 16 * b, 16),
        send_sem.at[2],
        recv_sem.at[2],
    )
    spectrum = fdot(hy_ref[:, 0:128], modes[:, 128:384])
    for block in range(CY):
        s2[24 * block : 24 * block + 16, :] = spectrum[16 * block : 16 * block + 16, 0:128]
    beside[...] = spectrum[:, 128:256]
    send_halo(beside, s1, s2)
    swap_across_plane(
        lambda b: s2.at[pl.ds(pl.multiple_of(24 * lax.rem(b, CY), 8), 24), :],
        lambda b: r2.at[pl.ds(pl.multiple_of(24 * b, 8), 24), :],
        send_sem.at[3],
        recv_sem.at[3],
    )
    for g, (ref, step) in enumerate(((r1, 16), (r2, 24))):
        settle(ref, recv_sem.at[2 + g])
        for c in range(2):
            blocks = []
            for i in range(8):
                at = step * (8 * c + i)
                blocks.append(ref[at : at + 16, :])
            for i, block in enumerate(swap_windows(blocks)):
                at = 128 * g + 16 * i
                joined[at : at + 16, 128 * c : 128 * c + 128] = block
        both = fdot(joined[128 * g : 128 * g + 128, :], back_ref[...])
        phi[128 * g : 128 * g + 128, :] = both[:, :128]
        field[2, 128 * g : 128 * g + 128, :] = both[:, 128:]
    for c in range(2):
        blocks = []
        for i in range(8):
            at = 24 * (8 * c + i) + 16
            blocks.append(r2[at : at + 8, :])
        for i, block in enumerate(swap_windows(blocks)):
            joined[256 + 8 * i : 264 + 8 * i, 128 * c : 128 * c + 128] = block
    halo[...] = fdot(joined[256:320, :], back_ref[:, 0:128])
    receive_halo(halo, xh, yh)
    fill_fields(phi, xh, yh, field)
    for start in (0, 8, 240, 248):
        finish_rows(pl.ds(start, 8), pops, aux, field, post)
    copies = {}

    def send_faces(first, last):
        for n in range(first, last):
            source, target, i, j, k = messages[n]
            copies[n] = pltpu.make_async_remote_copy(
                src_ref=source,
                dst_ref=target,
                send_sem=fsend_sem.at[n],
                recv_sem=frecv_sem.at[n],
                device_id=partner(i, j, k),
                device_id_type=MESH,
            )
            copies[n].start()

    gather_corners(post, corner)
    send_faces(9, 13)
    gather_x_faces(post, xf)
    send_faces(0, 2)
    for start in (0, 15, 128, 143):
        finish_rows(pl.ds(start, 8, stride=16), pops, aux, field, post)
    gather_y_faces(post, yf)
    send_faces(2, 4)
    z_faces(edge, field, zf)
    send_faces(4, 9)

    def finish_block(i, carry):
        finish_rows(pl.ds(pl.multiple_of(8 * i, 8), 8), pops, aux, field, post)
        return carry

    lax.fori_loop(2, 30, finish_block, 0)
    run_inside(post, moved)
    settle(s0.at[:, pl.ds(0, 240), :], send_sem.at[0])
    settle(gathered.at[pl.ds(0, 600), :], send_sem.at[1])
    settle(gathered.at[pl.ds(0, 240), :], send_sem.at[2])
    settle(gathered.at[pl.ds(0, 360), :], send_sem.at[3])
    for n in (0, 1):
        copies[n].wait()
    run_x_edges(moved, xr)
    for n in (2, 3, 9, 10, 11, 12):
        copies[n].wait()
    run_y_edges(moved, yr, cr)
    for n in (4, 5, 6, 7, 8):
        copies[n].wait()
    run_z_edges(moved, zr, zx, zy)


def collide_all(table, flow_pops, ion_pos, ion_neg, gray):
    rows, square = (256, 128), (256, 256)
    anywhere = pl.BlockSpec(memory_space=pl.ANY)
    shapes = [(33, 256, 128), rows]
    buffers = [(128, 256), (128, 256), square, (704, 128), (7, 256, 128), (3, 256, 128), rows]
    buffers += [(14, 32, 128)]
    buffers += [(2, 256, 128), (2, 256, 128), (40, 128), (640, 128), (2, 128, 128), (128, 384)]
    buffers += [(128, 128), (128, 128), rows, (192, 128), (384, 128), (320, 256), (64, 128)]
    buffers += [(32, 128), (32, 128)]
    buffers += [(14, 16, 128), (14, 16, 128), (32, 128), (4, 8, 128)] + FACE_SHAPES
    return pl.pallas_call(
        main_kernel,
        out_shape=[pltpu.VMEM(s, f32) for s in shapes],
        in_specs=[pl.BlockSpec(memory_space=pltpu.SMEM)] + [anywhere] * 8,
        out_specs=[pl.BlockSpec(memory_space=pltpu.VMEM)] * 2,
        scratch_shapes=[pltpu.VMEM((33, 256, 128), f32)] * 2
        + [pltpu.VMEM(rows, jnp.int32)]
        + [pltpu.VMEM(s, f32) for s in buffers]
        + [pltpu.SemaphoreType.DMA((n,)) for n in (8, 4, 4, 13, 13)],
        compiler_params=pltpu.CompilerParams(
            collective_id=0, has_side_effects=True, vmem_limit_bytes=VMEM_LIMIT
        ),
        name="collision",
    )(table, ion_pos, ion_neg, flow_pops, gray, *(jnp.asarray(t) for t in tables()))


STORES = ((0, 4), (4, 4), (8, 4), (12, 4), (16, 3))


def store_kernel(moved, phi, flow_out, pos_out, neg_out, phi_out, sem):
    parts = [(moved.at[pl.ds(q, n)], flow_out.at[pl.ds(q, n)]) for q, n in STORES]
    parts += [(moved.at[pl.ds(19, 7)], pos_out), (moved.at[pl.ds(26, 7)], neg_out), (phi, phi_out)]
    copies = [pltpu.make_async_copy(a, b, sem.at[n]) for n, (a, b) in enumerate(parts)]
    for copy in copies:
        copy.start()
    for copy in copies:
        copy.wait()


def store_all(moved, phi):
    shapes = [(19, 256, 128), (7, 256, 128), (7, 256, 128), (256, 128)]
    return pl.pallas_call(
        store_kernel,
        out_shape=[jax.ShapeDtypeStruct(s, f32) for s in shapes],
        in_specs=[pl.BlockSpec(memory_space=pltpu.VMEM)] * 2,
        out_specs=[pl.BlockSpec(memory_space=pl.ANY)] * 4,
        scratch_shapes=[pltpu.SemaphoreType.DMA((8,))],
        compiler_params=pltpu.CompilerParams(vmem_limit_bytes=2 << 20),
        name="results",
    )(moved, phi)


def shards(flow_pops, ion_pos, ion_neg, gray_class, fraction_table):
    extent = gray_class.shape
    flow_pops = flow_pops.reshape(19, 256, 128)
    ion_pos = ion_pos.reshape(7, 256, 128)
    ion_neg = ion_neg.reshape(7, 256, 128)
    gray = gray_class.reshape(256, 128)
    moved, phi = collide_all(fraction_table, flow_pops, ion_pos, ion_neg, gray)
    flow_new, pos_new, neg_new, phi = store_all(moved, phi)
    return (
        flow_new.reshape(19, *extent),
        pos_new.reshape(7, *extent),
        neg_new.reshape(7, *extent),
        phi.reshape(extent),
    )


def solution(mesh):
    in_specs = (
        P(None, "flow", "cy", "cz"),
        P(None, "flow", "cy", "cz"),
        P(None, "flow", "cy", "cz"),
        P("flow", "cy", "cz"),
        P(),
    )
    out_specs = (
        P(None, "flow", "cy", "cz"),
        P(None, "flow", "cy", "cz"),
        P(None, "flow", "cy", "cz"),
        P("flow", "cy", "cz"),
    )
    return jax.shard_map(shards, mesh=mesh, in_specs=in_specs, out_specs=out_specs, check_vma=False)
```
